32 devices in a mesh: seq: 16 (over z, y, x), dp: 2 (over core).
Axes of the slice: x: 2, y: 2, z: 4, core: 2. Of those that a mesh axis runs over, the one named last changes fastest.
Arguments:
- tokens: bfloat16 [2, 64, 384, 256], P('dp', 'seq'), may hold values from -6 to 6
- column_rows: int32 [2, 384], P('dp', 'seq'), may hold values from 16 to 32, as said below
- cotangent: bfloat16 [2, 64, 384, 256], P('dp', 'seq'), may hold values from -6 to 6
- flat_params: bfloat16 [788736], P(('seq', 'dp')), as said below
Outputs:
- layer_out: bfloat16 [2, 64, 384, 256], P('dp', 'seq')
- input_grad: float32 [2, 64, 384, 256], P('dp', 'seq')
- param_grad: float32 [788736], P(('seq', 'dp'))
The draws below stay inside these ranges and needn't reach their ends.
Inputs may be any that keep to these rules, and one draw needn't show every extreme that they name: `column_rows`: each aligned block of 96 grid columns of a group holds one value: 32 (images of 32 rows and 96 columns) or 32 / 2 (images of 16 rows, two stacked per 32 rows); every group has blocks of both values. `flat_params`: the entries of the two gain segments lie between 0.6 and 1.4.
All inputs are finite; a program needn't handle non-finite values.
Results may differ from the reference program's by a relative error of at most 0.012.
Values may be sent and summed in bfloat16 or wider, within the bound.
No kernel may reach another device: no remote copies, remote signals or barrier semaphores. Data moves between devices by JAX's collectives and lax.ppermute only.
A program may use at most 128 MiB of HBM per device.

```python
import jax
import jax.numpy as jnp
from jax import lax

D = 256
FF = 1024
HEADS = 2
TALL = 32
STRIDE = 96
COLS = 384
R = 64
NPARAMS = 788736
N_DP = 2


def draw_column_rows(key, part):
    key = jax.random.fold_in(key, 11)
    blocks = COLS // STRIDE

    def one_group(group_key):
        bits_key, order_key = jax.random.split(group_key)
        extra_bits = jax.random.randint(bits_key, (blocks - 2,), 0, 2, dtype=jnp.int32)
        block_kinds = jnp.concatenate([jnp.array([1, 0], dtype=jnp.int32), extra_bits])
        block_kinds = block_kinds[jax.random.permutation(order_key, blocks)]
        block_rows = jnp.where(block_kinds == 1, TALL, TALL // 2).astype(jnp.int32)
        return jnp.repeat(block_rows, STRIDE, total_repeat_length=COLS)
    return jax.vmap(one_group)(jax.random.split(key, N_DP)).astype(jnp.int32)


def draw_flat_params(key, part):
    key = jax.random.fold_in(key, 23)
    base_key, gain_key = jax.random.split(key)
    base = jnp.clip(jax.random.normal(base_key, (NPARAMS,), jnp.float32), -4.0, 4.0)
    gain_draw = 1.0 + 0.4 * jax.random.uniform(gain_key, (NPARAMS,), jnp.float32, -1.0, 1.0)
    segments = [(D, 1.0, 1), (D, 0.5, 0), (3 * D * D, (D / 2.0) ** (-0.5), 0), (D * D, (D / 4.0) ** (-0.5), 0), (D, 1.0, 1), (D, 0.5, 0), (D * FF, D ** (-0.5), 0), (FF, 0.5, 0), (FF * D, (FF / 2.0) ** (-0.5), 0), (D, 0.3, 0)]
    scales = jnp.concatenate([jnp.full((amount,), factor, jnp.float32) for amount, factor, flag in segments])
    gain_flags = jnp.concatenate([jnp.full((amount,), flag, jnp.int32) for amount, factor, flag in segments])
    return jnp.where(gain_flags == 1, gain_draw, base * scales).astype(jnp.bfloat16)


def block_levels(key, shape, cuts, low, top_value):
    level, own = 1.0, jax.random.fold_in(key, 6)
    for dim, shards_of in cuts:
        draws = jnp.exp(jax.random.uniform(jax.random.fold_in(own, dim), (shards_of,), jnp.float32, low / len(cuts), top_value / len(cuts)))
        level = level * jnp.repeat(draws, shape[dim] // shards_of).reshape([-1 if axis == dim else 1 for axis in range(len(shape))])
    return level


def gaussian(own_key, shape, width, most, cuts=(), kind=jnp.bfloat16):
    values = width * jax.random.normal(own_key, shape, jnp.float32)
    if cuts:
        values = values * block_levels(own_key, shape, cuts, -0.22, 0.18)
    return jnp.clip(values, -most, most).astype(kind)


def setup_inputs(seed: int = 0) -> dict:
    key_of = jax.random.split(jax.random.key(seed), 5)
    return {
        "tokens": gaussian(key_of[0], (N_DP, R, COLS, D), 1.0, 6.0, ((0, 2), (1, 16))),
        "column_rows": draw_column_rows(jax.random.fold_in(key_of[4], 71), 0),
        "cotangent": gaussian(key_of[2], (N_DP, R, COLS, D), 1.0, 6.0, ((0, 2), (1, 16))),
        "flat_params": draw_flat_params(jax.random.fold_in(key_of[4], 71), 0),
    }


@jax.custom_vjp
def low(v):
    return lax.optimization_barrier(v.astype(jnp.bfloat16)).astype(jnp.float32)

@jax.custom_vjp
def low_back(v):
    return v

def low_keep(v):
    return (low(v), None)

def low_pass(kept, grad):
    return (grad,)

def back_keep(v):
    return (v, None)

def back_low(kept, grad):
    return (low(grad),)
low.defvjp(low_keep, low_pass)
low_back.defvjp(back_keep, back_low)
EPSILON = 1e-05
HIGHEST = lax.Precision.HIGHEST

def unpack(flat_params, model_width, hidden_width):
    amounts = [model_width, model_width, model_width * 3 * model_width, model_width * model_width, model_width, model_width, model_width * hidden_width, hidden_width, hidden_width * model_width, model_width]
    pieces = []
    offset = 0
    for amount in amounts:
        pieces.append(flat_params[offset:offset + amount])
        offset = offset + amount
    return (pieces[0], pieces[1], pieces[2].reshape(model_width, 3 * model_width), pieces[3].reshape(model_width, model_width), pieces[4], pieces[5], pieces[6].reshape(model_width, hidden_width), pieces[7], pieces[8].reshape(hidden_width, model_width), pieces[9])

def normalize(inputs, gain_vec, shift_vec):
    center = inputs - lax.optimization_barrier(jnp.mean(inputs, axis=-1, keepdims=True))
    spread = lax.optimization_barrier(jnp.mean(center * center, axis=-1, keepdims=True))
    return center * lax.rsqrt(spread + EPSILON) * gain_vec + shift_vec

def allowed_pairs(column_span):
    later_rows = jnp.arange(TALL, dtype=jnp.int32)[None, :, None]
    earlier_rows = jnp.arange(TALL, dtype=jnp.int32)[None, None, :]
    span_wide = column_span.astype(jnp.int32)[:, None, None]
    same_image = later_rows // span_wide == earlier_rows // span_wide
    return (later_rows >= earlier_rows) & same_image

def block_layer(flat_params, col_block, column_span):
    gain_one, shift_one, w_qkv, w_out, gain_two, shift_two, w_in, bias_in, w_back, bias_back = unpack(flat_params, D, FF)
    rows_all = col_block.shape[0]
    grid_cols = col_block.shape[1]
    head_size = D // HEADS
    scale_factor = head_size ** (-0.5)
    normed = low(normalize(col_block, gain_one, shift_one))
    packed = low_back(low(jnp.einsum('rcd,de->rce', normed, w_qkv, precision=HIGHEST)))
    grouped = packed.reshape(rows_all // TALL, TALL, grid_cols, 3, HEADS, head_size)
    queries = grouped[:, :, :, 0]
    key_rows = grouped[:, :, :, 1]
    values = grouped[:, :, :, 2]
    scores = low_back(jnp.einsum('qichd,qjchd->qchij', queries, key_rows, precision=HIGHEST) * scale_factor)
    pair_mask = allowed_pairs(column_span)[None, :, None]
    probabilities = low(jax.nn.softmax(jnp.where(pair_mask, scores, -1e+30), axis=-1))
    attended = jnp.einsum('qchij,qjchd->qichd', probabilities, values, precision=HIGHEST)
    attended = low_back(low(attended.reshape(rows_all, grid_cols, D)))
    branch = low_back(jnp.einsum('rcd,de->rce', attended, w_out, precision=HIGHEST))
    middle = col_block + branch
    normed_two = low(normalize(middle, gain_two, shift_two))
    inner = low_back(jnp.einsum('rcd,df->rcf', normed_two, w_in, precision=HIGHEST) + bias_in)
    activated = low(jax.nn.gelu(inner))
    second = low_back(jnp.einsum('rcf,fd->rcd', activated, w_back, precision=HIGHEST) + bias_back)
    return middle + second

def to_blocks(source, group_cols):
    groups, rows_all, grid_cols = (source.shape[0], source.shape[1], source.shape[2])
    shaped = source.reshape(groups, rows_all, grid_cols // group_cols, group_cols, -1)
    shaped = jnp.transpose(shaped, (0, 2, 1, 3, 4))
    return shaped.reshape(groups * (grid_cols // group_cols), rows_all, group_cols, -1)

def from_blocks(source, groups, grid_cols):
    num_blocks, rows_all, group_cols, feature_dim = source.shape
    shaped = source.reshape(groups, grid_cols // group_cols, rows_all, group_cols, feature_dim)
    shaped = jnp.transpose(shaped, (0, 2, 1, 3, 4))
    return shaped.reshape(groups, rows_all, grid_cols, feature_dim)

def reference(tokens, column_rows, cotangent, flat_params):
    groups, rows_all, grid_cols = (tokens.shape[0], tokens.shape[1], tokens.shape[2])
    group_cols = max(1, 4096 // rows_all)
    while grid_cols % group_cols != 0:
        group_cols = group_cols - 1
    input_blocks = to_blocks(tokens.astype(jnp.float32), group_cols)
    grad_blocks = to_blocks(cotangent.astype(jnp.float32), group_cols)
    span_blocks = column_rows.reshape(groups * (grid_cols // group_cols), group_cols).astype(jnp.int32)
    params_wide = flat_params.astype(jnp.float32)
    layer_step = jax.checkpoint(block_layer)

    def forward(param_vec, block_inputs):
        return lax.map(lambda pair: layer_step(param_vec, pair[0], pair[1]), (block_inputs, span_blocks))
    outputs, pullback = jax.vjp(forward, params_wide, input_blocks)
    param_grad, input_grad_blocks = pullback(grad_blocks)
    layer_out = from_blocks(outputs, groups, grid_cols).astype(jnp.bfloat16)
    input_grad = from_blocks(input_grad_blocks, groups, grid_cols)
    return (layer_out, input_grad, param_grad)
```

```python
import jax
import jax.numpy as jnp
from jax import lax
from jax.experimental import pallas as pl
from jax.experimental.pallas import tpu as pltpu
from jax.sharding import PartitionSpec as P

D = 256
FF = 1024
HEADS = 2
HEAD = D // HEADS
TALL = 32
STRIDE = 96
EPSILON = 1e-05
LANES = 128
PLANE = 4
CORES = 2
BLOCK = 16
HALF = 8
TOKENS = TALL * BLOCK
TILE = TALL * HALF
VMEM_BYTES = 50 * 1024 * 1024

ROW_GAIN_ONE = 0
ROW_SHIFT_ONE = 2
ROW_QKV = 4
ROW_OUT = ROW_QKV + 6 * D
ROW_GAIN_TWO = ROW_OUT + 2 * D
ROW_SHIFT_TWO = ROW_GAIN_TWO + 2
ROW_IN = ROW_SHIFT_TWO + 2
ROW_BIAS_IN = ROW_IN + 8 * D
ROW_BACK = ROW_BIAS_IN + 8
ROW_BIAS_BACK = ROW_BACK + 2 * FF
ROWS = ROW_BIAS_BACK + 2

F32 = jnp.float32
BF16 = jnp.bfloat16


def nn(left, right):
    return lax.dot_general(left, right, (((1,), (0,)), ((), ())), preferred_element_type=F32)


def nt(left, right):
    return lax.dot_general(left, right, (((1,), (1,)), ((), ())), preferred_element_type=F32)


def tn(left, right):
    return lax.dot_general(left, right, (((0,), (0,)), ((), ())), preferred_element_type=F32)


def to_tokens(block):
    width = block.shape[-1]
    return jnp.concatenate(
        [block[:, :HALF].reshape(TILE, width), block[:, HALF:].reshape(TILE, width)], axis=0
    )


def from_tokens(flat):
    width = flat.shape[-1]
    return jnp.concatenate(
        [flat[:TILE].reshape(TALL, HALF, width), flat[TILE:].reshape(TALL, HALF, width)], axis=1
    )


def center(value):
    offset = value - jnp.mean(value, axis=-1, keepdims=True)
    inverse = lax.rsqrt(jnp.mean(offset * offset, axis=-1, keepdims=True) + EPSILON)
    return offset * inverse, inverse


def center_back(grad_hat, hat, inverse):
    mean_one = jnp.mean(grad_hat, axis=-1, keepdims=True)
    mean_two = jnp.mean(grad_hat * hat, axis=-1, keepdims=True)
    return inverse * (grad_hat - mean_one - hat * mean_two)


def allowed(span):
    key = lax.broadcasted_iota(jnp.int32, (TILE, TILE), 0)
    query = lax.broadcasted_iota(jnp.int32, (TILE, TILE), 1)
    same_column = (key % HALF) == (query % HALF)
    half_tile = TILE // 2
    same_image = (key // half_tile == query // half_tile) | (span >= TALL)
    return same_column & (key <= query) & same_image


class Plan:
    def __init__(self, seq, shard):
        self.shard = shard
        self.deep = seq // PLANE
        self.count = seq * CORES
        self.pairwise = self.deep == 4
        rows = (shard + LANES - 2) // LANES + 1
        self.rows = -(-rows // 16) * 16
        self.lead = -(-(ROW_OUT * LANES) // (PLANE * CORES * shard))

    def first_row(self, device):
        return self.shard * device // LANES


def prepare(plan):
    def kernel(place_ref, *refs):
        sources, rest = refs[: CORES * PLANE], refs[CORES * PLANE :]
        w_qkv, w_out, w_in, w_back, vectors, bias_in, held, flat, sems = rest
        deep_at, plane_at, core_at = place_ref[0], place_ref[1], place_ref[2]
        copies = []
        for core in range(CORES):
            for plane in range(PLANE):
                source = sources[core * PLANE + plane]
                for deep in range(plan.deep):
                    slot = deep ^ deep_at if plan.pairwise else deep
                    copies.append(
                        pltpu.make_async_copy(
                            source.at[deep],
                            held.at[slot, plane ^ plane_at, core ^ core_at],
                            sems.at[len(copies)],
                        )
                    )
        for copy in copies:
            copy.start()
        for copy in copies:
            copy.wait()
        for device in range(plan.count):
            row = plan.first_row(device)
            value = held[device // 8, device // 2 % PLANE, device % CORES].astype(F32)
            if plan.shard * device % LANES:
                before = flat[row : row + 1]
                flat[row : row + plan.rows] = value
                flat[row : row + 1] = flat[row : row + 1] + before
            else:
                flat[row : row + plan.rows] = value
        for ref, row, wide in (
            (w_qkv, ROW_QKV, 6),
            (w_out, ROW_OUT, 2),
            (w_in, ROW_IN, 8),
            (w_back, ROW_BACK, 2),
        ):
            for part in range(wide):
                ref[:, part * LANES : (part + 1) * LANES] = flat[
                    pl.ds(row + part, ref.shape[0], stride=wide)
                ].astype(BF16)
        for index, row in enumerate(
            (ROW_GAIN_ONE, ROW_SHIFT_ONE, ROW_GAIN_TWO, ROW_SHIFT_TWO, ROW_BIAS_BACK)
        ):
            for part in range(2):
                vectors[index : index + 1, part * LANES : (part + 1) * LANES] = flat[
                    row + part : row + part + 1
                ]
        for part in range(8):
            bias_in[0:1, part * LANES : (part + 1) * LANES] = flat[
                ROW_BIAS_IN + part : ROW_BIAS_IN + part + 1
            ]

    shapes = [((D, 3 * D), BF16), ((D, D), BF16), ((D, FF), BF16), ((FF, D), BF16)]
    shapes += [((8, D), F32), ((8, FF), F32)]
    return pl.pallas_call(
        kernel,
        out_shape=[jax.ShapeDtypeStruct(shape, kind) for shape, kind in shapes],
        in_specs=[pl.BlockSpec(memory_space=pltpu.SMEM)]
        + [pl.BlockSpec(memory_space=pl.ANY)] * (CORES * PLANE),
        out_specs=[pl.BlockSpec(memory_space=pltpu.VMEM)] * len(shapes),
        scratch_shapes=[
            pltpu.VMEM((plan.deep, PLANE, CORES, plan.rows, LANES), BF16),
            pltpu.VMEM((ROWS + plan.rows + 8, LANES), F32),
            pltpu.SemaphoreType.DMA((plan.count,)),
        ],
        compiler_params=pltpu.CompilerParams(vmem_limit_bytes=VMEM_BYTES),
        name="prepare",
    )


def forward_kernel(
    span_ref, x_ref, w_qkv, w_out, vectors, packed_ref, attended_ref, middle_ref, logsum_ref
):
    x = to_tokens(x_ref[...].astype(F32))
    hat, _ = center(x)
    normed = (hat * vectors[0:1] + vectors[1:2]).astype(BF16)
    packed = nn(normed, w_qkv[...]).astype(BF16)
    packed_ref[...] = packed
    mask = allowed(span_ref[0, 0])
    scale = HEAD**-0.5
    tiles = []
    for half in range(2):
        rows = packed[half * TILE : (half + 1) * TILE]
        heads = []
        for head in range(HEADS):
            query = rows[:, head * HEAD : (head + 1) * HEAD]
            key = rows[:, D + head * HEAD : D + (head + 1) * HEAD]
            value = rows[:, 2 * D + head * HEAD : 2 * D + (head + 1) * HEAD]
            scores = jnp.where(mask, nt(key, query) * scale, -1e30)
            peak = jnp.max(scores, axis=0, keepdims=True)
            terms = jnp.exp(scores - peak)
            total = jnp.sum(terms, axis=0, keepdims=True)
            probs = (terms * (1.0 / total)).astype(BF16)
            heads.append(tn(probs, value).astype(BF16))
            slot = half * HEADS + head
            logsum_ref[0, slot : slot + 1] = peak + jnp.log(total)
        tiles.append(jnp.concatenate(heads, axis=1))
    attended = jnp.concatenate(tiles, axis=0)
    attended_ref[...] = attended
    middle_ref[...] = x + nn(attended, w_out[...])


def flatten(flat, base, matrix, row, wide):
    for part in range(wide):
        flat[pl.ds(row - base + part, matrix.shape[0], stride=wide)] = matrix[
            :, part * LANES : (part + 1) * LANES
        ]


def feed_kernel(plan):
    base = ROW_OUT - 4

    def kernel(
        place_ref,
        middle_ref,
        attended_ref,
        cot_ref,
        w_out,
        w_in,
        w_back,
        vectors,
        bias_in,
        out_ref,
        grad_att_ref,
        grad_mid_ref,
        parts_ref,
        first_ref,
        acc_in,
        acc_back,
        acc_out,
        acc_vec,
        acc_bias,
        flat,
    ):
        step = pl.program_id(0)

        @pl.when(step == 0)
        def _():
            for ref in (acc_in, acc_back, acc_out, acc_vec, acc_bias):
                ref[...] = jnp.zeros_like(ref)

        middle = middle_ref[...]
        hat, inverse = center(middle)
        normed = (hat * vectors[2:3] + vectors[3:4]).astype(BF16)
        cot_wide = to_tokens(cot_ref[...].astype(F32))
        cot = cot_wide.astype(BF16)
        out = middle + vectors[4:5]
        grad_normed = jnp.zeros((TOKENS, D), F32)
        rate = (2.0 / jnp.pi) ** 0.5
        for part in range(FF // D):
            cut = slice(part * D, (part + 1) * D)
            inner = nn(normed, w_in[:, cut]) + bias_in[0:1, cut]
            square = inner * inner
            bend = jnp.tanh(inner * (rate + (rate * 0.044715) * square))
            half = 0.5 * inner
            activated = (half + half * bend).astype(BF16)
            slope = (0.5 + 0.5 * bend) + half * (1.0 - bend * bend) * (
                rate + (3.0 * rate * 0.044715) * square
            )
            grad_inner_wide = nt(cot, w_back[cut, :]) * slope
            grad_inner = grad_inner_wide.astype(BF16)
            acc_bias[0:1, cut] += jnp.sum(grad_inner.astype(F32), axis=0, keepdims=True)
            out = out + nn(activated, w_back[cut, :])
            grad_normed = grad_normed + nt(grad_inner, w_in[:, cut])
            acc_back[:, cut] += tn(cot, activated)
            acc_in[:, cut] += tn(normed, grad_inner)
        out_ref[...] = from_tokens(out).astype(BF16)
        acc_vec[0:1] += jnp.sum(grad_normed * hat, axis=0, keepdims=True)
        acc_vec[1:2] += jnp.sum(grad_normed, axis=0, keepdims=True)
        acc_vec[2:3] += jnp.sum(cot_wide, axis=0, keepdims=True)
        grad_mid = cot_wide + center_back(grad_normed * vectors[2:3], hat, inverse)
        grad_mid_ref[...] = grad_mid
        grad_branch = grad_mid.astype(BF16)
        acc_out[...] += tn(attended_ref[...], grad_branch)
        grad_att_ref[...] = nt(grad_branch, w_out[...]).astype(BF16)

        @pl.when(step == pl.num_programs(0) - 1)
        def _():
            flatten(flat, base, acc_out[...], ROW_OUT, 2)
            flatten(flat, base, acc_in[...], ROW_IN, 8)
            flatten(flat, base, acc_back[...].T, ROW_BACK, 2)
            for index, row in ((0, ROW_GAIN_TWO), (1, ROW_SHIFT_TWO), (2, ROW_BIAS_BACK)):
                for part in range(2):
                    flat[row - base + part : row - base + part + 1] = acc_vec[
                        index : index + 1, part * LANES : (part + 1) * LANES
                    ]
            for part in range(8):
                flat[ROW_BIAS_IN - base + part : ROW_BIAS_IN - base + part + 1] = acc_bias[
                    0:1, part * LANES : (part + 1) * LANES
                ]
            first_ref[...] = flat[ROW_OUT - base : ROW_OUT - base + 8]
            send_rows(plan, place_ref, flat, base, parts_ref, plan.lead, plan.deep)

    return kernel


def send_rows(plan, place_ref, flat, base, parts_ref, low, high):
    plane_at, core_at = place_ref[1], place_ref[2]
    for device in range(low * PLANE * CORES, high * PLANE * CORES):
        row = plan.first_row(device) - base
        parts_ref[
            (device % CORES) ^ core_at, (device // CORES % PLANE) ^ plane_at, device // 8 - low
        ] = flat[row : row + plan.rows].astype(BF16)


def back_kernel(plan):
    def kernel(
        place_ref,
        span_ref,
        x_ref,
        packed_ref,
        logsum_ref,
        grad_att_ref,
        grad_mid_ref,
        first_ref,
        w_qkv,
        vectors,
        grad_x_ref,
        parts_ref,
        acc_qkv,
        acc_vec,
        flat,
    ):
        step = pl.program_id(0)

        @pl.when(step == 0)
        def _():
            for ref in (acc_qkv, acc_vec):
                ref[...] = jnp.zeros_like(ref)

        mask = allowed(span_ref[0, 0])
        scale = HEAD**-0.5
        tiles = []
        for half in range(2):
            rows = packed_ref[half * TILE : (half + 1) * TILE]
            grads = grad_att_ref[half * TILE : (half + 1) * TILE]
            pieces = [[], [], []]
            for head in range(HEADS):
                query = rows[:, head * HEAD : (head + 1) * HEAD]
                key = rows[:, D + head * HEAD : D + (head + 1) * HEAD]
                value = rows[:, 2 * D + head * HEAD : 2 * D + (head + 1) * HEAD]
                grad = grads[:, head * HEAD : (head + 1) * HEAD]
                slot = half * HEADS + head
                scores = nt(key, query) * scale - logsum_ref[0, slot : slot + 1]
                probs = jnp.exp(jnp.where(mask, scores, -1e30))
                grad_probs = nt(value, grad)
                weighted = probs * grad_probs
                total = jnp.sum(weighted, axis=0, keepdims=True)
                grad_scores = (weighted - probs * total).astype(BF16)
                pieces[0].append((tn(grad_scores, key) * scale).astype(BF16))
                pieces[1].append((nn(grad_scores, query) * scale).astype(BF16))
                pieces[2].append(nn(probs.astype(BF16), grad).astype(BF16))
            tiles.append(jnp.concatenate(pieces[0] + pieces[1] + pieces[2], axis=1))
        grad_packed = jnp.concatenate(tiles, axis=0)
        hat, inverse = center(to_tokens(x_ref[...].astype(F32)))
        normed = (hat * vectors[0:1] + vectors[1:2]).astype(BF16)
        acc_qkv[...] += tn(normed, grad_packed)
        grad_normed = nt(grad_packed, w_qkv[...])
        acc_vec[0:1] += jnp.sum(grad_normed * hat, axis=0, keepdims=True)
        acc_vec[1:2] += jnp.sum(grad_normed, axis=0, keepdims=True)
        grad_x = grad_mid_ref[...] + center_back(grad_normed * vectors[0:1], hat, inverse)
        grad_x_ref[...] = from_tokens(grad_x).astype(BF16)

        @pl.when(step == pl.num_programs(0) - 1)
        def _():
            flatten(flat, 0, acc_qkv[...], ROW_QKV, 6)
            for index, row in ((0, ROW_GAIN_ONE), (1, ROW_SHIFT_ONE)):
                for part in range(2):
                    flat[row + part : row + part + 1] = acc_vec[
                        index : index + 1, part * LANES : (part + 1) * LANES
                    ]
            flat[ROW_OUT : ROW_OUT + 8] = first_ref[...]
            send_rows(plan, place_ref, flat, 0, parts_ref, 0, plan.lead)

    return kernel


def whole(shape):
    return pl.BlockSpec(shape, lambda step: (0,) * len(shape))


def local(mesh_shape, tokens, column_rows, cotangent, flat_params):
    seq = mesh_shape["seq"]
    local_rows, columns = tokens.shape[1], tokens.shape[2]
    group = TALL // local_rows
    owned = columns // group
    steps = owned // BLOCK
    plan = Plan(seq, flat_params.shape[0])
    seq_at = lax.axis_index("seq")
    core_at = lax.axis_index("dp")
    deep_at, plane_at = seq_at // PLANE, seq_at % PLANE
    place = jnp.stack([deep_at, plane_at, core_at]).astype(jnp.int32)
    shift = plan.shard * (seq_at * CORES + core_at) % LANES
    smem = pl.BlockSpec(memory_space=pltpu.SMEM)
    params = pltpu.CompilerParams(
        vmem_limit_bytes=VMEM_BYTES, dimension_semantics=("arbitrary",)
    )

    groups = [[group * g + i for i in range(group)] for g in range(seq // group)]
    deep_groups = [[PLANE * z + q for z in range(plan.deep)] for q in range(PLANE)]

    def to_columns(rows):
        cut = rows.reshape(local_rows, group, owned, D).transpose(1, 0, 2, 3)
        moved = lax.all_to_all(cut, "seq", 0, 0, axis_index_groups=groups, tiled=True)
        return moved.reshape(TALL, owned, D)

    def to_rows(cols):
        moved = lax.all_to_all(
            cols.reshape(group, local_rows, owned, D),
            "seq",
            0,
            0,
            axis_index_groups=groups,
            tiled=True,
        )
        return moved.transpose(1, 0, 2, 3).reshape(tokens.shape)

    def swap_seq(value, distance):
        return lax.ppermute(value, "seq", [(i, i ^ distance) for i in range(seq)])

    def swap_core(value):
        return lax.ppermute(value, "dp", [(0, 1), (1, 0)])

    per_block = STRIDE // owned
    holders = seq * STRIDE // columns
    routes = []
    for target in range(seq):
        index, place_in = target // group, target % group
        source = place_in // per_block * holders + index * per_block + place_in % per_block
        routes.append((source, target))
    span = lax.ppermute(column_rows[:1, :1], "seq", routes)

    own = lax.dynamic_update_slice(
        jnp.zeros((plan.rows * LANES,), BF16), flat_params, (shift,)
    ).reshape(plan.rows, LANES)
    if plan.pairwise:
        deep = jnp.stack([own] + [swap_seq(own, PLANE * k) for k in range(1, plan.deep)])
    else:
        deep = lax.all_gather(own, "seq", axis=0, axis_index_groups=deep_groups)
    plane = [deep] + [swap_seq(deep, k) for k in range(1, PLANE)]
    pieces = plane + [swap_core(piece) for piece in plane]
    x = to_columns(tokens)
    cot = to_columns(cotangent)

    w_qkv, w_out, w_in, w_back, vectors, bias_in = prepare(plan)(place, *pieces)

    count = TALL * owned
    token_spec = lambda width: pl.BlockSpec((TOKENS, width), lambda step: (step, 0))
    grid_spec = pl.BlockSpec((TALL, BLOCK, D), lambda step: (0, step, 0))
    logsum_spec = pl.BlockSpec((1, 8, TILE), lambda step: (step, 0, 0))
    shape = jax.ShapeDtypeStruct
    packed, attended, middle, logsum = pl.pallas_call(
        forward_kernel,
        grid=(steps,),
        in_specs=[smem, grid_spec, whole((D, 3 * D)), whole((D, D)), whole((8, D))],
        out_specs=[token_spec(3 * D), token_spec(D), token_spec(D), logsum_spec],
        out_shape=[
            shape((count, 3 * D), BF16),
            shape((count, D), BF16),
            shape((count, D), F32),
            shape((steps, 8, TILE), F32),
        ],
        compiler_params=params,
        cost_estimate=pl.CostEstimate(
            flops=10**9, bytes_accessed=7 * 10**6, transcendentals=10**6
        ),
        name="forward",
    )(span, x, w_qkv, w_out, vectors)

    feed_rows = ROWS - (ROW_OUT - 4) + plan.rows
    out, grad_att, grad_mid, parts, first = pl.pallas_call(
        feed_kernel(plan),
        grid=(steps,),
        in_specs=[
            smem,
            token_spec(D),
            token_spec(D),
            grid_spec,
            whole((D, D)),
            whole((D, FF)),
            whole((FF, D)),
            whole((8, D)),
            whole((8, FF)),
        ],
        out_specs=[
            grid_spec,
            token_spec(D),
            token_spec(D),
            whole((CORES, PLANE, plan.deep - plan.lead, plan.rows, LANES)),
            whole((8, LANES)),
        ],
        out_shape=[
            shape((TALL, owned, D), BF16),
            shape((count, D), BF16),
            shape((count, D), F32),
            shape((CORES, PLANE, plan.deep - plan.lead, plan.rows, LANES), BF16),
            shape((8, LANES), F32),
        ],
        scratch_shapes=[
            pltpu.VMEM((D, FF), F32),
            pltpu.VMEM((D, FF), F32),
            pltpu.VMEM((D, D), F32),
            pltpu.VMEM((8, D), F32),
            pltpu.VMEM((8, FF), F32),
            pltpu.VMEM((feed_rows, LANES), F32),
        ],
        compiler_params=params,
        cost_estimate=pl.CostEstimate(
            flops=5 * 10**9, bytes_accessed=10**7, transcendentals=2 * 10**6
        ),
        name="feed",
    )(place, middle, attended, cot, w_out, w_in, w_back, vectors, bias_in)

    layer_out = to_rows(out)

    def stages(value):
        value = value[0].astype(F32) + swap_core(value[1]).astype(F32)
        total = value[0]
        sent = value.astype(BF16)
        for k in range(1, PLANE):
            total = total + swap_seq(sent[k], k).astype(F32)
        return total

    later = stages(parts)

    grad_x, lead_parts = pl.pallas_call(
        back_kernel(plan),
        grid=(steps,),
        in_specs=[
            smem,
            smem,
            grid_spec,
            token_spec(3 * D),
            logsum_spec,
            token_spec(D),
            token_spec(D),
            whole((8, LANES)),
            whole((D, 3 * D)),
            whole((8, D)),
        ],
        out_specs=[grid_spec, whole((CORES, PLANE, plan.lead, plan.rows, LANES))],
        out_shape=[
            shape((TALL, owned, D), BF16),
            shape((CORES, PLANE, plan.lead, plan.rows, LANES), BF16),
        ],
        scratch_shapes=[
            pltpu.VMEM((D, 3 * D), F32),
            pltpu.VMEM((8, D), F32),
            pltpu.VMEM((ROW_OUT + plan.rows + 8, LANES), F32),
        ],
        compiler_params=params,
        cost_estimate=pl.CostEstimate(
            flops=3 * 10**9, bytes_accessed=8 * 10**6, transcendentals=10**6
        ),
        name="back",
    )(place, span, x, packed, logsum, grad_att, grad_mid, first, w_qkv, vectors)

    input_grad = to_rows(grad_x).astype(F32)
    total = jnp.concatenate([stages(lead_parts), later], axis=0)
    if plan.pairwise:
        sent = total.astype(BF16)
        result = lax.dynamic_index_in_dim(total, deep_at, 0, keepdims=False)
        for k in range(1, plan.deep):
            piece = lax.dynamic_index_in_dim(sent, deep_at ^ k, 0, keepdims=False)
            result = result + swap_seq(piece, PLANE * k).astype(F32)
    else:
        moved = lax.all_to_all(
            total.astype(BF16), "seq", 0, 0, axis_index_groups=deep_groups, tiled=True
        )
        result = jnp.sum(moved.astype(F32), axis=0)
    param_grad = lax.dynamic_slice(result.reshape(-1), (shift,), (plan.shard,))
    return layer_out, input_grad, param_grad


def solution(mesh):
    shape = dict(mesh.shape)
    rows = P("dp", "seq", None, None)
    flat = P(("seq", "dp"))
    return jax.shard_map(
        lambda *args: local(shape, *args),
        mesh=mesh,
        in_specs=(rows, P("dp", "seq"), rows, flat),
        out_specs=(rows, rows, flat),
        check_vma=False,
    )
```

```python
import jax
import jax.numpy as jnp
from jax import lax
from jax.experimental import pallas as pl
from jax.experimental.pallas import tpu as pltpu
from jax.sharding import PartitionSpec as P

D = 256
FF = 1024
HEADS = 2
HEAD = D // HEADS
TALL = 32
STRIDE = 96
EPSILON = 1e-05
LANES = 128
PLANE = 4
CORES = 2
BLOCK = 16
HALF = 8
TOKENS = TALL * BLOCK
TILE = TALL * HALF
VMEM_BYTES = 60 * 1024 * 1024

ROW_GAIN_ONE = 0
ROW_SHIFT_ONE = 2
ROW_QKV = 4
ROW_OUT = ROW_QKV + 6 * D
ROW_GAIN_TWO = ROW_OUT + 2 * D
ROW_SHIFT_TWO = ROW_GAIN_TWO + 2
ROW_IN = ROW_SHIFT_TWO + 2
ROW_BIAS_IN = ROW_IN + 8 * D
ROW_BACK = ROW_BIAS_IN + 8
ROW_BIAS_BACK = ROW_BACK + 2 * FF
ROWS = ROW_BIAS_BACK + 2

SPAN = 5

F32 = jnp.float32
BF16 = jnp.bfloat16


def nn(left, right):
    return lax.dot_general(left, right, (((1,), (0,)), ((), ())), preferred_element_type=F32)


def nt(left, right):
    return lax.dot_general(left, right, (((1,), (1,)), ((), ())), preferred_element_type=F32)


def tn(left, right):
    return lax.dot_general(left, right, (((0,), (0,)), ((), ())), preferred_element_type=F32)


def to_tokens(block):
    width = block.shape[-1]
    return jnp.concatenate(
        [block[:, :HALF].reshape(TILE, width), block[:, HALF:].reshape(TILE, width)], axis=0
    )


def from_tokens(flat):
    width = flat.shape[-1]
    return jnp.concatenate(
        [flat[:TILE].reshape(TALL, HALF, width), flat[TILE:].reshape(TALL, HALF, width)], axis=1
    )


def center(value):
    offset = value - jnp.mean(value, axis=-1, keepdims=True)
    inverse = lax.rsqrt(jnp.mean(offset * offset, axis=-1, keepdims=True) + EPSILON)
    return offset * inverse, inverse


def center_back(grad_hat, hat, inverse):
    mean_one = jnp.mean(grad_hat, axis=-1, keepdims=True)
    mean_two = jnp.mean(grad_hat * hat, axis=-1, keepdims=True)
    return inverse * (grad_hat - mean_one - hat * mean_two)


def allowed(span):
    key = lax.broadcasted_iota(jnp.int32, (TILE, TILE), 0)
    query = lax.broadcasted_iota(jnp.int32, (TILE, TILE), 1)
    same_column = (key % HALF) == (query % HALF)
    half_tile = TILE // 2
    same_image = (key // half_tile == query // half_tile) | (span >= TALL)
    return same_column & (key <= query) & same_image


class Plan:
    def __init__(self, seq, shard):
        self.shard = shard
        self.deep = seq // PLANE
        self.count = seq * CORES
        self.pairwise = self.deep == 4
        rows = (shard + LANES - 2) // LANES + 2
        self.rows = -(-rows // 16) * 16
        self.lead = -(-(ROW_OUT * LANES) // (PLANE * CORES * shard))

    def first_row(self, device):
        return self.shard * device // LANES


def prepare(plan):
    def kernel(place_ref, *refs):
        sources, rest = refs[: CORES * PLANE], refs[CORES * PLANE :]
        w_qkv, w_out, w_in, w_back, vectors, bias_in, held, flat, sems = rest
        deep_at, plane_at, core_at = place_ref[0], place_ref[1], place_ref[2]
        copies = []
        for core in range(CORES):
            for plane in range(PLANE):
                source = sources[core * PLANE + plane]
                for deep in range(plan.deep):
                    slot = deep ^ deep_at if plan.pairwise else deep
                    copies.append(
                        pltpu.make_async_copy(
                            source.at[deep],
                            held.at[slot, plane ^ plane_at, core ^ core_at],
                            sems.at[len(copies)],
                        )
                    )
        for copy in copies:
            copy.start()
        for copy in copies:
            copy.wait()
        for device in range(plan.count):
            row = plan.first_row(device)
            value = held[device // 8, device // 2 % PLANE, device % CORES].astype(F32)
            if plan.shard * device % LANES:
                before = flat[row : row + 1]
                flat[row : row + plan.rows] = value
                flat[row : row + 1] = flat[row : row + 1] + before
            else:
                flat[row : row + plan.rows] = value
        for ref, row, wide in (
            (w_qkv, ROW_QKV, 6),
            (w_out, ROW_OUT, 2),
            (w_in, ROW_IN, 8),
            (w_back, ROW_BACK, 2),
        ):
            for part in range(wide):
                ref[:, part * LANES : (part + 1) * LANES] = flat[
                    pl.ds(row + part, ref.shape[0], stride=wide)
                ].astype(BF16)
        for index, row in enumerate(
            (ROW_GAIN_ONE, ROW_SHIFT_ONE, ROW_GAIN_TWO, ROW_SHIFT_TWO, ROW_BIAS_BACK)
        ):
            for part in range(2):
                vectors[index : index + 1, part * LANES : (part + 1) * LANES] = flat[
                    row + part : row + part + 1
                ]
        holder = place_ref[3]
        vectors[SPAN : SPAN + 1, :LANES] = held[holder // PLANE, holder % PLANE, core_at][
            plan.rows - 1 :
        ].astype(F32)
        for part in range(8):
            bias_in[0:1, part * LANES : (part + 1) * LANES] = flat[
                ROW_BIAS_IN + part : ROW_BIAS_IN + part + 1
            ]

    shapes = [((D, 3 * D), BF16), ((D, D), BF16), ((D, FF), BF16), ((FF, D), BF16)]
    shapes += [((8, D), F32), ((8, FF), F32)]
    return pl.pallas_call(
        kernel,
        out_shape=[jax.ShapeDtypeStruct(shape, kind) for shape, kind in shapes],
        in_specs=[pl.BlockSpec(memory_space=pltpu.SMEM)]
        + [pl.BlockSpec(memory_space=pl.ANY)] * (CORES * PLANE),
        out_specs=[pl.BlockSpec(memory_space=pltpu.VMEM)] * len(shapes),
        scratch_shapes=[
            pltpu.VMEM((plan.deep, PLANE, CORES, plan.rows, LANES), BF16),
            pltpu.VMEM((ROWS + plan.rows + 8, LANES), F32),
            pltpu.SemaphoreType.DMA((plan.count,)),
        ],
        compiler_params=pltpu.CompilerParams(vmem_limit_bytes=VMEM_BYTES),
        name="prepare",
    )


def forward_kernel(
    x_ref, w_qkv, w_out, vectors, packed_ref, attended_ref, middle_ref, logsum_ref
):
    x = to_tokens(x_ref[...].astype(F32))
    hat, _ = center(x)
    normed = (hat * vectors[0:1] + vectors[1:2]).astype(BF16)
    packed = nn(normed, w_qkv[...]).astype(BF16)
    packed_ref[...] = packed
    mask = allowed(vectors[SPAN : SPAN + 1, 0:1])
    scale = HEAD**-0.5
    tiles = []
    for half in range(2):
        rows = packed[half * TILE : (half + 1) * TILE]
        heads = []
        for head in range(HEADS):
            query = rows[:, head * HEAD : (head + 1) * HEAD]
            key = rows[:, D + head * HEAD : D + (head + 1) * HEAD]
            value = rows[:, 2 * D + head * HEAD : 2 * D + (head + 1) * HEAD]
            scores = jnp.where(mask, nt(key, query) * scale, -1e30)
            peak = jnp.max(scores, axis=0, keepdims=True)
            terms = jnp.exp(scores - peak)
            total = jnp.sum(terms, axis=0, keepdims=True)
            probs = (terms * (1.0 / total)).astype(BF16)
            heads.append(tn(probs, value).astype(BF16))
            slot = half * HEADS + head
            logsum_ref[0, slot : slot + 1] = peak + jnp.log(total)
        tiles.append(jnp.concatenate(heads, axis=1))
    attended = jnp.concatenate(tiles, axis=0)
    attended_ref[...] = attended
    middle_ref[...] = x + nn(attended, w_out[...])


def flatten(flat, base, matrix, row, wide):
    for part in range(wide):
        flat[pl.ds(row - base + part, matrix.shape[0], stride=wide)] = matrix[
            :, part * LANES : (part + 1) * LANES
        ]


def feed_kernel(plan, group):
    base = ROW_OUT - 4

    def kernel(place_ref, middle_ref, attended_ref, cot_ref, *refs):
        w_out, w_in, w_back, vectors, bias_in = refs[:5]
        out_ref, grad_att_ref, grad_mid_ref, keep_ref, send_ref, first_ref = refs[5:11]
        acc_in, acc_back, acc_out, acc_vec, acc_bias, flat = refs[11:]
        step = pl.program_id(0)

        @pl.when(step == 0)
        def _():
            for ref in (acc_in, acc_back, acc_out, acc_vec, acc_bias):
                ref[...] = jnp.zeros_like(ref)

        middle = middle_ref[...]
        hat, inverse = center(middle)
        normed = (hat * vectors[2:3] + vectors[3:4]).astype(BF16)
        cot_wide = to_tokens(cot_ref[...].astype(F32))
        cot = cot_wide.astype(BF16)
        out = middle + vectors[4:5]
        grad_normed = jnp.zeros((TOKENS, D), F32)
        rate = (2.0 / jnp.pi) ** 0.5
        for part in range(FF // D):
            cut = slice(part * D, (part + 1) * D)
            inner = nn(normed, w_in[:, cut]) + bias_in[0:1, cut]
            square = inner * inner
            bend = jnp.tanh(inner * (rate + (rate * 0.044715) * square))
            half = 0.5 * inner
            activated = (half + half * bend).astype(BF16)
            slope = (0.5 + 0.5 * bend) + half * (1.0 - bend * bend) * (
                rate + (3.0 * rate * 0.044715) * square
            )
            grad_inner_wide = nt(cot, w_back[cut, :]) * slope
            grad_inner = grad_inner_wide.astype(BF16)
            acc_bias[0:1, cut] += jnp.sum(grad_inner.astype(F32), axis=0, keepdims=True)
            out = out + nn(activated, w_back[cut, :])
            grad_normed = grad_normed + nt(grad_inner, w_in[:, cut])
            acc_back[:, cut] += tn(cot, activated)
            acc_in[:, cut] += tn(normed, grad_inner)
        out_ref[...] = from_tokens(out).astype(BF16)
        acc_vec[0:1] += jnp.sum(grad_normed * hat, axis=0, keepdims=True)
        acc_vec[1:2] += jnp.sum(grad_normed, axis=0, keepdims=True)
        acc_vec[2:3] += jnp.sum(cot_wide, axis=0, keepdims=True)
        grad_mid = cot_wide + center_back(grad_normed * vectors[2:3], hat, inverse)
        grad_mid_ref[...] = grad_mid
        grad_branch = grad_mid.astype(BF16)
        acc_out[...] += tn(attended_ref[...], grad_branch)
        grad_att_ref[...] = nt(grad_branch, w_out[...]).astype(BF16)

        @pl.when(step == pl.num_programs(0) - 1)
        def _():
            flatten(flat, base, acc_out[...], ROW_OUT, 2)
            flatten(flat, base, acc_in[...], ROW_IN, 8)
            flatten(flat, base, acc_back[...].T, ROW_BACK, 2)
            for index, row in ((0, ROW_GAIN_TWO), (1, ROW_SHIFT_TWO), (2, ROW_BIAS_BACK)):
                for part in range(2):
                    flat[row - base + part : row - base + part + 1] = acc_vec[
                        index : index + 1, part * LANES : (part + 1) * LANES
                    ]
            for part in range(8):
                flat[ROW_BIAS_IN - base + part : ROW_BIAS_IN - base + part + 1] = acc_bias[
                    0:1, part * LANES : (part + 1) * LANES
                ]
            first_ref[...] = flat[ROW_OUT - base : ROW_OUT - base + 8]
            send_rows(plan, place_ref, flat, base, (keep_ref, send_ref), plan.lead, plan.deep)

    return kernel


def send_rows(plan, place_ref, flat, base, refs, low, high):
    plane_at, core_at = place_ref[1], place_ref[2]

    def write(own_core):
        for device in range(low * PLANE * CORES, high * PLANE * CORES):
            row = plan.first_row(device) - base
            ref = refs[(device % CORES) ^ own_core]
            ref[(device // CORES % PLANE) ^ plane_at, device // (PLANE * CORES) - low] = flat[
                row : row + plan.rows
            ].astype(BF16)

    for own_core in range(CORES):
        pl.when(core_at == own_core)(lambda own_core=own_core: write(own_core))


def attend_back_kernel(plan):
    def kernel(
        place_ref,
        x_ref,
        packed_ref,
        logsum_ref,
        grad_att_ref,
        grad_mid_ref,
        first_ref,
        w_qkv,
        vectors,
        grad_x_ref,
        keep_ref,
        send_ref,
        acc_qkv,
        acc_vec,
        flat,
    ):
        step = pl.program_id(0)

        @pl.when(step == 0)
        def _():
            for ref in (acc_qkv, acc_vec):
                ref[...] = jnp.zeros_like(ref)

        mask = allowed(vectors[SPAN : SPAN + 1, 0:1])
        scale = HEAD**-0.5
        tiles = []
        for half in range(2):
            rows = packed_ref[half * TILE : (half + 1) * TILE]
            grads = grad_att_ref[half * TILE : (half + 1) * TILE]
            pieces = [[], [], []]
            for head in range(HEADS):
                query = rows[:, head * HEAD : (head + 1) * HEAD]
                key = rows[:, D + head * HEAD : D + (head + 1) * HEAD]
                value = rows[:, 2 * D + head * HEAD : 2 * D + (head + 1) * HEAD]
                grad = grads[:, head * HEAD : (head + 1) * HEAD]
                slot = half * HEADS + head
                scores = nt(key, query) * scale - logsum_ref[0, slot : slot + 1]
                probs = jnp.exp(jnp.where(mask, scores, -1e30))
                grad_probs = nt(value, grad)
                weighted = probs * grad_probs
                total = jnp.sum(weighted, axis=0, keepdims=True)
                grad_scores = (weighted - probs * total).astype(BF16)
                pieces[0].append((tn(grad_scores, key) * scale).astype(BF16))
                pieces[1].append((nn(grad_scores, query) * scale).astype(BF16))
                pieces[2].append(nn(probs.astype(BF16), grad).astype(BF16))
            tiles.append(jnp.concatenate(pieces[0] + pieces[1] + pieces[2], axis=1))
        grad_packed = jnp.concatenate(tiles, axis=0)
        hat, inverse = center(to_tokens(x_ref[...].astype(F32)))
        normed = (hat * vectors[0:1] + vectors[1:2]).astype(BF16)
        acc_qkv[...] += tn(normed, grad_packed)
        grad_normed = nt(grad_packed, w_qkv[...])
        acc_vec[0:1] += jnp.sum(grad_normed * hat, axis=0, keepdims=True)
        acc_vec[1:2] += jnp.sum(grad_normed, axis=0, keepdims=True)
        grad_x = grad_mid_ref[...] + center_back(grad_normed * vectors[0:1], hat, inverse)
        grad_x_ref[...] = from_tokens(grad_x).astype(BF16)

        @pl.when(step == pl.num_programs(0) - 1)
        def _():
            flatten(flat, 0, acc_qkv[...], ROW_QKV, 6)
            for index, row in ((0, ROW_GAIN_ONE), (1, ROW_SHIFT_ONE)):
                for part in range(2):
                    flat[row + part : row + part + 1] = acc_vec[
                        index : index + 1, part * LANES : (part + 1) * LANES
                    ]
            flat[ROW_OUT : ROW_OUT + 8] = first_ref[...]
            send_rows(plan, place_ref, flat, 0, (keep_ref, send_ref), 0, plan.lead)

    return kernel


def cut_rows_kernel(group, owned):
    def kernel(rows_ref, out_ref):
        for index in range(group):
            out_ref[index] = rows_ref[:, index * owned : (index + 1) * owned]

    return kernel


def cut_pieces_kernel(group, owned):
    def kernel(place_ref, rows_ref, *pieces):
        for index, piece in enumerate(pieces):
            column = pl.multiple_of((index ^ place_ref[3]) * owned, 16)
            piece[...] = rows_ref[:, pl.ds(column, owned)]

    return kernel


def whole(shape):
    return pl.BlockSpec(shape, lambda step: (0,) * len(shape))


def local(mesh_shape, tokens, column_rows, cotangent, flat_params):
    seq = mesh_shape["seq"]
    local_rows, columns = tokens.shape[1], tokens.shape[2]
    group = TALL // local_rows
    owned = columns // group
    steps = owned // BLOCK
    plan = Plan(seq, flat_params.shape[0])
    seq_at = lax.axis_index("seq")
    core_at = lax.axis_index("dp")
    deep_at, plane_at = seq_at // PLANE, seq_at % PLANE
    holder = seq_at % group * owned // STRIDE * (seq * STRIDE // columns)
    place = jnp.stack([deep_at, plane_at, core_at, holder]).astype(jnp.int32)
    shift = plan.shard * (seq_at * CORES + core_at) % LANES
    smem = pl.BlockSpec(memory_space=pltpu.SMEM)
    params = pltpu.CompilerParams(
        vmem_limit_bytes=VMEM_BYTES, dimension_semantics=("arbitrary",)
    )

    groups = [[group * g + i for i in range(group)] for g in range(seq // group)]
    deep_groups = [[PLANE * z + q for z in range(plan.deep)] for q in range(PLANE)]

    def exchange(blocks):
        return lax.all_to_all(blocks, "seq", 0, 0, axis_index_groups=groups, tiled=True)

    def to_rows(cols):
        moved = exchange(cols.reshape(group, local_rows, owned, D))
        return moved.transpose(1, 0, 2, 3).reshape(tokens.shape)

    def swap_seq(value, distance):
        return lax.ppermute(value, "seq", [(i, i ^ distance) for i in range(seq)])

    def swap_core(value):
        return lax.ppermute(value, "dp", [(0, 1), (1, 0)])

    blank = jnp.zeros((plan.rows - 1) * LANES, BF16)
    blank = jnp.concatenate([blank, jnp.broadcast_to(column_rows[0, 0].astype(BF16), (LANES,))])
    own = lax.dynamic_update_slice(blank, flat_params, (shift,)).reshape(plan.rows, LANES)
    if plan.pairwise:
        arrived = [swap_seq(own, PLANE * k) for k in range(1, plan.deep)]
        deep = jnp.stack([own] + arrived)
    else:
        arrived = [own]
        deep = lax.all_gather(own, "seq", axis=0, axis_index_groups=deep_groups)
    vmem = pl.BlockSpec(memory_space=pltpu.VMEM)
    x_cut = pl.pallas_call(
        cut_rows_kernel(group, owned),
        out_shape=jax.ShapeDtypeStruct((group, local_rows, owned, D), BF16),
        in_specs=[vmem],
        out_specs=vmem,
        name="cut_tokens",
    )(tokens.reshape(local_rows, columns, D))
    x_cut, _ = lax.optimization_barrier((x_cut, arrived))
    x = exchange(x_cut).reshape(TALL, owned, D)
    plane = [deep] + [swap_seq(deep, k) for k in range(1, PLANE)]
    pieces = plane + [swap_core(piece) for piece in plane]
    cot_cut = pl.pallas_call(
        cut_rows_kernel(group, owned),
        out_shape=jax.ShapeDtypeStruct((group, local_rows, owned, D), BF16),
        in_specs=[vmem],
        out_specs=vmem,
        name="cut_cotangent",
    )(cotangent.reshape(local_rows, columns, D))
    cot_cut, _ = lax.optimization_barrier((cot_cut, (x, plane[1:])))
    cot = exchange(cot_cut).reshape(TALL, owned, D)

    w_qkv, w_out, w_in, w_back, vectors, bias_in = prepare(plan)(place, *pieces)

    count = TALL * owned
    token_spec = lambda width: pl.BlockSpec((TOKENS, width), lambda step: (step, 0))
    grid_spec = pl.BlockSpec((TALL, BLOCK, D), lambda step: (0, step, 0))
    logsum_spec = pl.BlockSpec((1, 8, TILE), lambda step: (step, 0, 0))
    shape = jax.ShapeDtypeStruct
    packed, attended, middle, logsum = pl.pallas_call(
        forward_kernel,
        grid=(steps,),
        in_specs=[grid_spec, whole((D, 3 * D)), whole((D, D)), whole((8, D))],
        out_specs=[token_spec(3 * D), token_spec(D), token_spec(D), logsum_spec],
        out_shape=[
            shape((count, 3 * D), BF16),
            shape((count, D), BF16),
            shape((count, D), F32),
            shape((steps, 8, TILE), F32),
        ],
        compiler_params=params,
        cost_estimate=pl.CostEstimate(
            flops=10**9, bytes_accessed=7 * 10**6, transcendentals=10**6
        ),
        name="forward",
    )(x, w_qkv, w_out, vectors)

    feed_rows = ROWS - (ROW_OUT - 4) + plan.rows
    parts_shape = lambda deep: (PLANE, deep, plan.rows, LANES)
    out, grad_att, grad_mid, keep, send, first = pl.pallas_call(
        feed_kernel(plan, group),
        grid=(steps,),
        in_specs=[
            smem,
            token_spec(D),
            token_spec(D),
            grid_spec,
            whole((D, D)),
            whole((D, FF)),
            whole((FF, D)),
            whole((8, D)),
            whole((8, FF)),
        ],
        out_specs=[
            grid_spec,
            token_spec(D),
            token_spec(D),
            *[whole(parts_shape(plan.deep - plan.lead))] * CORES,
            whole((8, LANES)),
        ],
        out_shape=[
            shape((TALL, owned, D), BF16),
            shape((count, D), BF16),
            shape((count, D), F32),
            *[shape(parts_shape(plan.deep - plan.lead), BF16)] * CORES,
            shape((8, LANES), F32),
        ],
        scratch_shapes=[
            pltpu.VMEM((D, FF), F32),
            pltpu.VMEM((D, FF), F32),
            pltpu.VMEM((D, D), F32),
            pltpu.VMEM((8, D), F32),
            pltpu.VMEM((8, FF), F32),
            pltpu.VMEM((feed_rows, LANES), F32),
        ],
        compiler_params=params,
        cost_estimate=pl.CostEstimate(
            flops=5 * 10**9, bytes_accessed=10**7, transcendentals=2 * 10**6
        ),
        name="feed",
    )(place, middle, attended, cot, w_out, w_in, w_back, vectors, bias_in)

    layer_out = to_rows(out)

    def core_sum(keep, send):
        return keep.astype(F32) + swap_core(send).astype(F32)

    def plane_sum(value):
        total = value[0]
        sent = value.astype(BF16)
        for k in range(1, PLANE):
            total = total + swap_seq(sent[k], k).astype(F32)
        return total

    later = plane_sum(core_sum(keep, send))

    grad_x, lead_keep, lead_send = pl.pallas_call(
        attend_back_kernel(plan),
        grid=(steps,),
        in_specs=[
            smem,
            grid_spec,
            token_spec(3 * D),
            logsum_spec,
            token_spec(D),
            token_spec(D),
            whole((8, LANES)),
            whole((D, 3 * D)),
            whole((8, D)),
        ],
        out_specs=[grid_spec, *[whole(parts_shape(plan.lead))] * CORES],
        out_shape=[
            shape((TALL, owned, D), BF16),
            *[shape(parts_shape(plan.lead), BF16)] * CORES,
        ],
        scratch_shapes=[
            pltpu.VMEM((D, 3 * D), F32),
            pltpu.VMEM((8, D), F32),
            pltpu.VMEM((ROW_OUT + plan.rows + 8, LANES), F32),
        ],
        compiler_params=params,
        cost_estimate=pl.CostEstimate(
            flops=10 * 10**9, bytes_accessed=8 * 10**6, transcendentals=10**6
        ),
        name="attend_back",
    )(place, x, packed, logsum, grad_att, grad_mid, first, w_qkv, vectors)
    (grad_x, lead_keep, lead_send), layer_out, later = lax.optimization_barrier(
        ((grad_x, lead_keep, lead_send), layer_out, later)
    )
    total = jnp.concatenate([plane_sum(core_sum(lead_keep, lead_send)), later], axis=0)
    input_grad = to_rows(grad_x).astype(F32)
    if plan.pairwise:
        sent = total.astype(BF16)
        result = lax.dynamic_index_in_dim(total, deep_at, 0, keepdims=False)
        for k in range(1, plan.deep):
            piece = lax.dynamic_index_in_dim(sent, deep_at ^ k, 0, keepdims=False)
            result = result + swap_seq(piece, PLANE * k).astype(F32)
    else:
        moved = lax.all_to_all(
            total.astype(BF16), "seq", 0, 0, axis_index_groups=deep_groups, tiled=True
        )
        result = jnp.sum(moved.astype(F32), axis=0)
    param_grad = lax.dynamic_slice(result.reshape(-1), (shift,), (plan.shard,))
    return layer_out, input_grad, param_grad


def solution(mesh):
    shape = dict(mesh.shape)
    rows = P("dp", "seq", None, None)
    flat = P(("seq", "dp"))
    return jax.shard_map(
        lambda *args: local(shape, *args),
        mesh=mesh,
        in_specs=(rows, P("dp", "seq"), rows, flat),
        out_specs=(rows, rows, flat),
        check_vma=False,
    )
```

```python
import jax
import jax.numpy as jnp
from jax import lax
from jax.experimental import pallas as pl
from jax.experimental.pallas import tpu as pltpu
from jax.sharding import PartitionSpec as P

D = 256
FF = 1024
HEADS = 2
HEAD = D // HEADS
TALL = 32
STRIDE = 96
EPSILON = 1e-05
LANES = 128
PLANE = 4
CORES = 2
BLOCK = 16
HALF = 8
TOKENS = TALL * BLOCK
TILE = TALL * HALF
VMEM_BYTES = 60 * 1024 * 1024

ROW_GAIN_ONE = 0
ROW_SHIFT_ONE = 2
ROW_QKV = 4
ROW_OUT = ROW_QKV + 6 * D
ROW_GAIN_TWO = ROW_OUT + 2 * D
ROW_SHIFT_TWO = ROW_GAIN_TWO + 2
ROW_IN = ROW_SHIFT_TWO + 2
ROW_BIAS_IN = ROW_IN + 8 * D
ROW_BACK = ROW_BIAS_IN + 8
ROW_BIAS_BACK = ROW_BACK + 2 * FF
ROWS = ROW_BIAS_BACK + 2

SPAN = 5

F32 = jnp.float32
BF16 = jnp.bfloat16


def nn(left, right):
    return lax.dot_general(left, right, (((1,), (0,)), ((), ())), preferred_element_type=F32)


def nt(left, right):
    return lax.dot_general(left, right, (((1,), (1,)), ((), ())), preferred_element_type=F32)


def tn(left, right):
    return lax.dot_general(left, right, (((0,), (0,)), ((), ())), preferred_element_type=F32)


def to_tokens(block):
    width = block.shape[-1]
    return jnp.concatenate(
        [block[:, :HALF].reshape(TILE, width), block[:, HALF:].reshape(TILE, width)], axis=0
    )


def from_tokens(flat):
    width = flat.shape[-1]
    return jnp.concatenate(
        [flat[:TILE].reshape(TALL, HALF, width), flat[TILE:].reshape(TALL, HALF, width)], axis=1
    )


def read_block(ref):
    return to_tokens(ref[...].reshape(TALL, BLOCK, D).astype(F32))


def center(value):
    offset = value - jnp.mean(value, axis=-1, keepdims=True)
    inverse = lax.rsqrt(jnp.mean(offset * offset, axis=-1, keepdims=True) + EPSILON)
    return offset * inverse, inverse


def center_back(grad_hat, hat, inverse):
    mean_one = jnp.mean(grad_hat, axis=-1, keepdims=True)
    mean_two = jnp.mean(grad_hat * hat, axis=-1, keepdims=True)
    return inverse * (grad_hat - mean_one - hat * mean_two)


def allowed(span):
    key = lax.broadcasted_iota(jnp.int32, (TILE, TILE), 0)
    query = lax.broadcasted_iota(jnp.int32, (TILE, TILE), 1)
    same_column = (key % HALF) == (query % HALF)
    half_tile = TILE // 2
    same_image = (key // half_tile == query // half_tile) | (span >= TALL)
    return same_column & (key <= query) & same_image


class Plan:
    def __init__(self, seq, shard):
        self.shard = shard
        self.deep = seq // PLANE
        self.count = seq * CORES
        self.pairwise = self.deep == 4
        rows = (shard + LANES - 2) // LANES + 2
        self.rows = -(-rows // 16) * 16
        self.lead = -(-(ROW_OUT * LANES) // (PLANE * CORES * shard))

    def first_row(self, device):
        return self.shard * device // LANES


def prepare(plan):
    def kernel(place_ref, *refs):
        sources, rest = refs[: CORES * PLANE], refs[CORES * PLANE :]
        w_qkv, w_out, w_in, w_back, vectors, bias_in, held, flat, sems = rest
        deep_at, plane_at, core_at = place_ref[0], place_ref[1], place_ref[2]
        copies = []
        for core in range(CORES):
            for plane in range(PLANE):
                source = sources[core * PLANE + plane]
                for deep in range(plan.deep):
                    slot = deep ^ deep_at if plan.pairwise else deep
                    copies.append(
                        pltpu.make_async_copy(
                            source.at[deep],
                            held.at[slot, plane ^ plane_at, core ^ core_at],
                            sems.at[len(copies)],
                        )
                    )
        for copy in copies:
            copy.start()
        for copy in copies:
            copy.wait()
        for device in range(plan.count):
            row = plan.first_row(device)
            value = held[device // 8, device // 2 % PLANE, device % CORES].astype(F32)
            if plan.shard * device % LANES:
                before = flat[row : row + 1]
                flat[row : row + plan.rows] = value
                flat[row : row + 1] = flat[row : row + 1] + before
            else:
                flat[row : row + plan.rows] = value
        for ref, row, wide in (
            (w_qkv, ROW_QKV, 6),
            (w_out, ROW_OUT, 2),
            (w_in, ROW_IN, 8),
            (w_back, ROW_BACK, 2),
        ):
            for part in range(wide):
                ref[:, part * LANES : (part + 1) * LANES] = flat[
                    pl.ds(row + part, ref.shape[0], stride=wide)
                ].astype(BF16)
        for index, row in enumerate(
            (ROW_GAIN_ONE, ROW_SHIFT_ONE, ROW_GAIN_TWO, ROW_SHIFT_TWO, ROW_BIAS_BACK)
        ):
            for part in range(2):
                vectors[index : index + 1, part * LANES : (part + 1) * LANES] = flat[
                    row + part : row + part + 1
                ]
        holder = place_ref[3]
        vectors[SPAN : SPAN + 1, :LANES] = held[holder // PLANE, holder % PLANE, core_at][
            plan.rows - 1 :
        ].astype(F32)
        for part in range(8):
            bias_in[0:1, part * LANES : (part + 1) * LANES] = flat[
                ROW_BIAS_IN + part : ROW_BIAS_IN + part + 1
            ]

    shapes = [((D, 3 * D), BF16), ((D, D), BF16), ((D, FF), BF16), ((FF, D), BF16)]
    shapes += [((8, D), F32), ((8, FF), F32)]
    return pl.pallas_call(
        kernel,
        out_shape=[jax.ShapeDtypeStruct(shape, kind) for shape, kind in shapes],
        in_specs=[pl.BlockSpec(memory_space=pltpu.SMEM)]
        + [pl.BlockSpec(memory_space=pl.ANY)] * (CORES * PLANE),
        out_specs=[pl.BlockSpec(memory_space=pltpu.VMEM)] * len(shapes),
        scratch_shapes=[
            pltpu.VMEM((plan.deep, PLANE, CORES, plan.rows, LANES), BF16),
            pltpu.VMEM((ROWS + plan.rows + 8, LANES), F32),
            pltpu.SemaphoreType.DMA((plan.count,)),
        ],
        compiler_params=pltpu.CompilerParams(vmem_limit_bytes=VMEM_BYTES),
        cost_estimate=pl.CostEstimate(flops=25500000000, bytes_accessed=4 * 10**6, transcendentals=0),
        name="prepare",
    )


def forward_kernel(
    x_ref, w_qkv, w_out, vectors, packed_ref, attended_ref, middle_ref, logsum_ref
):
    x = read_block(x_ref)
    hat, _ = center(x)
    normed = (hat * vectors[0:1] + vectors[1:2]).astype(BF16)
    packed = nn(normed, w_qkv[...]).astype(BF16)
    packed_ref[...] = packed
    mask = allowed(vectors[SPAN : SPAN + 1, 0:1])
    scale = HEAD**-0.5
    tiles = []
    for half in range(2):
        rows = packed[half * TILE : (half + 1) * TILE]
        heads = []
        for head in range(HEADS):
            query = rows[:, head * HEAD : (head + 1) * HEAD]
            key = rows[:, D + head * HEAD : D + (head + 1) * HEAD]
            value = rows[:, 2 * D + head * HEAD : 2 * D + (head + 1) * HEAD]
            scores = jnp.where(mask, nt(key, query) * scale, -1e30)
            peak = jnp.max(scores, axis=0, keepdims=True)
            terms = jnp.exp(scores - peak)
            total = jnp.sum(terms, axis=0, keepdims=True)
            probs = (terms * (1.0 / total)).astype(BF16)
            heads.append(tn(probs, value).astype(BF16))
            slot = half * HEADS + head
            logsum_ref[0, slot : slot + 1] = peak + jnp.log(total)
        tiles.append(jnp.concatenate(heads, axis=1))
    attended = jnp.concatenate(tiles, axis=0)
    attended_ref[...] = attended
    middle_ref[...] = x + nn(attended, w_out[...])


def flatten(flat, base, matrix, row, wide):
    for part in range(wide):
        flat[pl.ds(row - base + part, matrix.shape[0], stride=wide)] = matrix[
            :, part * LANES : (part + 1) * LANES
        ]


def feed_kernel(plan, group):
    base = ROW_OUT - 4

    def kernel(place_ref, middle_ref, attended_ref, cot_ref, *refs):
        w_out, w_in, w_back, vectors, bias_in = refs[:5]
        out_ref, grad_att_ref, grad_mid_ref, keep_ref, send_ref, first_ref = refs[5:11]
        acc_in, acc_back, acc_out, acc_vec, acc_bias, flat = refs[11:]
        step = pl.program_id(0)

        @pl.when(step == 0)
        def _():
            for ref in (acc_in, acc_back, acc_out, acc_vec, acc_bias):
                ref[...] = jnp.zeros_like(ref)

        middle = middle_ref[...]
        hat, inverse = center(middle)
        normed = (hat * vectors[2:3] + vectors[3:4]).astype(BF16)
        cot_wide = read_block(cot_ref)
        cot = cot_wide.astype(BF16)
        out = middle + vectors[4:5]
        grad_normed = jnp.zeros((TOKENS, D), F32)
        rate = (2.0 / jnp.pi) ** 0.5
        for part in range(FF // D):
            cut = slice(part * D, (part + 1) * D)
            inner = nn(normed, w_in[:, cut]) + bias_in[0:1, cut]
            square = inner * inner
            bend = jnp.tanh(inner * (rate + (rate * 0.044715) * square))
            half = 0.5 * inner
            activated = (half + half * bend).astype(BF16)
            slope = (0.5 + 0.5 * bend) + half * (1.0 - bend * bend) * (
                rate + (3.0 * rate * 0.044715) * square
            )
            grad_inner_wide = nt(cot, w_back[cut, :]) * slope
            grad_inner = grad_inner_wide.astype(BF16)
            acc_bias[0:1, cut] += jnp.sum(grad_inner.astype(F32), axis=0, keepdims=True)
            out = out + nn(activated, w_back[cut, :])
            grad_normed = grad_normed + nt(grad_inner, w_in[:, cut])
            acc_back[:, cut] += tn(cot, activated)
            acc_in[:, cut] += tn(normed, grad_inner)
        out_ref[...] = from_tokens(out).astype(BF16)
        acc_vec[0:1] += jnp.sum(grad_normed * hat, axis=0, keepdims=True)
        acc_vec[1:2] += jnp.sum(grad_normed, axis=0, keepdims=True)
        acc_vec[2:3] += jnp.sum(cot_wide, axis=0, keepdims=True)
        grad_mid = cot_wide + center_back(grad_normed * vectors[2:3], hat, inverse)
        grad_mid_ref[...] = grad_mid
        grad_branch = grad_mid.astype(BF16)
        acc_out[...] += tn(attended_ref[...], grad_branch)
        grad_att_ref[...] = nt(grad_branch, w_out[...]).astype(BF16)

        @pl.when(step == pl.num_programs(0) - 1)
        def _():
            flatten(flat, base, acc_out[...], ROW_OUT, 2)
            flatten(flat, base, acc_in[...], ROW_IN, 8)
            flatten(flat, base, acc_back[...].T, ROW_BACK, 2)
            for index, row in ((0, ROW_GAIN_TWO), (1, ROW_SHIFT_TWO), (2, ROW_BIAS_BACK)):
                for part in range(2):
                    flat[row - base + part : row - base + part + 1] = acc_vec[
                        index : index + 1, part * LANES : (part + 1) * LANES
                    ]
            for part in range(8):
                flat[ROW_BIAS_IN - base + part : ROW_BIAS_IN - base + part + 1] = acc_bias[
                    0:1, part * LANES : (part + 1) * LANES
                ]
            first_ref[...] = flat[ROW_OUT - base : ROW_OUT - base + 8]
            send_rows(plan, place_ref, flat, base, (keep_ref, send_ref), plan.lead, plan.deep)

    return kernel


def send_rows(plan, place_ref, flat, base, refs, low, high):
    plane_at, core_at = place_ref[1], place_ref[2]

    def write(own_core):
        for device in range(low * PLANE * CORES, high * PLANE * CORES):
            row = plan.first_row(device) - base
            ref = refs[(device % CORES) ^ own_core]
            ref[(device // CORES % PLANE) ^ plane_at, device // (PLANE * CORES) - low] = flat[
                row : row + plan.rows
            ].astype(BF16)

    for own_core in range(CORES):
        pl.when(core_at == own_core)(lambda own_core=own_core: write(own_core))


def attend_back_kernel(plan):
    def kernel(
        place_ref,
        x_ref,
        packed_ref,
        logsum_ref,
        grad_att_ref,
        grad_mid_ref,
        first_ref,
        w_qkv,
        vectors,
        grad_x_ref,
        keep_ref,
        send_ref,
        acc_qkv,
        acc_vec,
        flat,
    ):
        step = pl.program_id(0)

        @pl.when(step == 0)
        def _():
            for ref in (acc_qkv, acc_vec):
                ref[...] = jnp.zeros_like(ref)

        mask = allowed(vectors[SPAN : SPAN + 1, 0:1])
        scale = HEAD**-0.5
        tiles = []
        for half in range(2):
            rows = packed_ref[half * TILE : (half + 1) * TILE]
            grads = grad_att_ref[half * TILE : (half + 1) * TILE]
            pieces = [[], [], []]
            for head in range(HEADS):
                query = rows[:, head * HEAD : (head + 1) * HEAD]
                key = rows[:, D + head * HEAD : D + (head + 1) * HEAD]
                value = rows[:, 2 * D + head * HEAD : 2 * D + (head + 1) * HEAD]
                grad = grads[:, head * HEAD : (head + 1) * HEAD]
                slot = half * HEADS + head
                scores = nt(key, query) * scale - logsum_ref[0, slot : slot + 1]
                probs = jnp.exp(jnp.where(mask, scores, -1e30))
                grad_probs = nt(value, grad)
                weighted = probs * grad_probs
                total = jnp.sum(weighted, axis=0, keepdims=True)
                grad_scores = (weighted - probs * total).astype(BF16)
                pieces[0].append((tn(grad_scores, key) * scale).astype(BF16))
                pieces[1].append((nn(grad_scores, query) * scale).astype(BF16))
                pieces[2].append(nn(probs.astype(BF16), grad).astype(BF16))
            tiles.append(jnp.concatenate(pieces[0] + pieces[1] + pieces[2], axis=1))
        grad_packed = jnp.concatenate(tiles, axis=0)
        hat, inverse = center(read_block(x_ref))
        normed = (hat * vectors[0:1] + vectors[1:2]).astype(BF16)
        acc_qkv[...] += tn(normed, grad_packed)
        grad_normed = nt(grad_packed, w_qkv[...])
        acc_vec[0:1] += jnp.sum(grad_normed * hat, axis=0, keepdims=True)
        acc_vec[1:2] += jnp.sum(grad_normed, axis=0, keepdims=True)
        grad_x = grad_mid_ref[...] + center_back(grad_normed * vectors[0:1], hat, inverse)
        grad_x_ref[...] = from_tokens(grad_x).astype(BF16)

        @pl.when(step == pl.num_programs(0) - 1)
        def _():
            flatten(flat, 0, acc_qkv[...], ROW_QKV, 6)
            for index, row in ((0, ROW_GAIN_ONE), (1, ROW_SHIFT_ONE)):
                for part in range(2):
                    flat[row + part : row + part + 1] = acc_vec[
                        index : index + 1, part * LANES : (part + 1) * LANES
                    ]
            flat[ROW_OUT : ROW_OUT + 8] = first_ref[...]
            send_rows(plan, place_ref, flat, 0, (keep_ref, send_ref), 0, plan.lead)

    return kernel


def cut_kernel(group, steps):
    def kernel(rows_ref, cot_ref, out_ref):
        for member in range(group):
            for step in range(steps):
                column = (member * steps + step) * BLOCK
                for kind, ref in enumerate((rows_ref, cot_ref)):
                    out_ref[member, step, kind] = ref[:, column : column + BLOCK]

    return kernel


def whole(shape):
    return pl.BlockSpec(shape, lambda step: (0,) * len(shape))


def local(mesh_shape, tokens, column_rows, cotangent, flat_params):
    seq = mesh_shape["seq"]
    local_rows, columns = tokens.shape[1], tokens.shape[2]
    group = TALL // local_rows
    owned = columns // group
    steps = owned // BLOCK
    plan = Plan(seq, flat_params.shape[0])
    seq_at = lax.axis_index("seq")
    core_at = lax.axis_index("dp")
    deep_at, plane_at = seq_at // PLANE, seq_at % PLANE
    holder = seq_at % group * owned // STRIDE * (seq * STRIDE // columns)
    place = jnp.stack([deep_at, plane_at, core_at, holder]).astype(jnp.int32)
    shift = plan.shard * (seq_at * CORES + core_at) % LANES
    smem = pl.BlockSpec(memory_space=pltpu.SMEM)
    params = pltpu.CompilerParams(
        vmem_limit_bytes=VMEM_BYTES, dimension_semantics=("arbitrary",)
    )

    groups = [[group * g + i for i in range(group)] for g in range(seq // group)]
    deep_groups = [[PLANE * z + q for z in range(plan.deep)] for q in range(PLANE)]

    def exchange(blocks):
        return lax.all_to_all(blocks, "seq", 0, 0, axis_index_groups=groups, tiled=True)

    def to_rows(cols):
        moved = exchange(cols.reshape(group, local_rows, owned, D))
        return moved.transpose(1, 0, 2, 3).reshape(tokens.shape)

    def swap_seq(value, distance):
        return lax.ppermute(value, "seq", [(i, i ^ distance) for i in range(seq)])

    def swap_core(value):
        return lax.ppermute(value, "dp", [(0, 1), (1, 0)])

    blank = jnp.zeros((plan.rows - 1) * LANES, BF16)
    blank = jnp.concatenate([blank, jnp.broadcast_to(column_rows[0, 0].astype(BF16), (LANES,))])
    own = lax.dynamic_update_slice(blank, flat_params, (shift,)).reshape(plan.rows, LANES)
    if plan.pairwise:
        arrived = [swap_seq(own, PLANE * k) for k in range(1, plan.deep)]
        deep = jnp.stack([own] + arrived)
    else:
        arrived = [own]
        deep = lax.all_gather(own, "seq", axis=0, axis_index_groups=deep_groups)
    vmem = pl.BlockSpec(memory_space=pltpu.VMEM)
    both = pl.pallas_call(
        cut_kernel(group, steps),
        out_shape=jax.ShapeDtypeStruct((group, steps, 2, local_rows, BLOCK, D), BF16),
        in_specs=[vmem, vmem],
        out_specs=vmem,
        compiler_params=pltpu.CompilerParams(vmem_limit_bytes=VMEM_BYTES),
        name="cut",
    )(tokens.reshape(local_rows, columns, D), cotangent.reshape(local_rows, columns, D))
    deep, both = lax.optimization_barrier((deep, both))
    both = exchange(both)
    plane = [deep] + [swap_seq(deep, k) for k in range(1, PLANE)]
    pieces = plane + [swap_core(piece) for piece in plane]
    w_qkv, w_out, w_in, w_back, vectors, bias_in = prepare(plan)(place, *pieces)

    count = TALL * owned
    token_spec = lambda width: pl.BlockSpec((TOKENS, width), lambda step: (step, 0))
    grid_spec = pl.BlockSpec((TALL, BLOCK, D), lambda step: (0, step, 0))
    moved = (group, 1, 1, local_rows, BLOCK, D)
    x_spec = pl.BlockSpec(moved, lambda step: (0, step, 0, 0, 0, 0))
    cot_spec = pl.BlockSpec(moved, lambda step: (0, step, 1, 0, 0, 0))
    logsum_spec = pl.BlockSpec((1, 8, TILE), lambda step: (step, 0, 0))
    shape = jax.ShapeDtypeStruct
    packed, attended, middle, logsum = pl.pallas_call(
        forward_kernel,
        grid=(steps,),
        in_specs=[x_spec, whole((D, 3 * D)), whole((D, D)), whole((8, D))],
        out_specs=[token_spec(3 * D), token_spec(D), token_spec(D), logsum_spec],
        out_shape=[
            shape((count, 3 * D), BF16),
            shape((count, D), BF16),
            shape((count, D), F32),
            shape((steps, 8, TILE), F32),
        ],
        compiler_params=params,
        cost_estimate=pl.CostEstimate(
            flops=10**9, bytes_accessed=7 * 10**6, transcendentals=10**6
        ),
        name="forward",
    )(both, w_qkv, w_out, vectors)

    feed_rows = ROWS - (ROW_OUT - 4) + plan.rows
    parts_shape = lambda deep: (PLANE, deep, plan.rows, LANES)
    out, grad_att, grad_mid, keep, send, first = pl.pallas_call(
        feed_kernel(plan, group),
        grid=(steps,),
        in_specs=[
            smem,
            token_spec(D),
            token_spec(D),
            cot_spec,
            whole((D, D)),
            whole((D, FF)),
            whole((FF, D)),
            whole((8, D)),
            whole((8, FF)),
        ],
        out_specs=[
            grid_spec,
            token_spec(D),
            token_spec(D),
            *[whole(parts_shape(plan.deep - plan.lead))] * CORES,
            whole((8, LANES)),
        ],
        out_shape=[
            shape((TALL, owned, D), BF16),
            shape((count, D), BF16),
            shape((count, D), F32),
            *[shape(parts_shape(plan.deep - plan.lead), BF16)] * CORES,
            shape((8, LANES), F32),
        ],
        scratch_shapes=[
            pltpu.VMEM((D, FF), F32),
            pltpu.VMEM((D, FF), F32),
            pltpu.VMEM((D, D), F32),
            pltpu.VMEM((8, D), F32),
            pltpu.VMEM((8, FF), F32),
            pltpu.VMEM((feed_rows, LANES), F32),
        ],
        compiler_params=params,
        cost_estimate=pl.CostEstimate(
            flops=5 * 10**9, bytes_accessed=10**7, transcendentals=2 * 10**6
        ),
        name="feed",
    )(place, middle, attended, both, w_out, w_in, w_back, vectors, bias_in)

    layer_out = to_rows(out)

    def core_sum(keep, send):
        return keep.astype(F32) + swap_core(send).astype(F32)

    def plane_sum(value):
        total = value[0]
        sent = value.astype(BF16)
        for k in range(1, PLANE):
            total = total + swap_seq(sent[k], k).astype(F32)
        return total

    later = plane_sum(core_sum(keep, send))

    grad_x, lead_keep, lead_send = pl.pallas_call(
        attend_back_kernel(plan),
        grid=(steps,),
        in_specs=[
            smem,
            x_spec,
            token_spec(3 * D),
            logsum_spec,
            token_spec(D),
            token_spec(D),
            whole((8, LANES)),
            whole((D, 3 * D)),
            whole((8, D)),
        ],
        out_specs=[grid_spec, *[whole(parts_shape(plan.lead))] * CORES],
        out_shape=[
            shape((TALL, owned, D), BF16),
            *[shape(parts_shape(plan.lead), BF16)] * CORES,
        ],
        scratch_shapes=[
            pltpu.VMEM((D, 3 * D), F32),
            pltpu.VMEM((8, D), F32),
            pltpu.VMEM((ROW_OUT + plan.rows + 8, LANES), F32),
        ],
        compiler_params=params,
        cost_estimate=pl.CostEstimate(
            flops=10 * 10**9, bytes_accessed=8 * 10**6, transcendentals=10**6
        ),
        name="attend_back",
    )(place, both, packed, logsum, grad_att, grad_mid, first, w_qkv, vectors)
    (lead_keep, lead_send), layer_out, later = lax.optimization_barrier(
        ((lead_keep, lead_send), layer_out, later)
    )
    total = jnp.concatenate([plane_sum(core_sum(lead_keep, lead_send)), later], axis=0)
    moved_x = exchange(grad_x.reshape(group, local_rows, owned, D))
    total, moved_x = lax.optimization_barrier((total, moved_x))
    input_grad = moved_x.transpose(1, 0, 2, 3).reshape(tokens.shape).astype(F32)
    if plan.pairwise:
        sent = total.astype(BF16)
        result = lax.dynamic_index_in_dim(total, deep_at, 0, keepdims=False)
        for k in range(1, plan.deep):
            piece = lax.dynamic_index_in_dim(sent, deep_at ^ k, 0, keepdims=False)
            result = result + swap_seq(piece, PLANE * k).astype(F32)
    else:
        moved = lax.all_to_all(
            total.astype(BF16), "seq", 0, 0, axis_index_groups=deep_groups, tiled=True
        )
        result = jnp.sum(moved.astype(F32), axis=0)
    param_grad = lax.dynamic_slice(result.reshape(-1), (shift,), (plan.shard,))
    return layer_out, input_grad, param_grad


def solution(mesh):
    shape = dict(mesh.shape)
    rows = P("dp", "seq", None, None)
    flat = P(("seq", "dp"))
    return jax.shard_map(
        lambda *args: local(shape, *args),
        mesh=mesh,
        in_specs=(rows, P("dp", "seq"), rows, flat),
        out_specs=(rows, rows, flat),
        check_vma=False,
    )
```

```python
import jax
import jax.numpy as jnp
from jax import lax
from jax.experimental import pallas as pl
from jax.experimental.pallas import tpu as pltpu
from jax.sharding import PartitionSpec as P

D = 256
FF = 1024
HEADS = 2
HEAD = D // HEADS
TALL = 32
STRIDE = 96
EPSILON = 1e-05
LANES = 128
PLANE = 4
CORES = 2
BLOCK = 16
HALF = 8
TOKENS = TALL * BLOCK
TILE = TALL * HALF
VMEM_BYTES = 60 * 1024 * 1024

ROW_GAIN_ONE = 0
ROW_SHIFT_ONE = 2
ROW_QKV = 4
ROW_OUT = ROW_QKV + 6 * D
ROW_GAIN_TWO = ROW_OUT + 2 * D
ROW_SHIFT_TWO = ROW_GAIN_TWO + 2
ROW_IN = ROW_SHIFT_TWO + 2
ROW_BIAS_IN = ROW_IN + 8 * D
ROW_BACK = ROW_BIAS_IN + 8
ROW_BIAS_BACK = ROW_BACK + 2 * FF
ROWS = ROW_BIAS_BACK + 2

SPAN = 5

F32 = jnp.float32
BF16 = jnp.bfloat16


def nn(left, right):
    return lax.dot_general(left, right, (((1,), (0,)), ((), ())), preferred_element_type=F32)


def nt(left, right):
    return lax.dot_general(left, right, (((1,), (1,)), ((), ())), preferred_element_type=F32)


def tn(left, right):
    return lax.dot_general(left, right, (((0,), (0,)), ((), ())), preferred_element_type=F32)


def center(value):
    offset = value - jnp.mean(value, axis=-1, keepdims=True)
    inverse = lax.rsqrt(jnp.mean(offset * offset, axis=-1, keepdims=True) + EPSILON)
    return offset * inverse, inverse


def center_back(grad_hat, hat, inverse):
    mean_one = jnp.mean(grad_hat, axis=-1, keepdims=True)
    mean_two = jnp.mean(grad_hat * hat, axis=-1, keepdims=True)
    return inverse * (grad_hat - mean_one - hat * mean_two)


def allowed(span):
    key = lax.broadcasted_iota(jnp.int32, (TILE, TILE), 0)
    query = lax.broadcasted_iota(jnp.int32, (TILE, TILE), 1)
    same_column = (key % HALF) == (query % HALF)
    half_tile = TILE // 2
    same_image = (key // half_tile == query // half_tile) | (span >= TALL)
    return same_column & (key <= query) & same_image


class Plan:
    def __init__(self, seq, group, shard):
        self.shard = shard
        self.group = group
        self.deep = seq // PLANE
        self.count = seq * CORES
        self.pairwise = self.deep == 4
        rows = (shard + LANES - 2) // LANES + 2
        self.rows = -(-rows // 16) * 16
        self.lead = -(-(ROW_OUT * LANES) // (PLANE * CORES * shard))

    def first_row(self, device):
        return self.shard * device // LANES


def prepare(plan):
    def kernel(place_ref, *refs):
        sources, rest = refs[: CORES * PLANE], refs[CORES * PLANE :]
        w_qkv, w_out, w_in, w_back, vectors, bias_in, held, flat, sems = rest
        deep_at, plane_at, core_at = place_ref[0], place_ref[1], place_ref[2]
        copies = []
        for core in range(CORES):
            for plane in range(PLANE):
                source = sources[core * PLANE + plane]
                for deep in range(plan.deep):
                    slot = deep ^ deep_at if plan.pairwise else deep
                    copies.append(
                        pltpu.make_async_copy(
                            source.at[deep],
                            held.at[slot, plane ^ plane_at, core ^ core_at],
                            sems.at[len(copies)],
                        )
                    )
        for copy in copies:
            copy.start()
        for copy in copies:
            copy.wait()
        for device in range(plan.count):
            row = plan.first_row(device)
            value = held[device // 8, device // 2 % PLANE, device % CORES].astype(F32)
            if plan.shard * device % LANES:
                before = flat[row : row + 1]
                flat[row : row + plan.rows] = value
                flat[row : row + 1] = flat[row : row + 1] + before
            else:
                flat[row : row + plan.rows] = value
        for ref, row, wide in (
            (w_qkv, ROW_QKV, 6),
            (w_out, ROW_OUT, 2),
            (w_in, ROW_IN, 8),
            (w_back, ROW_BACK, 2),
        ):
            for part in range(wide):
                ref[:, part * LANES : (part + 1) * LANES] = flat[
                    pl.ds(row + part, ref.shape[0], stride=wide)
                ].astype(BF16)
        for index, row in enumerate(
            (ROW_GAIN_ONE, ROW_SHIFT_ONE, ROW_GAIN_TWO, ROW_SHIFT_TWO, ROW_BIAS_BACK)
        ):
            for part in range(2):
                vectors[index : index + 1, part * LANES : (part + 1) * LANES] = flat[
                    row + part : row + part + 1
                ]
        holder = place_ref[3]
        vectors[SPAN : SPAN + 1, :LANES] = held[holder // PLANE, holder % PLANE, core_at][
            plan.rows - 1 :
        ].astype(F32)
        for part in range(8):
            bias_in[0:1, part * LANES : (part + 1) * LANES] = flat[
                ROW_BIAS_IN + part : ROW_BIAS_IN + part + 1
            ]

    shapes = [((D, 3 * D), BF16), ((D, D), BF16), ((D, FF), BF16), ((FF, D), BF16)]
    shapes += [((8, D), F32), ((8, FF), F32)]
    return pl.pallas_call(
        kernel,
        out_shape=[jax.ShapeDtypeStruct(shape, kind) for shape, kind in shapes],
        in_specs=[pl.BlockSpec(memory_space=pltpu.SMEM)]
        + [pl.BlockSpec(memory_space=pl.ANY)] * (CORES * PLANE),
        out_specs=[pl.BlockSpec(memory_space=pltpu.VMEM)] * len(shapes),
        scratch_shapes=[
            pltpu.VMEM((plan.deep, PLANE, CORES, plan.rows, LANES), BF16),
            pltpu.VMEM((ROWS + plan.rows + 8, LANES), F32),
            pltpu.SemaphoreType.DMA((plan.count,)),
        ],
        compiler_params=pltpu.CompilerParams(vmem_limit_bytes=VMEM_BYTES),
        cost_estimate=pl.CostEstimate(flops=25500000000, bytes_accessed=4 * 10**6, transcendentals=0),
        name="prepare",
    )


SUB = 2
LOG2E = 1.4426950408889634
SCORE_RATE = HEAD**-0.5 * LOG2E
PIECE = 128
SLAB = 32
GELU_RATE = (2.0 / jnp.pi) ** 0.5
GELU_CUBE = GELU_RATE * 0.044715


def interleave(*lists):
    keyed = []
    for order, steps in enumerate(lists):
        for index, step in enumerate(steps):
            keyed.append(((index + 0.5) / len(steps), order, index, step))
    for _, _, _, step in sorted(keyed, key=lambda entry: entry[:3]):
        step()


def fold(value):
    return jnp.sum(value.reshape(-1, 8, value.shape[-1]), axis=0)


def column_sum(value):
    return jnp.sum(value, axis=0, keepdims=True)


class Copies:
    def __init__(self, sems):
        self.sems = sems
        self.used = 0

    def start(self, source, target):
        copy = pltpu.make_async_copy(source, target, self.sems.at[self.used])
        self.used += 1
        copy.start()
        return copy


def tile_rows(tile):
    return slice(tile * TILE, (tile + 1) * TILE)


def step_rows(step):
    return slice(step * TOKENS, (step + 1) * TOKENS)


def pieces_of(tile, size):
    return [
        slice(start, start + size) for start in range(tile * TILE, (tile + 1) * TILE, size)
    ]


def split(block):
    width = block.shape[-1]
    return [
        block[:, :, side * HALF : (side + 1) * HALF].reshape(-1, width) for side in range(2)
    ]


def join(left, right):
    width = left.shape[-1]
    return jnp.concatenate(
        [left.reshape(-1, HALF, width), right.reshape(-1, HALF, width)], axis=1
    )


def two_heads(value):
    blank = jnp.zeros((value.shape[0], HEAD), value.dtype)
    return jnp.concatenate(
        [
            jnp.concatenate([value[:, :HEAD], blank], axis=1),
            jnp.concatenate([blank, value[:, HEAD:]], axis=1),
        ],
        axis=0,
    )


def own_heads(value):
    rows = value.shape[0] // 2
    return jnp.concatenate([value[:rows, :HEAD], value[rows:, HEAD:]], axis=1)


def quarters():
    for head in range(HEADS):
        for part in range(TILE // LANES):
            yield (
                slice(head * TILE, head * TILE + (part + 1) * LANES),
                slice(part * LANES, (part + 1) * LANES),
                head,
            )


def caps(cap, keys, part):
    return cap[: keys.stop - keys.start, part]


def clear_later(*refs):
    for ref in refs:
        for head in range(HEADS):
            for part in range(TILE // LANES - 1):
                keys = slice(head * TILE + (part + 1) * LANES, (head + 1) * TILE)
                cut = slice(part * LANES, (part + 1) * LANES)
                ref[:, keys, cut] = jnp.zeros_like(ref[:, keys, cut])


def flatten(flat, base, matrix, row, wide):
    for part in range(wide):
        flat[pl.ds(row - base + part, matrix.shape[0], stride=wide)] = matrix[
            :, part * LANES : (part + 1) * LANES
        ]


def flatten_vector(flat, row, vector):
    for part in range(vector.shape[-1] // LANES):
        flat[row + part : row + part + 1] = vector[:, part * LANES : (part + 1) * LANES]


def send_rows(plan, place_ref, flat, base, refs, low, high):
    plane_at, core_at = place_ref[1], place_ref[2]

    def write(own_core):
        for device in range(low * PLANE * CORES, high * PLANE * CORES):
            row = plan.first_row(device) - base
            ref = refs[(device % CORES) ^ own_core]
            ref[(device // CORES % PLANE) ^ plane_at, device // (PLANE * CORES) - low] = flat[
                row : row + plan.rows
            ].astype(BF16)

    for own_core in range(CORES):
        pl.when(core_at == own_core)(lambda own_core=own_core: write(own_core))


class Sums:
    def __init__(self, **widths):
        for name, width in widths.items():
            setattr(self, name, jnp.zeros((8, width), F32))


def layer(plan, steps, local_rows):
    group, tiles, count = plan.group, 2 * steps, steps * TOKENS
    base = ROW_OUT - 4
    deep = plan.deep - plan.lead
    names = (
        "x_in", "cot_in", "wq", "wo", "wi", "wb", "normed", "packed", "scores", "probs", "cap",
        "attended", "middle", "hats", "inverses", "normed_two", "cots", "inner", "grad_act",
        "activated", "grad_inner", "grad_normed", "branch", "out_blocks", "acc_in", "acc_back",
        "acc_out", "flat", "keep_in", "send_in", "sems",
    )

    def kernel(place_ref, both, w_qkv, w_out, w_in, w_back, vectors, bias_in, *refs):
        packed_out, logsum, out, branch_out, keep, send, first = refs[:7]
        r = dict(zip(names, refs[7:]))
        x_in, cot_in, packed, middle, hats = (
            r[n] for n in ("x_in", "cot_in", "packed", "middle", "hats")
        )
        scores, probs, cap, attended = (r[n] for n in ("scores", "probs", "cap", "attended"))
        normed, normed_two, cots = r["normed"], r["normed_two"], r["cots"]
        inner, grad_act, activated, grad_inner = (
            r[n] for n in ("inner", "grad_act", "activated", "grad_inner")
        )
        inverses, grad_normed, branch, flat = (
            r[n] for n in ("inverses", "grad_normed", "branch", "flat")
        )
        copies = Copies(r["sems"])
        waits = {}
        arriving = [[copies.start(both.at[:, 0, 0], x_in.at[0])]]
        arriving[0] += [copies.start(w_qkv, r["wq"]), copies.start(w_out, r["wo"])]
        arriving.append([copies.start(both.at[:, 0, 1], cot_in.at[0])])
        arriving[1] += [copies.start(w_in, r["wi"]), copies.start(w_back, r["wb"])]
        for step in range(1, steps):
            arriving.append(
                [
                    copies.start(both.at[:, step, 0], x_in.at[step]),
                    copies.start(both.at[:, step, 1], cot_in.at[step]),
                ]
            )
        outs = []

        def arrive():
            for copy in arriving.pop(0):
                copy.wait()

        cap[...] = jnp.where(allowed(vectors[SPAN : SPAN + 1, 0:1]), jnp.inf, -1e30)
        clear_later(probs)
        sums = Sums(gain=D, shift=D, cot=D, **{f"bias{p}": D for p in range(FF // D)})

        def read_tokens(step):
            def one(index):
                members = slice(index * SUB, (index + 1) * SUB)
                value = x_in[step, members].astype(F32)
                hat, _ = center(value)
                hat = hat * vectors[0:1] + vectors[1:2]
                for side, (x_rows, n_rows) in enumerate(zip(split(value), split(hat))):
                    size = x_rows.shape[0]
                    start = (2 * step + side) * TILE + index * size
                    middle[start : start + size] = x_rows
                    normed[start : start + size] = n_rows.astype(BF16)

            return [lambda i=i: one(i) for i in range(group // SUB)]

        def read_cots(step):
            def one(index):
                members = slice(index * SUB, (index + 1) * SUB)
                for side, rows in enumerate(split(cot_in[step, members].astype(F32))):
                    size = rows.shape[0]
                    start = (2 * step + side) * TILE + index * size
                    cots[start : start + size] = rows.astype(BF16)
                    sums.cot = sums.cot + fold(rows)

            return [lambda i=i: one(i) for i in range(group // SUB)]

        def attention(tile):
            rows = tile_rows(tile)
            slot = tile % 2

            def project(part):
                cut = slice(part * D, (part + 1) * D)
                packed[rows, cut] = nn(normed[rows], r["wq"][:, cut]).astype(BF16)

            def score():
                scores[slot] = nt(two_heads(packed[rows, D : 2 * D]), packed[rows, :D])

            def soften(keys, part, head):
                value = jnp.minimum(scores[slot, keys, part] * SCORE_RATE, caps(cap, keys, part))
                peak = jnp.max(value, axis=0, keepdims=True)
                terms = jnp.exp2(value - peak)
                total = jnp.sum(terms, axis=0, keepdims=True)
                probs[slot, keys, part] = (terms * (1.0 / total)).astype(BF16)
                row = tile * HEADS + head
                logsum[row : row + 1, part] = peak + jnp.log2(total)

            def mix():
                attended[rows] = tn(probs[slot], two_heads(packed[rows, 2 * D :])).astype(BF16)

            def add():
                middle[rows] = middle[rows] + nn(attended[rows], r["wo"][...])

            def norm(piece):
                hat, inverse = center(middle[piece])
                hats[piece] = hat
                inverses[piece] = jnp.broadcast_to(inverse, (PIECE, LANES))
                normed_two[piece] = (hat * vectors[2:3] + vectors[3:4]).astype(BF16)

            return (
                [lambda p=p: project(p) for p in range(3)]
                + [score]
                + [lambda q=q: soften(*q) for q in quarters()]
                + [mix, add]
                + [lambda p=p: norm(p) for p in pieces_of(tile, PIECE)]
            )

        def expand(tile, part):
            rows, cut = tile_rows(tile), slice(part * D, (part + 1) * D)
            slot = part % 2

            def up():
                inner[slot] = nn(normed_two[rows], r["wi"][:, cut])

            def down():
                grad_act[slot] = nt(cots[rows], r["wb"][cut, :])

            return up, down

        def activate(tile, part, index):
            cut = slice(part * D, (part + 1) * D)
            slot = part % 2
            inside = slice(index * SLAB, (index + 1) * SLAB)
            rows = slice(tile * TILE + index * SLAB, tile * TILE + (index + 1) * SLAB)
            value = inner[slot, inside] + bias_in[0:1, cut]
            cube = value * (GELU_CUBE * (value * value))
            angle = GELU_RATE * value + cube
            bend = jnp.tanh(angle)
            gate = 0.5 * bend + 0.5
            activated[rows, cut] = (value * gate).astype(BF16)
            slope = gate * ((1.0 - bend) * (angle + (cube + cube)) + 1.0)
            grad = grad_act[slot, inside] * slope
            grad_inner[rows, cut] = grad.astype(BF16)
            name = f"bias{part}"
            setattr(sums, name, getattr(sums, name) + fold(grad))

        def hidden(tile):
            listed = []
            slabs = TILE // SLAB
            for part in range(FF // D):
                ahead = expand(tile, part + 1) if part + 1 < FF // D else ()
                for index in range(slabs):
                    if ahead and index % (slabs // 2) == 0:
                        listed.append(ahead[index // (slabs // 2)])
                    listed.append(lambda p=part, i=index: activate(tile, p, i))
            return listed

        def finish(tile):
            rows = tile_rows(tile)

            def second():
                middle[rows] = middle[rows] + nn(activated[rows], r["wb"][...])

            def back():
                grad_normed[rows] = nt(grad_inner[rows], r["wi"][...])

            def norm_back(piece):
                hat, grad = hats[piece], grad_normed[piece]
                inverse = jnp.concatenate([inverses[piece]] * 2, axis=1)
                sums.gain = sums.gain + fold(grad * hat)
                sums.shift = sums.shift + fold(grad)
                grad = cots[piece].astype(F32) + center_back(grad * vectors[2:3], hat, inverse)
                branch[piece] = grad.astype(BF16)

            return [second, back] + [lambda p=p: norm_back(p) for p in pieces_of(tile, PIECE)]

        def release(step):
            rows = step_rows(step)
            kept = {}

            def write(index):
                part = TALL // 4
                sides = []
                for side in range(2):
                    start = (2 * step + side) * TILE + index * part * HALF
                    sides.append(middle[start : start + part * HALF] + vectors[4:5])
                block = r["out_blocks"].at[step]
                block[index * part : (index + 1) * part] = join(*sides).astype(BF16)

            def turn_cots():
                kept["cots"] = cots[rows].T

            def turn_normed():
                kept["normed"] = normed_two[rows].T

            def add_to(ref, cut, value):
                if step == 0:
                    ref[:, cut] = value
                else:
                    ref[:, cut] += value

            def weigh(part):
                cut = slice(part * D, (part + 1) * D)
                add_to(r["acc_back"], cut, nn(kept["cots"], activated[rows, cut]))

            def weigh_in(part):
                cut = slice(part * D, (part + 1) * D)
                add_to(r["acc_in"], cut, nn(kept["normed"], grad_inner[rows, cut]))

            def weigh_out():
                add_to(r["acc_out"], slice(0, D), tn(attended[rows], branch[rows]))

            listed = [turn_cots, turn_normed]
            for part in range(FF // D):
                listed.append(lambda p=part: weigh(p))
                listed.append(lambda p=part: weigh_in(p))
                listed.append(lambda p=part: write(p))
            return listed + [weigh_out]

        def send_packed(step):
            rows = step_rows(step)
            outs.append(copies.start(packed.at[rows], packed_out.at[rows]))

        def send_step(step):
            rows = step_rows(step)
            outs.append(copies.start(branch.at[rows], branch_out.at[rows]))
            outs.append(
                copies.start(
                    r["out_blocks"].at[step], out.at[:, step * BLOCK : (step + 1) * BLOCK]
                )
            )

        arrive()
        for one in read_tokens(0) + attention(0):
            one()
        arrive()
        for one in read_cots(0) + list(expand(0, 0)):
            one()
        for tile in range(tiles):
            if tile % 2 and tile + 1 < tiles:
                arrive()
                send_packed(tile // 2)
                if tile > 3:
                    send_step((tile - 5) // 2)
            lists = [hidden(tile)]
            if tile + 1 < tiles:
                before = read_tokens((tile + 1) // 2) if tile % 2 else []
                after = list(expand(tile + 1, 0))
                if tile % 2:
                    after = read_cots((tile + 1) // 2) + after
                lists.append(before + attention(tile + 1) + after)
            if tile:
                lists.append(finish(tile - 1))
            if tile > 1 and tile % 2:
                lists.append(release((tile - 3) // 2))
            interleave(*lists)
        last = steps - 1
        send_packed(last)
        for step in range(max(0, (tiles - 1 - 5 + 1) // 2), last):
            send_step(step)
        for one in finish(tiles - 1):
            one()
        for one in release(last):
            one()
        send_step(last)
        flatten(flat, base, r["acc_back"][...].T, ROW_BACK, 2)
        flatten(flat, base, r["acc_in"][...], ROW_IN, 8)
        flatten(flat, base, r["acc_out"][...], ROW_OUT, 2)
        flatten_vector(flat, ROW_GAIN_TWO - base, column_sum(sums.gain))
        flatten_vector(flat, ROW_SHIFT_TWO - base, column_sum(sums.shift))
        flatten_vector(flat, ROW_BIAS_BACK - base, column_sum(sums.cot))
        for part in range(FF // D):
            flatten_vector(
                flat, ROW_BIAS_IN - base + 2 * part, column_sum(getattr(sums, f"bias{part}"))
            )
        first[...] = flat[ROW_OUT - base : ROW_OUT - base + 8]
        send_rows(
            plan, place_ref, flat, base, (r["keep_in"], r["send_in"]), plan.lead, plan.deep
        )
        outs.append(copies.start(r["send_in"], send))
        outs.append(copies.start(r["keep_in"], keep))
        for copy in outs:
            copy.wait()

    vmem = pl.BlockSpec(memory_space=pltpu.VMEM)
    hbm = pl.BlockSpec(memory_space=pl.ANY)
    shape = jax.ShapeDtypeStruct
    parts = (PLANE, deep, plan.rows, LANES)
    moved = pltpu.VMEM((steps, group, local_rows, BLOCK, D), BF16)
    wide = lambda width, kind: pltpu.VMEM((count, width), kind)
    pair = lambda rows, kind: pltpu.VMEM((2, rows, TILE), kind)
    scratch = dict(
        x_in=moved,
        cot_in=moved,
        wq=pltpu.VMEM((D, 3 * D), BF16),
        wo=pltpu.VMEM((D, D), BF16),
        wi=pltpu.VMEM((D, FF), BF16),
        wb=pltpu.VMEM((FF, D), BF16),
        normed=wide(D, BF16),
        packed=wide(3 * D, BF16),
        scores=pair(HEADS * TILE, F32),
        probs=pair(HEADS * TILE, BF16),
        cap=pltpu.VMEM((TILE, TILE), F32),
        attended=wide(D, BF16),
        middle=wide(D, F32),
        hats=wide(D, F32),
        inverses=wide(LANES, F32),
        normed_two=wide(D, BF16),
        cots=wide(D, BF16),
        inner=pair(TILE, F32),
        grad_act=pair(TILE, F32),
        activated=wide(FF, BF16),
        grad_inner=wide(FF, BF16),
        grad_normed=wide(D, F32),
        branch=wide(D, BF16),
        out_blocks=pltpu.VMEM((steps, TALL, BLOCK, D), BF16),
        acc_in=pltpu.VMEM((D, FF), F32),
        acc_back=pltpu.VMEM((D, FF), F32),
        acc_out=pltpu.VMEM((D, D), F32),
        flat=pltpu.VMEM((ROWS - base + plan.rows, LANES), F32),
        keep_in=pltpu.VMEM(parts, BF16),
        send_in=pltpu.VMEM(parts, BF16),
        sems=pltpu.SemaphoreType.DMA((6 + 5 * steps,)),
    )
    return pl.pallas_call(
        kernel,
        in_specs=[pl.BlockSpec(memory_space=pltpu.SMEM)] + [hbm] * 5 + [vmem] * 2,
        out_specs=[hbm, vmem, hbm, hbm, hbm, hbm, vmem],
        out_shape=[
            shape((count, 3 * D), BF16),
            shape((-(-tiles * HEADS // 8) * 8, TILE), F32),
            shape((TALL, steps * BLOCK, D), BF16),
            shape((count, D), BF16),
            shape(parts, BF16),
            shape(parts, BF16),
            shape((8, LANES), F32),
        ],
        scratch_shapes=[scratch[name] for name in names],
        compiler_params=pltpu.CompilerParams(vmem_limit_bytes=VMEM_BYTES),
        cost_estimate=pl.CostEstimate(
            flops=15 * 10**9, bytes_accessed=10**7, transcendentals=2 * 10**6
        ),
        name="layer",
    )


def back(plan, steps, local_rows):
    group, tiles, count = plan.group, 2 * steps, steps * TOKENS
    names = (
        "x_in", "packed_in", "branch_in", "wq", "wo", "hats", "inverses", "normed", "grad_att",
        "scores", "grad_probs", "probs", "grad_scores", "grad_packed", "grad_normed", "x_blocks",
        "cap", "acc", "flat", "keep_in", "send_in", "sems",
    )

    def kernel(place_ref, both, packed, branch, w_qkv, w_out, vectors, logsum, first, *refs):
        grad_x, keep, send = refs[:3]
        r = dict(zip(names, refs[3:]))
        x_in, packed_in, branch_in = r["x_in"], r["packed_in"], r["branch_in"]
        hats, inverses, normed, cap = r["hats"], r["inverses"], r["normed"], r["cap"]
        grad_att, scores, grad_probs = r["grad_att"], r["scores"], r["grad_probs"]
        probs, grad_scores = r["probs"], r["grad_scores"]
        grad_packed, grad_normed, flat = r["grad_packed"], r["grad_normed"], r["flat"]
        copies = Copies(r["sems"])
        arriving = []
        for step in range(steps):
            rows = step_rows(step)
            arriving.append([copies.start(branch.at[rows], branch_in.at[rows])])
            if step == 0:
                arriving[0].append(copies.start(w_out, r["wo"]))
            arriving[step].append(copies.start(packed.at[rows], packed_in.at[rows]))
            arriving[step].append(copies.start(both.at[:, step, 0], x_in.at[step]))
            if step == 0:
                arriving[0].append(copies.start(w_qkv, r["wq"]))

        def arrive():
            for copy in arriving.pop(0):
                copy.wait()

        outs = []
        cap[...] = jnp.where(allowed(vectors[SPAN : SPAN + 1, 0:1]), jnp.inf, -1e30)
        clear_later(probs, grad_scores)
        sums = Sums(gain=D, shift=D)
        scale = HEAD**-0.5

        def start(tile):
            rows, slot = tile_rows(tile), tile % 2

            def project():
                grad_att[rows] = nt(branch_in[rows], r["wo"][...]).astype(BF16)

            def score():
                scores[slot] = nt(two_heads(packed_in[rows, D : 2 * D]), packed_in[rows, :D])

            def spread():
                grad_probs[slot] = nt(two_heads(packed_in[rows, 2 * D :]), grad_att[rows])

            return [project, score, spread]

        def soften(tile):
            slot = tile % 2

            def one(keys, part, head):
                value = jnp.minimum(scores[slot, keys, part] * SCORE_RATE, caps(cap, keys, part))
                row = tile * HEADS + head
                prob = jnp.exp2(value - logsum[row : row + 1, part])
                weighted = prob * grad_probs[slot, keys, part]
                total = jnp.sum(weighted, axis=0, keepdims=True)
                probs[slot, keys, part] = prob.astype(BF16)
                grad_scores[slot, keys, part] = (weighted - prob * total).astype(BF16)

            return [lambda q=q: one(*q) for q in quarters()]

        def gather(tile):
            rows, slot = tile_rows(tile), tile % 2

            def queries():
                wide = two_heads(packed_in[rows, D : 2 * D])
                grad_packed[rows, :D] = (tn(grad_scores[slot], wide) * scale).astype(BF16)

            def keys():
                value = own_heads(nn(grad_scores[slot], packed_in[rows, :D]))
                grad_packed[rows, D : 2 * D] = (value * scale).astype(BF16)

            def values():
                value = own_heads(nn(probs[slot], grad_att[rows]))
                grad_packed[rows, 2 * D :] = value.astype(BF16)

            return [queries, keys, values]

        def read_tokens(step):
            def one(index):
                members = slice(index * SUB, (index + 1) * SUB)
                hat, inverse = center(x_in[step, members].astype(F32))
                inverse = jnp.broadcast_to(inverse, hat.shape[:-1] + (LANES,))
                for side, (h_rows, i_rows) in enumerate(zip(split(hat), split(inverse))):
                    size = h_rows.shape[0]
                    begin = (2 * step + side) * TILE + index * size
                    hats[begin : begin + size] = h_rows
                    inverses[begin : begin + size] = i_rows
                    normed[begin : begin + size] = (
                        h_rows * vectors[0:1] + vectors[1:2]
                    ).astype(BF16)

            return [lambda i=i: one(i) for i in range(group // SUB)]

        def finish(tile):
            rows = tile_rows(tile)

            def spread():
                grad_normed[rows] = nt(grad_packed[rows], r["wq"][...])

            def norm_back(piece):
                hat, grad = hats[piece], grad_normed[piece]
                inverse = jnp.concatenate([inverses[piece]] * 2, axis=1)
                sums.gain = sums.gain + fold(grad * hat)
                sums.shift = sums.shift + fold(grad)
                grad = branch_in[piece].astype(F32) + center_back(
                    grad * vectors[0:1], hat, inverse
                )
                grad_normed[piece] = grad

            return [spread] + [lambda p=p: norm_back(p) for p in pieces_of(tile, PIECE)]

        def release(step):
            rows = step_rows(step)
            kept = {}

            def write(index):
                part = TALL // 4
                sides = []
                for side in range(2):
                    begin = (2 * step + side) * TILE + index * part * HALF
                    sides.append(grad_normed[begin : begin + part * HALF])
                block = r["x_blocks"].at[step]
                block[index * part : (index + 1) * part] = join(*sides).astype(BF16)

            def turn():
                kept["normed"] = normed[rows].T

            def weigh(part):
                cut = slice(part * D, (part + 1) * D)
                value = nn(kept["normed"], grad_packed[rows, cut])
                if step == 0:
                    r["acc"][:, cut] = value
                else:
                    r["acc"][:, cut] += value

            return (
                [lambda i=i: write(i) for i in range(4)]
                + [turn]
                + [lambda p=p: weigh(p) for p in range(3)]
            )

        def send_step(step):
            outs.append(
                copies.start(
                    r["x_blocks"].at[step], grad_x.at[:, step * BLOCK : (step + 1) * BLOCK]
                )
            )

        arrive()
        for one in start(0):
            one()
        for tile in range(tiles):
            if tile % 2 and tile + 1 < tiles:
                arrive()
            lists = [soften(tile) + gather(tile)]
            if tile + 1 < tiles:
                lists.append(start(tile + 1))
            if tile % 2 == 0:
                lists.append(read_tokens(tile // 2))
            if tile:
                lists.append(finish(tile - 1))
            if tile > 1 and tile % 2:
                lists.append(release((tile - 3) // 2))
            interleave(*lists)
        for one in finish(tiles - 1):
            one()
        for step in range(steps - 1):
            send_step(step)
        for one in release(steps - 1):
            one()
        send_step(steps - 1)
        flatten(flat, 0, r["acc"][...], ROW_QKV, 6)
        flatten_vector(flat, ROW_GAIN_ONE, column_sum(sums.gain))
        flatten_vector(flat, ROW_SHIFT_ONE, column_sum(sums.shift))
        flat[ROW_OUT : ROW_OUT + 8] = first[...]
        send_rows(plan, place_ref, flat, 0, (r["keep_in"], r["send_in"]), 0, plan.lead)
        outs.append(copies.start(r["send_in"], send))
        outs.append(copies.start(r["keep_in"], keep))
        for copy in outs:
            copy.wait()

    vmem = pl.BlockSpec(memory_space=pltpu.VMEM)
    hbm = pl.BlockSpec(memory_space=pl.ANY)
    shape = jax.ShapeDtypeStruct
    parts = (PLANE, plan.lead, plan.rows, LANES)
    wide = lambda width, kind: pltpu.VMEM((count, width), kind)
    pair = lambda kind: pltpu.VMEM((2, HEADS * TILE, TILE), kind)
    scratch = dict(
        x_in=pltpu.VMEM((steps, group, local_rows, BLOCK, D), BF16),
        packed_in=wide(3 * D, BF16),
        branch_in=wide(D, BF16),
        wq=pltpu.VMEM((D, 3 * D), BF16),
        wo=pltpu.VMEM((D, D), BF16),
        hats=wide(D, F32),
        inverses=wide(LANES, F32),
        normed=wide(D, BF16),
        grad_att=wide(D, BF16),
        scores=pair(F32),
        grad_probs=pair(F32),
        probs=pair(BF16),
        grad_scores=pair(BF16),
        grad_packed=wide(3 * D, BF16),
        grad_normed=wide(D, F32),
        x_blocks=pltpu.VMEM((steps, TALL, BLOCK, D), BF16),
        cap=pltpu.VMEM((TILE, TILE), F32),
        acc=pltpu.VMEM((D, 3 * D), F32),
        flat=pltpu.VMEM((ROW_OUT + plan.rows + 8, LANES), F32),
        keep_in=pltpu.VMEM(parts, BF16),
        send_in=pltpu.VMEM(parts, BF16),
        sems=pltpu.SemaphoreType.DMA((4 + 4 * steps,)),
    )
    return pl.pallas_call(
        kernel,
        in_specs=[pl.BlockSpec(memory_space=pltpu.SMEM)] + [hbm] * 5 + [vmem] * 3,
        out_specs=[hbm] * 3,
        out_shape=[
            shape((TALL, steps * BLOCK, D), BF16),
            shape(parts, BF16),
            shape(parts, BF16),
        ],
        scratch_shapes=[scratch[name] for name in names],
        compiler_params=pltpu.CompilerParams(vmem_limit_bytes=VMEM_BYTES),
        cost_estimate=pl.CostEstimate(
            flops=10 * 10**9, bytes_accessed=8 * 10**6, transcendentals=10**6
        ),
        name="back",
    )


def cut_kernel(group, steps):
    def kernel(rows_ref, cot_ref, out_ref):
        for member in range(group):
            for step in range(steps):
                column = (member * steps + step) * BLOCK
                for kind, ref in enumerate((rows_ref, cot_ref)):
                    out_ref[member, step, kind] = ref[:, column : column + BLOCK]

    return kernel


def local(mesh_shape, tokens, column_rows, cotangent, flat_params):
    seq = mesh_shape["seq"]
    local_rows, columns = tokens.shape[1], tokens.shape[2]
    group = TALL // local_rows
    owned = columns // group
    steps = owned // BLOCK
    plan = Plan(seq, group, flat_params.shape[0])
    seq_at = lax.axis_index("seq")
    core_at = lax.axis_index("dp")
    deep_at, plane_at = seq_at // PLANE, seq_at % PLANE
    holder = seq_at % group * owned // STRIDE * (seq * STRIDE // columns)
    place = jnp.stack([deep_at, plane_at, core_at, holder]).astype(jnp.int32)
    shift = plan.shard * (seq_at * CORES + core_at) % LANES
    groups = [[group * g + i for i in range(group)] for g in range(seq // group)]
    deep_groups = [[PLANE * z + q for z in range(plan.deep)] for q in range(PLANE)]

    def exchange(blocks):
        return lax.all_to_all(blocks, "seq", 0, 0, axis_index_groups=groups, tiled=True)

    def to_rows(cols):
        moved = exchange(cols.reshape(group, local_rows, owned, D))
        return moved.transpose(1, 0, 2, 3).reshape(tokens.shape)

    def swap_seq(value, distance):
        return lax.ppermute(value, "seq", [(i, i ^ distance) for i in range(seq)])

    def swap_core(value):
        return lax.ppermute(value, "dp", [(0, 1), (1, 0)])

    blank = jnp.zeros((plan.rows - 1) * LANES, BF16)
    blank = jnp.concatenate([blank, jnp.broadcast_to(column_rows[0, 0].astype(BF16), (LANES,))])
    own = lax.dynamic_update_slice(blank, flat_params, (shift,)).reshape(plan.rows, LANES)
    if plan.pairwise:
        arrived = [swap_seq(own, PLANE * k) for k in range(1, plan.deep)]
        deep = jnp.stack([own] + arrived)
    else:
        arrived = [own]
        deep = lax.all_gather(own, "seq", axis=0, axis_index_groups=deep_groups)
    vmem = pl.BlockSpec(memory_space=pltpu.VMEM)
    both = pl.pallas_call(
        cut_kernel(group, steps),
        out_shape=jax.ShapeDtypeStruct((group, steps, 2, local_rows, BLOCK, D), BF16),
        in_specs=[vmem, vmem],
        out_specs=vmem,
        compiler_params=pltpu.CompilerParams(vmem_limit_bytes=VMEM_BYTES),
        name="cut",
    )(tokens.reshape(local_rows, columns, D), cotangent.reshape(local_rows, columns, D))
    deep, both = lax.optimization_barrier((deep, both))
    both = exchange(both)
    plane = [deep] + [swap_seq(deep, k) for k in range(1, PLANE)]
    pieces = plane + [swap_core(piece) for piece in plane]
    w_qkv, w_out, w_in, w_back, vectors, bias_in = prepare(plan)(place, *pieces)

    packed, logsum, out, branch, keep, send, first = layer(plan, steps, local_rows)(
        place, both, w_qkv, w_out, w_in, w_back, vectors, bias_in
    )

    layer_out = to_rows(out)

    def core_sum(keep, send):
        return keep.astype(F32) + swap_core(send).astype(F32)

    def plane_sum(value):
        total = value[0]
        sent = value.astype(BF16)
        for k in range(1, PLANE):
            total = total + swap_seq(sent[k], k).astype(F32)
        return total

    later = plane_sum(core_sum(keep, send))

    grad_x, lead_keep, lead_send = back(plan, steps, local_rows)(
        place, both, packed, branch, w_qkv, w_out, vectors, logsum, first
    )
    (lead_keep, lead_send), layer_out, later = lax.optimization_barrier(
        ((lead_keep, lead_send), layer_out, later)
    )
    total = jnp.concatenate([plane_sum(core_sum(lead_keep, lead_send)), later], axis=0)
    moved_x = exchange(grad_x.reshape(group, local_rows, owned, D))
    total, moved_x = lax.optimization_barrier((total, moved_x))
    input_grad = moved_x.transpose(1, 0, 2, 3).reshape(tokens.shape).astype(F32)
    if plan.pairwise:
        sent = total.astype(BF16)
        result = lax.dynamic_index_in_dim(total, deep_at, 0, keepdims=False)
        for k in range(1, plan.deep):
            piece = lax.dynamic_index_in_dim(sent, deep_at ^ k, 0, keepdims=False)
            result = result + swap_seq(piece, PLANE * k).astype(F32)
    else:
        moved = lax.all_to_all(
            total.astype(BF16), "seq", 0, 0, axis_index_groups=deep_groups, tiled=True
        )
        result = jnp.sum(moved.astype(F32), axis=0)
    param_grad = lax.dynamic_slice(result.reshape(-1), (shift,), (plan.shard,))
    return layer_out, input_grad, param_grad


def solution(mesh):
    shape = dict(mesh.shape)
    rows = P("dp", "seq", None, None)
    flat = P(("seq", "dp"))
    return jax.shard_map(
        lambda *args: local(shape, *args),
        mesh=mesh,
        in_specs=(rows, P("dp", "seq"), rows, flat),
        out_specs=(rows, rows, flat),
        check_vma=False,
    )
```

```python
import jax
import jax.numpy as jnp
from jax import lax
from jax.experimental import pallas as pl
from jax.experimental.pallas import tpu as pltpu
from jax.sharding import PartitionSpec as P

D = 256
FF = 1024
HEADS = 2
HEAD = D // HEADS
TALL = 32
STRIDE = 96
EPSILON = 1e-05
LANES = 128
PLANE = 4
CORES = 2
BLOCK = 16
HALF = 8
TOKENS = TALL * BLOCK
TILE = TALL * HALF
VMEM_BYTES = 63 * 1024 * 1024

ROW_GAIN_ONE = 0
ROW_SHIFT_ONE = 2
ROW_QKV = 4
ROW_OUT = ROW_QKV + 6 * D
ROW_GAIN_TWO = ROW_OUT + 2 * D
ROW_SHIFT_TWO = ROW_GAIN_TWO + 2
ROW_IN = ROW_SHIFT_TWO + 2
ROW_BIAS_IN = ROW_IN + 8 * D
ROW_BACK = ROW_BIAS_IN + 8
ROW_BIAS_BACK = ROW_BACK + 2 * FF
ROWS = ROW_BIAS_BACK + 2

SPAN = 5

F32 = jnp.float32
BF16 = jnp.bfloat16


def nn(left, right):
    return lax.dot_general(left, right, (((1,), (0,)), ((), ())), preferred_element_type=F32)


def nt(left, right):
    return lax.dot_general(left, right, (((1,), (1,)), ((), ())), preferred_element_type=F32)


def tn(left, right):
    return lax.dot_general(left, right, (((0,), (0,)), ((), ())), preferred_element_type=F32)


def center(value):
    offset = value - jnp.mean(value, axis=-1, keepdims=True)
    inverse = lax.rsqrt(jnp.mean(offset * offset, axis=-1, keepdims=True) + EPSILON)
    return offset * inverse, inverse


def center_back(grad_hat, hat, inverse):
    mean_one = jnp.mean(grad_hat, axis=-1, keepdims=True)
    mean_two = jnp.mean(grad_hat * hat, axis=-1, keepdims=True)
    return inverse * (grad_hat - mean_one - hat * mean_two)


def allowed(span):
    key = lax.broadcasted_iota(jnp.int32, (TILE, TILE), 0)
    query = lax.broadcasted_iota(jnp.int32, (TILE, TILE), 1)
    same_column = (key % HALF) == (query % HALF)
    half_tile = TILE // 2
    same_image = (key // half_tile == query // half_tile) | (span >= TALL)
    return same_column & (key <= query) & same_image


class Plan:
    def __init__(self, seq, group, shard):
        self.shard = shard
        self.group = group
        self.deep = seq // PLANE
        self.count = seq * CORES
        self.pairwise = self.deep == 4
        rows = (shard + LANES - 2) // LANES + 2
        self.rows = -(-rows // 16) * 16
        self.lead = -(-(ROW_OUT * LANES) // (PLANE * CORES * shard))

    def first_row(self, device):
        return self.shard * device // LANES


def prepare(plan):
    def kernel(place_ref, *refs):
        sources, rest = refs[: CORES * PLANE], refs[CORES * PLANE :]
        w_qkv, w_out, w_in, w_back, vectors, bias_in, held, flat, sems = rest
        deep_at, plane_at, core_at = place_ref[0], place_ref[1], place_ref[2]
        copies = []
        for core in range(CORES):
            for plane in range(PLANE):
                source = sources[core * PLANE + plane]
                for deep in range(plan.deep):
                    slot = deep ^ deep_at if plan.pairwise else deep
                    copies.append(
                        pltpu.make_async_copy(
                            source.at[deep],
                            held.at[slot, plane ^ plane_at, core ^ core_at],
                            sems.at[len(copies)],
                        )
                    )
        for copy in copies:
            copy.start()
        for copy in copies:
            copy.wait()
        for device in range(plan.count):
            row = plan.first_row(device)
            value = held[device // 8, device // 2 % PLANE, device % CORES].astype(F32)
            if plan.shard * device % LANES:
                before = flat[row : row + 1]
                flat[row : row + plan.rows] = value
                flat[row : row + 1] = flat[row : row + 1] + before
            else:
                flat[row : row + plan.rows] = value
        for ref, row, wide in (
            (w_qkv, ROW_QKV, 6),
            (w_out, ROW_OUT, 2),
            (w_in, ROW_IN, 8),
            (w_back, ROW_BACK, 2),
        ):
            for part in range(wide):
                ref[:, part * LANES : (part + 1) * LANES] = flat[
                    pl.ds(row + part, ref.shape[0], stride=wide)
                ].astype(BF16)
        for index, row in enumerate(
            (ROW_GAIN_ONE, ROW_SHIFT_ONE, ROW_GAIN_TWO, ROW_SHIFT_TWO, ROW_BIAS_BACK)
        ):
            for part in range(2):
                vectors[index : index + 1, part * LANES : (part + 1) * LANES] = flat[
                    row + part : row + part + 1
                ]
        holder = place_ref[3]
        vectors[SPAN : SPAN + 1, :LANES] = held[holder // PLANE, holder % PLANE, core_at][
            plan.rows - 1 :
        ].astype(F32)
        for part in range(8):
            bias_in[0:1, part * LANES : (part + 1) * LANES] = flat[
                ROW_BIAS_IN + part : ROW_BIAS_IN + part + 1
            ]

    shapes = [((D, 3 * D), BF16), ((D, D), BF16), ((D, FF), BF16), ((FF, D), BF16)]
    shapes += [((8, D), F32), ((8, FF), F32)]
    return pl.pallas_call(
        kernel,
        out_shape=[jax.ShapeDtypeStruct(shape, kind) for shape, kind in shapes],
        in_specs=[pl.BlockSpec(memory_space=pltpu.SMEM)]
        + [pl.BlockSpec(memory_space=pl.ANY)] * (CORES * PLANE),
        out_specs=[pl.BlockSpec(memory_space=pltpu.VMEM)] * len(shapes),
        scratch_shapes=[
            pltpu.VMEM((plan.deep, PLANE, CORES, plan.rows, LANES), BF16),
            pltpu.VMEM((ROWS + plan.rows + 8, LANES), F32),
            pltpu.SemaphoreType.DMA((plan.count,)),
        ],
        compiler_params=pltpu.CompilerParams(vmem_limit_bytes=VMEM_BYTES),
        cost_estimate=pl.CostEstimate(flops=25500000000, bytes_accessed=4 * 10**6, transcendentals=0),
        name="prepare",
    )


SUB = 2
LOG2E = 1.4426950408889634
SCORE_RATE = HEAD**-0.5 * LOG2E
PIECE = 128
SLAB = 32
GELU_RATE = (2.0 / jnp.pi) ** 0.5
GELU_CUBE = GELU_RATE * 0.044715


def interleave(*lists):
    keyed = []
    for order, steps in enumerate(lists):
        for index, step in enumerate(steps):
            keyed.append(((index + 0.5) / len(steps), order, index, step))
    for _, _, _, step in sorted(keyed, key=lambda entry: entry[:3]):
        step()


def fold(value):
    return jnp.sum(value.reshape(-1, 8, value.shape[-1]), axis=0)


def column_sum(value):
    return jnp.sum(value, axis=0, keepdims=True)


class Copies:
    def __init__(self, sems):
        self.sems = sems
        self.used = 0

    def start(self, source, target):
        copy = pltpu.make_async_copy(source, target, self.sems.at[self.used])
        self.used += 1
        copy.start()
        return copy


def tile_rows(tile):
    return slice(tile * TILE, (tile + 1) * TILE)


def step_rows(step):
    return slice(step * TOKENS, (step + 1) * TOKENS)


def pieces_of(tile, size):
    return [
        slice(start, start + size) for start in range(tile * TILE, (tile + 1) * TILE, size)
    ]


def split(block):
    width = block.shape[-1]
    return [
        block[:, :, side * HALF : (side + 1) * HALF].reshape(-1, width) for side in range(2)
    ]


def join(left, right):
    width = left.shape[-1]
    return jnp.concatenate(
        [left.reshape(-1, HALF, width), right.reshape(-1, HALF, width)], axis=1
    )


def two_heads(value):
    blank = jnp.zeros((value.shape[0], HEAD), value.dtype)
    return jnp.concatenate(
        [
            jnp.concatenate([value[:, :HEAD], blank], axis=1),
            jnp.concatenate([blank, value[:, HEAD:]], axis=1),
        ],
        axis=0,
    )


def own_heads(value):
    rows = value.shape[0] // 2
    return jnp.concatenate([value[:rows, :HEAD], value[rows:, HEAD:]], axis=1)


def quarters():
    for head in range(HEADS):
        for part in range(TILE // LANES):
            yield (
                slice(head * TILE, head * TILE + (part + 1) * LANES),
                slice(part * LANES, (part + 1) * LANES),
                head,
            )


def caps(cap, keys, part):
    return cap[: keys.stop - keys.start, part]


def clear_later(*refs):
    for ref in refs:
        for head in range(HEADS):
            for part in range(TILE // LANES - 1):
                keys = slice(head * TILE + (part + 1) * LANES, (head + 1) * TILE)
                cut = slice(part * LANES, (part + 1) * LANES)
                ref[:, keys, cut] = jnp.zeros_like(ref[:, keys, cut])


def flatten(flat, base, matrix, row, wide):
    for part in range(wide):
        flat[pl.ds(row - base + part, matrix.shape[0], stride=wide)] = matrix[
            :, part * LANES : (part + 1) * LANES
        ]


def flatten_vector(flat, row, vector):
    for part in range(vector.shape[-1] // LANES):
        flat[row + part : row + part + 1] = vector[:, part * LANES : (part + 1) * LANES]


def send_rows(plan, place_ref, flat, base, parts, low, high):
    plane_at, core_at = place_ref[1], place_ref[2]
    for device in range(low * PLANE * CORES, high * PLANE * CORES):
        row = plan.first_row(device) - base
        parts[
            (device % CORES) ^ core_at,
            (device // CORES % PLANE) ^ plane_at,
            device // (PLANE * CORES) - low,
        ] = flat[row : row + plan.rows].astype(BF16)


class Sums:
    def __init__(self, **widths):
        for name, width in widths.items():
            setattr(self, name, jnp.zeros((8, width), F32))


def layer(plan, steps, local_rows):
    group, tiles, count = plan.group, 2 * steps, steps * TOKENS
    base = ROW_OUT - 4
    deep = plan.deep - plan.lead
    names = (
        "x_in", "cot_in", "wq", "wo", "wi", "wb", "normed", "packed", "scores", "probs", "cap",
        "attended", "middle", "hats", "inverses", "normed_two", "cots", "inner", "grad_act",
        "activated", "grad_inner", "grad_normed", "branch", "out_blocks", "acc_in", "acc_back",
        "acc_out", "flat", "parts_in", "sems",
    )

    def kernel(place_ref, both, w_qkv, w_out, w_in, w_back, vectors, bias_in, *refs):
        packed_out, logsum, out, branch_out, keep, send, first = refs[:7]
        r = dict(zip(names, refs[7:]))
        x_in, cot_in, packed, middle, hats = (
            r[n] for n in ("x_in", "cot_in", "packed", "middle", "hats")
        )
        scores, probs, cap, attended = (r[n] for n in ("scores", "probs", "cap", "attended"))
        normed, normed_two, cots = r["normed"], r["normed_two"], r["cots"]
        inner, grad_act, activated, grad_inner = (
            r[n] for n in ("inner", "grad_act", "activated", "grad_inner")
        )
        inverses, grad_normed, branch, flat = (
            r[n] for n in ("inverses", "grad_normed", "branch", "flat")
        )
        copies = Copies(r["sems"])
        waits = {}
        arriving = [[copies.start(both.at[:, 0, 0], x_in.at[0])]]
        arriving[0].append(copies.start(w_qkv, r["wq"]))
        arriving.append([copies.start(both.at[:, 1, 0], x_in.at[1])])
        arriving[1].append(copies.start(w_out, r["wo"]))
        arriving.append([copies.start(both.at[:, 0, 1], cot_in.at[0])])
        arriving[2] += [copies.start(w_in, r["wi"]), copies.start(w_back, r["wb"])]
        arriving[2] += [
            copies.start(both.at[:, step, 0], x_in.at[step]) for step in range(2, steps)
        ]
        arriving.append(
            [copies.start(both.at[:, step, 1], cot_in.at[step]) for step in range(1, steps)]
        )
        outs = []

        def arrive():
            for copy in arriving.pop(0):
                copy.wait()

        cap[...] = jnp.where(allowed(vectors[SPAN : SPAN + 1, 0:1]), jnp.inf, -1e30)
        clear_later(probs)
        sums = Sums(gain=D, shift=D, cot=D, **{f"bias{p}": D for p in range(FF // D)})

        def read_tokens(step):
            def one(index):
                members = slice(index * SUB, (index + 1) * SUB)
                value = x_in[step, members].astype(F32)
                hat, _ = center(value)
                hat = hat * vectors[0:1] + vectors[1:2]
                for side, (x_rows, n_rows) in enumerate(zip(split(value), split(hat))):
                    size = x_rows.shape[0]
                    start = (2 * step + side) * TILE + index * size
                    middle[start : start + size] = x_rows
                    normed[start : start + size] = n_rows.astype(BF16)

            return [lambda i=i: one(i) for i in range(group // SUB)]

        def read_cots(step):
            def one(index):
                members = slice(index * SUB, (index + 1) * SUB)
                for side, rows in enumerate(split(cot_in[step, members].astype(F32))):
                    size = rows.shape[0]
                    start = (2 * step + side) * TILE + index * size
                    cots[start : start + size] = rows.astype(BF16)
                    sums.cot = sums.cot + fold(rows)

            return [lambda i=i: one(i) for i in range(group // SUB)]

        def attention(tile):
            rows = tile_rows(tile)
            slot = tile % 2

            def project(part):
                cut = slice(part * D, (part + 1) * D)
                packed[rows, cut] = nn(normed[rows], r["wq"][:, cut]).astype(BF16)

            def score():
                scores[slot] = nt(two_heads(packed[rows, D : 2 * D]), packed[rows, :D])

            def soften(keys, part, head):
                value = jnp.minimum(scores[slot, keys, part] * SCORE_RATE, caps(cap, keys, part))
                peak = jnp.max(value, axis=0, keepdims=True)
                terms = jnp.exp2(value - peak)
                total = jnp.sum(terms, axis=0, keepdims=True)
                probs[slot, keys, part] = (terms * (1.0 / total)).astype(BF16)
                row = tile * HEADS + head
                logsum[row : row + 1, part] = peak + jnp.log2(total)

            def mix():
                attended[rows] = tn(probs[slot], two_heads(packed[rows, 2 * D :])).astype(BF16)

            def add():
                middle[rows] = middle[rows] + nn(attended[rows], r["wo"][...])

            def norm(piece):
                hat, inverse = center(middle[piece])
                hats[piece] = hat
                inverses[piece] = jnp.broadcast_to(inverse, (PIECE, LANES))
                normed_two[piece] = (hat * vectors[2:3] + vectors[3:4]).astype(BF16)

            return (
                [lambda p=p: project(p) for p in range(3)],
                [score] + [lambda q=q: soften(*q) for q in quarters()],
                [mix, add] + [lambda p=p: norm(p) for p in pieces_of(tile, PIECE)],
            )

        def expand(tile, part):
            rows, cut = tile_rows(tile), slice(part * D, (part + 1) * D)
            slot = part

            def up():
                inner[slot] = nn(normed_two[rows], r["wi"][:, cut])

            def down():
                grad_act[slot] = nt(cots[rows], r["wb"][cut, :])

            return up, down

        def activate(tile, part, index):
            cut = slice(part * D, (part + 1) * D)
            slot = part
            inside = slice(index * SLAB, (index + 1) * SLAB)
            rows = slice(tile * TILE + index * SLAB, tile * TILE + (index + 1) * SLAB)
            value = inner[slot, inside] + bias_in[0:1, cut]
            cube = value * (GELU_CUBE * (value * value))
            angle = GELU_RATE * value + cube
            bend = jnp.tanh(angle)
            gate = 0.5 * bend + 0.5
            activated[rows, cut] = (value * gate).astype(BF16)
            slope = gate * ((1.0 - bend) * (angle + (cube + cube)) + 1.0)
            grad = grad_act[slot, inside] * slope
            grad_inner[rows, cut] = grad.astype(BF16)
            name = f"bias{part}"
            setattr(sums, name, getattr(sums, name) + fold(grad))

        def hidden(tile):
            listed = []
            slabs = TILE // SLAB
            for part in range(FF // D):
                ahead = expand(tile, part + 1) if part + 1 < FF // D else ()
                for index in range(slabs):
                    if ahead and index % (slabs // 2) == 0:
                        listed.append(ahead[index // (slabs // 2)])
                    listed.append(lambda p=part, i=index: activate(tile, p, i))
            return listed

        def finish(tile):
            rows = tile_rows(tile)

            def second():
                middle[rows] = middle[rows] + nn(activated[rows], r["wb"][...])

            def back():
                grad_normed[rows] = nt(grad_inner[rows], r["wi"][...])

            def norm_back(piece):
                hat, grad = hats[piece], grad_normed[piece]
                inverse = jnp.concatenate([inverses[piece]] * 2, axis=1)
                sums.gain = sums.gain + fold(grad * hat)
                sums.shift = sums.shift + fold(grad)
                grad = cots[piece].astype(F32) + center_back(grad * vectors[2:3], hat, inverse)
                branch[piece] = grad.astype(BF16)

            return [second, back] + [lambda p=p: norm_back(p) for p in pieces_of(tile, PIECE)]

        def release(step):
            rows = step_rows(step)
            kept = {}

            def write(index):
                part = TALL // 4
                sides = []
                for side in range(2):
                    start = (2 * step + side) * TILE + index * part * HALF
                    sides.append(middle[start : start + part * HALF] + vectors[4:5])
                block = r["out_blocks"].at[step]
                block[index * part : (index + 1) * part] = join(*sides).astype(BF16)

            def turn_cots():
                kept["cots"] = cots[rows].T

            def turn_normed():
                kept["normed"] = normed_two[rows].T

            def add_to(ref, cut, value):
                if step == 0:
                    ref[:, cut] = value
                else:
                    ref[:, cut] += value

            def weigh(part):
                cut = slice(part * D, (part + 1) * D)
                add_to(r["acc_back"], cut, nn(kept["cots"], activated[rows, cut]))

            def weigh_in(part):
                cut = slice(part * D, (part + 1) * D)
                add_to(r["acc_in"], cut, nn(kept["normed"], grad_inner[rows, cut]))

            def weigh_out():
                add_to(r["acc_out"], slice(0, D), tn(attended[rows], branch[rows]))

            parts = range(FF // D)
            weights = [turn_cots] + [lambda p=p: weigh(p) for p in parts]
            weights += [turn_normed] + [lambda p=p: weigh_in(p) for p in parts]
            return weights, [lambda p=p: write(p) for p in parts] + [weigh_out]

        def send_packed(step):
            rows = step_rows(step)
            outs.append(copies.start(packed.at[rows], packed_out.at[rows]))

        def send_step(step):
            rows = step_rows(step)
            outs.append(copies.start(branch.at[rows], branch_out.at[rows]))
            outs.append(
                copies.start(
                    r["out_blocks"].at[step], out.at[:, step * BLOCK : (step + 1) * BLOCK]
                )
            )

        stages = [attention(tile) for tile in range(tiles)]
        weights, closing = zip(*[release(step) for step in range(steps)])
        arrive()
        for one in read_tokens(0):
            one()
        arrive()
        interleave(stages[0][0], read_tokens(1))
        interleave(stages[1][0], stages[0][1])
        arrive()
        interleave(stages[2][0], stages[1][1], stages[0][2], read_cots(0))
        for one in expand(0, 0):
            one()
        for tile in range(tiles):
            if tile == 1:
                arrive()
                send_packed(0)
            if tile == 3:
                send_packed(1)
            if tile > 4 and tile % 2:
                send_step((tile - 5) // 2)
            lists = [hidden(tile)]
            if tile + 3 < tiles:
                lists.append(stages[tile + 3][0])
            if tile + 2 < tiles:
                lists.append(stages[tile + 2][1])
            if tile + 1 < tiles:
                lists.append(stages[tile + 1][2] + list(expand(tile + 1, 0)))
            if tile % 2 == 0 and tile // 2 + 2 < steps:
                lists.append(read_tokens(tile // 2 + 2))
            if tile % 2 and (tile + 1) // 2 < steps:
                lists.append(read_cots((tile + 1) // 2))
            if tile:
                lists.append(finish(tile - 1))
            if tile > 1 and tile % 2 == 0:
                lists.append(weights[tile // 2 - 1])
            if tile > 1 and tile % 2:
                lists.append(closing[(tile - 3) // 2])
            interleave(*lists)
        last = steps - 1
        send_packed(last)
        send_step(last - 1)
        interleave(finish(tiles - 1), weights[last])
        for one in closing[last]:
            one()
        send_step(last)
        flatten(flat, base, r["acc_back"][...].T, ROW_BACK, 2)
        flatten(flat, base, r["acc_in"][...], ROW_IN, 8)
        flatten(flat, base, r["acc_out"][...], ROW_OUT, 2)
        flatten_vector(flat, ROW_GAIN_TWO - base, column_sum(sums.gain))
        flatten_vector(flat, ROW_SHIFT_TWO - base, column_sum(sums.shift))
        flatten_vector(flat, ROW_BIAS_BACK - base, column_sum(sums.cot))
        for part in range(FF // D):
            flatten_vector(
                flat, ROW_BIAS_IN - base + 2 * part, column_sum(getattr(sums, f"bias{part}"))
            )
        first[...] = flat[ROW_OUT - base : ROW_OUT - base + 8]
        send_rows(
            plan, place_ref, flat, base, r["parts_in"], plan.lead, plan.deep
        )
        outs.append(copies.start(r["parts_in"].at[1], send))
        outs.append(copies.start(r["parts_in"].at[0], keep))
        for copy in outs:
            copy.wait()

    vmem = pl.BlockSpec(memory_space=pltpu.VMEM)
    hbm = pl.BlockSpec(memory_space=pl.ANY)
    shape = jax.ShapeDtypeStruct
    parts = (PLANE, deep, plan.rows, LANES)
    moved = pltpu.VMEM((steps, group, local_rows, BLOCK, D), BF16)
    wide = lambda width, kind: pltpu.VMEM((count, width), kind)
    pair = lambda rows, kind: pltpu.VMEM((2, rows, TILE), kind)
    scratch = dict(
        x_in=moved,
        cot_in=moved,
        wq=pltpu.VMEM((D, 3 * D), BF16),
        wo=pltpu.VMEM((D, D), BF16),
        wi=pltpu.VMEM((D, FF), BF16),
        wb=pltpu.VMEM((FF, D), BF16),
        normed=wide(D, BF16),
        packed=wide(3 * D, BF16),
        scores=pair(HEADS * TILE, F32),
        probs=pair(HEADS * TILE, BF16),
        cap=pltpu.VMEM((TILE, TILE), F32),
        attended=wide(D, BF16),
        middle=wide(D, F32),
        hats=wide(D, F32),
        inverses=wide(LANES, F32),
        normed_two=wide(D, BF16),
        cots=wide(D, BF16),
        inner=pltpu.VMEM((FF // D, TILE, D), F32),
        grad_act=pltpu.VMEM((FF // D, TILE, D), F32),
        activated=wide(FF, BF16),
        grad_inner=wide(FF, BF16),
        grad_normed=wide(D, F32),
        branch=wide(D, BF16),
        out_blocks=pltpu.VMEM((steps, TALL, BLOCK, D), BF16),
        acc_in=pltpu.VMEM((D, FF), F32),
        acc_back=pltpu.VMEM((D, FF), F32),
        acc_out=pltpu.VMEM((D, D), F32),
        flat=pltpu.VMEM((ROWS - base + plan.rows, LANES), F32),
        parts_in=pltpu.VMEM((CORES,) + parts, BF16),
        sems=pltpu.SemaphoreType.DMA((6 + 5 * steps,)),
    )
    return pl.pallas_call(
        kernel,
        in_specs=[pl.BlockSpec(memory_space=pltpu.SMEM)] + [hbm] * 5 + [vmem] * 2,
        out_specs=[hbm, vmem, hbm, hbm, hbm, hbm, vmem],
        out_shape=[
            shape((count, 3 * D), BF16),
            shape((-(-tiles * HEADS // 8) * 8, TILE), F32),
            shape((TALL, steps * BLOCK, D), BF16),
            shape((count, D), BF16),
            shape(parts, BF16),
            shape(parts, BF16),
            shape((8, LANES), F32),
        ],
        scratch_shapes=[scratch[name] for name in names],
        compiler_params=pltpu.CompilerParams(vmem_limit_bytes=VMEM_BYTES),
        cost_estimate=pl.CostEstimate(
            flops=15 * 10**9, bytes_accessed=10**7, transcendentals=2 * 10**6
        ),
        name="layer",
    )


def back(plan, steps, local_rows):
    group, tiles, count = plan.group, 2 * steps, steps * TOKENS
    names = (
        "x_in", "packed_in", "branch_in", "wq", "wo", "hats", "inverses", "normed", "grad_att",
        "scores", "grad_probs", "probs", "grad_scores", "grad_packed", "grad_normed", "x_blocks",
        "cap", "acc", "flat", "parts_in", "sems",
    )

    def kernel(place_ref, both, packed, branch, w_qkv, w_out, vectors, logsum, first, *refs):
        grad_x, keep, send = refs[:3]
        r = dict(zip(names, refs[3:]))
        x_in, packed_in, branch_in = r["x_in"], r["packed_in"], r["branch_in"]
        hats, inverses, normed, cap = r["hats"], r["inverses"], r["normed"], r["cap"]
        grad_att, scores, grad_probs = r["grad_att"], r["scores"], r["grad_probs"]
        probs, grad_scores = r["probs"], r["grad_scores"]
        grad_packed, grad_normed, flat = r["grad_packed"], r["grad_normed"], r["flat"]
        copies = Copies(r["sems"])
        arriving = []
        for step in range(steps):
            rows = step_rows(step)
            arriving.append([copies.start(branch.at[rows], branch_in.at[rows])])
            if step == 0:
                arriving[0].append(copies.start(w_out, r["wo"]))
            arriving[step].append(copies.start(packed.at[rows], packed_in.at[rows]))
            arriving[step].append(copies.start(both.at[:, step, 0], x_in.at[step]))
            if step == 0:
                arriving[0].append(copies.start(w_qkv, r["wq"]))

        def arrive():
            for copy in arriving.pop(0):
                copy.wait()

        outs = []
        cap[...] = jnp.where(allowed(vectors[SPAN : SPAN + 1, 0:1]), jnp.inf, -1e30)
        clear_later(probs, grad_scores)
        sums = Sums(gain=D, shift=D)
        scale = HEAD**-0.5

        def start(tile):
            rows, slot = tile_rows(tile), tile % 2

            def project():
                grad_att[rows] = nt(branch_in[rows], r["wo"][...]).astype(BF16)

            def score():
                scores[slot] = nt(two_heads(packed_in[rows, D : 2 * D]), packed_in[rows, :D])

            def spread():
                grad_probs[slot] = nt(two_heads(packed_in[rows, 2 * D :]), grad_att[rows])

            return [project, score, spread]

        def soften(tile):
            slot = tile % 2

            def one(keys, part, head):
                value = jnp.minimum(scores[slot, keys, part] * SCORE_RATE, caps(cap, keys, part))
                row = tile * HEADS + head
                prob = jnp.exp2(value - logsum[row : row + 1, part])
                weighted = prob * grad_probs[slot, keys, part]
                total = jnp.sum(weighted, axis=0, keepdims=True)
                probs[slot, keys, part] = prob.astype(BF16)
                grad_scores[slot, keys, part] = (weighted - prob * total).astype(BF16)

            return [lambda q=q: one(*q) for q in quarters()]

        def gather(tile):
            rows, slot = tile_rows(tile), tile % 2

            def queries():
                wide = two_heads(packed_in[rows, D : 2 * D])
                grad_packed[rows, :D] = (tn(grad_scores[slot], wide) * scale).astype(BF16)

            def keys():
                value = own_heads(nn(grad_scores[slot], packed_in[rows, :D]))
                grad_packed[rows, D : 2 * D] = (value * scale).astype(BF16)

            def values():
                value = own_heads(nn(probs[slot], grad_att[rows]))
                grad_packed[rows, 2 * D :] = value.astype(BF16)

            return [queries, keys, values]

        def read_tokens(step):
            def one(index):
                members = slice(index * SUB, (index + 1) * SUB)
                hat, inverse = center(x_in[step, members].astype(F32))
                inverse = jnp.broadcast_to(inverse, hat.shape[:-1] + (LANES,))
                for side, (h_rows, i_rows) in enumerate(zip(split(hat), split(inverse))):
                    size = h_rows.shape[0]
                    begin = (2 * step + side) * TILE + index * size
                    hats[begin : begin + size] = h_rows
                    inverses[begin : begin + size] = i_rows
                    normed[begin : begin + size] = (
                        h_rows * vectors[0:1] + vectors[1:2]
                    ).astype(BF16)

            return [lambda i=i: one(i) for i in range(group // SUB)]

        def finish(tile):
            rows = tile_rows(tile)

            def spread():
                grad_normed[rows] = nt(grad_packed[rows], r["wq"][...])

            def norm_back(piece):
                hat, grad = hats[piece], grad_normed[piece]
                inverse = jnp.concatenate([inverses[piece]] * 2, axis=1)
                sums.gain = sums.gain + fold(grad * hat)
                sums.shift = sums.shift + fold(grad)
                grad = branch_in[piece].astype(F32) + center_back(
                    grad * vectors[0:1], hat, inverse
                )
                grad_normed[piece] = grad

            return [spread] + [lambda p=p: norm_back(p) for p in pieces_of(tile, PIECE)]

        def release(step):
            rows = step_rows(step)
            kept = {}

            def write(index):
                part = TALL // 4
                sides = []
                for side in range(2):
                    begin = (2 * step + side) * TILE + index * part * HALF
                    sides.append(grad_normed[begin : begin + part * HALF])
                block = r["x_blocks"].at[step]
                block[index * part : (index + 1) * part] = join(*sides).astype(BF16)

            def turn():
                kept["normed"] = normed[rows].T

            def weigh(part):
                cut = slice(part * D, (part + 1) * D)
                value = nn(kept["normed"], grad_packed[rows, cut])
                if step == 0:
                    r["acc"][:, cut] = value
                else:
                    r["acc"][:, cut] += value

            return (
                [lambda i=i: write(i) for i in range(4)]
                + [turn]
                + [lambda p=p: weigh(p) for p in range(3)]
            )

        def send_step(step):
            outs.append(
                copies.start(
                    r["x_blocks"].at[step], grad_x.at[:, step * BLOCK : (step + 1) * BLOCK]
                )
            )

        released = [release(step) for step in range(steps)]
        arrive()
        for one in start(0):
            one()
        interleave(soften(0), start(1), read_tokens(0))
        for tile in range(tiles):
            if tile % 2 == 0 and tile + 2 < tiles:
                arrive()
            if tile > 4 and tile % 2:
                send_step((tile - 5) // 2)
            lists = [gather(tile)]
            if tile + 1 < tiles:
                lists.append(soften(tile + 1))
            if tile + 2 < tiles:
                lists.append(start(tile + 2))
            if tile % 2 and (tile + 1) // 2 < steps:
                lists.append(read_tokens((tile + 1) // 2))
            if tile:
                lists.append(finish(tile - 1))
            if tile > 1 and tile % 2:
                lists.append(released[(tile - 3) // 2])
            interleave(*lists)
        send_step(steps - 2)
        interleave(finish(tiles - 1), released[steps - 1][4:])
        for one in released[steps - 1][:4]:
            one()
        send_step(steps - 1)
        flatten(flat, 0, r["acc"][...], ROW_QKV, 6)
        flatten_vector(flat, ROW_GAIN_ONE, column_sum(sums.gain))
        flatten_vector(flat, ROW_SHIFT_ONE, column_sum(sums.shift))
        flat[ROW_OUT : ROW_OUT + 8] = first[...]
        send_rows(plan, place_ref, flat, 0, r["parts_in"], 0, plan.lead)
        outs.append(copies.start(r["parts_in"].at[1], send))
        outs.append(copies.start(r["parts_in"].at[0], keep))
        for copy in outs:
            copy.wait()

    vmem = pl.BlockSpec(memory_space=pltpu.VMEM)
    hbm = pl.BlockSpec(memory_space=pl.ANY)
    shape = jax.ShapeDtypeStruct
    parts = (PLANE, plan.lead, plan.rows, LANES)
    wide = lambda width, kind: pltpu.VMEM((count, width), kind)
    pair = lambda kind: pltpu.VMEM((2, HEADS * TILE, TILE), kind)
    scratch = dict(
        x_in=pltpu.VMEM((steps, group, local_rows, BLOCK, D), BF16),
        packed_in=wide(3 * D, BF16),
        branch_in=wide(D, BF16),
        wq=pltpu.VMEM((D, 3 * D), BF16),
        wo=pltpu.VMEM((D, D), BF16),
        hats=wide(D, F32),
        inverses=wide(LANES, F32),
        normed=wide(D, BF16),
        grad_att=wide(D, BF16),
        scores=pair(F32),
        grad_probs=pair(F32),
        probs=pair(BF16),
        grad_scores=pair(BF16),
        grad_packed=wide(3 * D, BF16),
        grad_normed=wide(D, F32),
        x_blocks=pltpu.VMEM((steps, TALL, BLOCK, D), BF16),
        cap=pltpu.VMEM((TILE, TILE), F32),
        acc=pltpu.VMEM((D, 3 * D), F32),
        flat=pltpu.VMEM((ROW_OUT + plan.rows + 8, LANES), F32),
        parts_in=pltpu.VMEM((CORES,) + parts, BF16),
        sems=pltpu.SemaphoreType.DMA((4 + 4 * steps,)),
    )
    return pl.pallas_call(
        kernel,
        in_specs=[pl.BlockSpec(memory_space=pltpu.SMEM)] + [hbm] * 5 + [vmem] * 3,
        out_specs=[hbm] * 3,
        out_shape=[
            shape((TALL, steps * BLOCK, D), BF16),
            shape(parts, BF16),
            shape(parts, BF16),
        ],
        scratch_shapes=[scratch[name] for name in names],
        compiler_params=pltpu.CompilerParams(vmem_limit_bytes=VMEM_BYTES),
        cost_estimate=pl.CostEstimate(
            flops=10 * 10**9, bytes_accessed=8 * 10**6, transcendentals=10**6
        ),
        name="back",
    )


def cut_kernel(group, steps):
    def kernel(rows_ref, cot_ref, out_ref):
        for member in range(group):
            for step in range(steps):
                column = (member * steps + step) * BLOCK
                for kind, ref in enumerate((rows_ref, cot_ref)):
                    out_ref[member, step, kind] = ref[:, column : column + BLOCK]

    return kernel


def local(mesh_shape, tokens, column_rows, cotangent, flat_params):
    seq = mesh_shape["seq"]
    local_rows, columns = tokens.shape[1], tokens.shape[2]
    group = TALL // local_rows
    owned = columns // group
    steps = owned // BLOCK
    plan = Plan(seq, group, flat_params.shape[0])
    seq_at = lax.axis_index("seq")
    core_at = lax.axis_index("dp")
    deep_at, plane_at = seq_at // PLANE, seq_at % PLANE
    holder = seq_at % group * owned // STRIDE * (seq * STRIDE // columns)
    place = jnp.stack([deep_at, plane_at, core_at, holder]).astype(jnp.int32)
    shift = plan.shard * (seq_at * CORES + core_at) % LANES
    groups = [[group * g + i for i in range(group)] for g in range(seq // group)]
    deep_groups = [[PLANE * z + q for z in range(plan.deep)] for q in range(PLANE)]

    def exchange(blocks):
        return lax.all_to_all(blocks, "seq", 0, 0, axis_index_groups=groups, tiled=True)

    def to_rows(cols):
        moved = exchange(cols.reshape(group, local_rows, owned, D))
        return moved.transpose(1, 0, 2, 3).reshape(tokens.shape)

    def swap_seq(value, distance):
        return lax.ppermute(value, "seq", [(i, i ^ distance) for i in range(seq)])

    def swap_core(value):
        return lax.ppermute(value, "dp", [(0, 1), (1, 0)])

    blank = jnp.zeros((plan.rows - 1) * LANES, BF16)
    blank = jnp.concatenate([blank, jnp.broadcast_to(column_rows[0, 0].astype(BF16), (LANES,))])
    own = lax.dynamic_update_slice(blank, flat_params, (shift,)).reshape(plan.rows, LANES)
    if plan.pairwise:
        arrived = [swap_seq(own, PLANE * k) for k in range(1, plan.deep)]
        deep = jnp.stack([own] + arrived)
    else:
        arrived = [own]
        deep = lax.all_gather(own, "seq", axis=0, axis_index_groups=deep_groups)
    vmem = pl.BlockSpec(memory_space=pltpu.VMEM)
    both = pl.pallas_call(
        cut_kernel(group, steps),
        out_shape=jax.ShapeDtypeStruct((group, steps, 2, local_rows, BLOCK, D), BF16),
        in_specs=[vmem, vmem],
        out_specs=vmem,
        compiler_params=pltpu.CompilerParams(vmem_limit_bytes=VMEM_BYTES),
        name="cut",
    )(tokens.reshape(local_rows, columns, D), cotangent.reshape(local_rows, columns, D))
    deep, both = lax.optimization_barrier((deep, both))
    both = exchange(both)
    plane = [deep] + [swap_seq(deep, k) for k in range(1, PLANE)]
    pieces = plane + [swap_core(piece) for piece in plane]
    w_qkv, w_out, w_in, w_back, vectors, bias_in = prepare(plan)(place, *pieces)

    packed, logsum, out, branch, keep, send, first = layer(plan, steps, local_rows)(
        place, both, w_qkv, w_out, w_in, w_back, vectors, bias_in
    )

    layer_out = to_rows(out)

    def core_sum(keep, send):
        return keep.astype(F32) + swap_core(send).astype(F32)

    def plane_sum(value):
        total = value[0]
        sent = value.astype(BF16)
        for k in range(1, PLANE):
            total = total + swap_seq(sent[k], k).astype(F32)
        return total

    later = plane_sum(core_sum(keep, send))

    grad_x, lead_keep, lead_send = back(plan, steps, local_rows)(
        place, both, packed, branch, w_qkv, w_out, vectors, logsum, first
    )
    (lead_keep, lead_send), layer_out, later = lax.optimization_barrier(
        ((lead_keep, lead_send), layer_out, later)
    )
    total = jnp.concatenate([plane_sum(core_sum(lead_keep, lead_send)), later], axis=0)
    moved_x = exchange(grad_x.reshape(group, local_rows, owned, D))
    total, moved_x = lax.optimization_barrier((total, moved_x))
    input_grad = moved_x.transpose(1, 0, 2, 3).reshape(tokens.shape).astype(F32)
    if plan.pairwise:
        sent = total.astype(BF16)
        result = lax.dynamic_index_in_dim(total, deep_at, 0, keepdims=False)
        for k in range(1, plan.deep):
            piece = lax.dynamic_index_in_dim(sent, deep_at ^ k, 0, keepdims=False)
            result = result + swap_seq(piece, PLANE * k).astype(F32)
    else:
        moved = lax.all_to_all(
            total.astype(BF16), "seq", 0, 0, axis_index_groups=deep_groups, tiled=True
        )
        result = jnp.sum(moved.astype(F32), axis=0)
    param_grad = lax.dynamic_slice(result.reshape(-1), (shift,), (plan.shard,))
    return layer_out, input_grad, param_grad


def solution(mesh):
    shape = dict(mesh.shape)
    rows = P("dp", "seq", None, None)
    flat = P(("seq", "dp"))
    return jax.shard_map(
        lambda *args: local(shape, *args),
        mesh=mesh,
        in_specs=(rows, P("dp", "seq"), rows, flat),
        out_specs=(rows, rows, flat),
        check_vma=False,
    )
```

```python
import jax
import jax.numpy as jnp
from jax import lax
from jax.experimental import pallas as pl
from jax.experimental.pallas import tpu as pltpu
from jax.sharding import PartitionSpec as P

D = 256
FF = 1024
HEADS = 2
HEAD = D // HEADS
TALL = 32
STRIDE = 96
EPSILON = 1e-05
LANES = 128
PLANE = 4
CORES = 2
BLOCK = 16
HALF = 8
TOKENS = TALL * BLOCK
TILE = TALL * HALF
VMEM_BYTES = 63 * 1024 * 1024

ROW_GAIN_ONE = 0
ROW_SHIFT_ONE = 2
ROW_QKV = 4
ROW_OUT = ROW_QKV + 6 * D
ROW_GAIN_TWO = ROW_OUT + 2 * D
ROW_SHIFT_TWO = ROW_GAIN_TWO + 2
ROW_IN = ROW_SHIFT_TWO + 2
ROW_BIAS_IN = ROW_IN + 8 * D
ROW_BACK = ROW_BIAS_IN + 8
ROW_BIAS_BACK = ROW_BACK + 2 * FF
ROWS = ROW_BIAS_BACK + 2

SPAN = 5

F32 = jnp.float32
BF16 = jnp.bfloat16


def nn(left, right):
    return lax.dot_general(left, right, (((1,), (0,)), ((), ())), preferred_element_type=F32)


def nt(left, right):
    return lax.dot_general(left, right, (((1,), (1,)), ((), ())), preferred_element_type=F32)


def tn(left, right):
    return lax.dot_general(left, right, (((0,), (0,)), ((), ())), preferred_element_type=F32)


def center(value):
    offset = value - jnp.mean(value, axis=-1, keepdims=True)
    inverse = lax.rsqrt(jnp.mean(offset * offset, axis=-1, keepdims=True) + EPSILON)
    return offset * inverse, inverse


def center_back(grad_hat, hat, inverse):
    mean_one = jnp.mean(grad_hat, axis=-1, keepdims=True)
    mean_two = jnp.mean(grad_hat * hat, axis=-1, keepdims=True)
    return inverse * (grad_hat - mean_one - hat * mean_two)


def allowed(span):
    key = lax.broadcasted_iota(jnp.int32, (TILE, TILE), 0)
    query = lax.broadcasted_iota(jnp.int32, (TILE, TILE), 1)
    same_column = (key % HALF) == (query % HALF)
    half_tile = TILE // 2
    same_image = (key // half_tile == query // half_tile) | (span >= TALL)
    return same_column & (key <= query) & same_image


class Plan:
    def __init__(self, seq, group, shard):
        self.shard = shard
        self.group = group
        self.deep = seq // PLANE
        self.count = seq * CORES
        self.pairwise = self.deep == 4
        rows = (shard + LANES - 2) // LANES + 2
        self.rows = -(-rows // 16) * 16
        self.lead = -(-(ROW_OUT * LANES) // (PLANE * CORES * shard))

    def first_row(self, device):
        return self.shard * device // LANES


def prepare(plan):
    def kernel(place_ref, *refs):
        sources, rest = refs[: CORES * PLANE], refs[CORES * PLANE :]
        w_qkv, w_out, w_in, w_back, vectors, bias_in, held, flat, sems = rest
        deep_at, plane_at, core_at = place_ref[0], place_ref[1], place_ref[2]
        copies = []
        for core in range(CORES):
            for plane in range(PLANE):
                source = sources[core * PLANE + plane]
                for deep in range(plan.deep):
                    slot = deep ^ deep_at if plan.pairwise else deep
                    copies.append(
                        pltpu.make_async_copy(
                            source.at[deep],
                            held.at[slot, plane ^ plane_at, core ^ core_at],
                            sems.at[len(copies)],
                        )
                    )
        for copy in copies:
            copy.start()
        for copy in copies:
            copy.wait()
        for device in range(plan.count):
            row = plan.first_row(device)
            value = held[device // 8, device // 2 % PLANE, device % CORES].astype(F32)
            if plan.shard * device % LANES:
                before = flat[row : row + 1]
                flat[row : row + plan.rows] = value
                flat[row : row + 1] = flat[row : row + 1] + before
            else:
                flat[row : row + plan.rows] = value
        for ref, row, wide in (
            (w_qkv, ROW_QKV, 6),
            (w_out, ROW_OUT, 2),
            (w_in, ROW_IN, 8),
            (w_back, ROW_BACK, 2),
        ):
            for part in range(wide):
                ref[:, part * LANES : (part + 1) * LANES] = flat[
                    pl.ds(row + part, ref.shape[0], stride=wide)
                ].astype(BF16)
        for index, row in enumerate(
            (ROW_GAIN_ONE, ROW_SHIFT_ONE, ROW_GAIN_TWO, ROW_SHIFT_TWO, ROW_BIAS_BACK)
        ):
            for part in range(2):
                vectors[index : index + 1, part * LANES : (part + 1) * LANES] = flat[
                    row + part : row + part + 1
                ]
        holder = place_ref[3]
        vectors[SPAN : SPAN + 1, :LANES] = held[holder // PLANE, holder % PLANE, core_at][
            plan.rows - 1 :
        ].astype(F32)
        for part in range(8):
            bias_in[0:1, part * LANES : (part + 1) * LANES] = flat[
                ROW_BIAS_IN + part : ROW_BIAS_IN + part + 1
            ]

    shapes = [((D, 3 * D), BF16), ((D, D), BF16), ((D, FF), BF16), ((FF, D), BF16)]
    shapes += [((8, D), F32), ((8, FF), F32)]
    return pl.pallas_call(
        kernel,
        out_shape=[jax.ShapeDtypeStruct(shape, kind) for shape, kind in shapes],
        in_specs=[pl.BlockSpec(memory_space=pltpu.SMEM)]
        + [pl.BlockSpec(memory_space=pl.ANY)] * (CORES * PLANE),
        out_specs=[pl.BlockSpec(memory_space=pltpu.VMEM)] * len(shapes),
        scratch_shapes=[
            pltpu.VMEM((plan.deep, PLANE, CORES, plan.rows, LANES), BF16),
            pltpu.VMEM((ROWS + plan.rows + 8, LANES), F32),
            pltpu.SemaphoreType.DMA((plan.count,)),
        ],
        compiler_params=pltpu.CompilerParams(vmem_limit_bytes=VMEM_BYTES),
        cost_estimate=pl.CostEstimate(flops=25500000000, bytes_accessed=4 * 10**6, transcendentals=0),
        name="prepare",
    )


SUB = 2
LOG2E = 1.4426950408889634
SCORE_RATE = HEAD**-0.5 * LOG2E
PIECE = 128
SLAB = 16
GELU_RATE = (2.0 / jnp.pi) ** 0.5
GELU_CUBE = GELU_RATE * 0.044715


def interleave(*lists):
    keyed = []
    for order, steps in enumerate(lists):
        for index, step in enumerate(steps):
            keyed.append(((index + 0.5) / len(steps), order, index, step))
    for _, _, _, step in sorted(keyed, key=lambda entry: entry[:3]):
        step()


def fold(value):
    return jnp.sum(value.reshape(-1, 8, value.shape[-1]), axis=0)


def column_sum(value):
    return jnp.sum(value, axis=0, keepdims=True)


class Copies:
    def __init__(self, sems):
        self.sems = sems
        self.used = 0

    def start(self, source, target):
        copy = pltpu.make_async_copy(source, target, self.sems.at[self.used])
        self.used += 1
        copy.start()
        return copy


def tile_rows(tile):
    return slice(tile * TILE, (tile + 1) * TILE)


def step_rows(step):
    return slice(step * TOKENS, (step + 1) * TOKENS)


def pieces_of(tile, size):
    return [
        slice(start, start + size) for start in range(tile * TILE, (tile + 1) * TILE, size)
    ]


def split(block):
    width = block.shape[-1]
    return [
        block[:, :, side * HALF : (side + 1) * HALF].reshape(-1, width) for side in range(2)
    ]


def join(left, right):
    width = left.shape[-1]
    return jnp.concatenate(
        [left.reshape(-1, HALF, width), right.reshape(-1, HALF, width)], axis=1
    )


def two_heads(value):
    blank = jnp.zeros((value.shape[0], HEAD), value.dtype)
    return jnp.concatenate(
        [
            jnp.concatenate([value[:, :HEAD], blank], axis=1),
            jnp.concatenate([blank, value[:, HEAD:]], axis=1),
        ],
        axis=0,
    )


def own_heads(value):
    rows = value.shape[0] // 2
    return jnp.concatenate([value[:rows, :HEAD], value[rows:, HEAD:]], axis=1)


def quarters():
    for head in range(HEADS):
        for part in range(TILE // LANES):
            yield (
                slice(head * TILE, head * TILE + (part + 1) * LANES),
                slice(part * LANES, (part + 1) * LANES),
                head,
            )


def caps(cap, keys, part):
    return cap[: keys.stop - keys.start, part]


def clear_later(*refs):
    for ref in refs:
        for head in range(HEADS):
            for part in range(TILE // LANES - 1):
                keys = slice(head * TILE + (part + 1) * LANES, (head + 1) * TILE)
                cut = slice(part * LANES, (part + 1) * LANES)
                ref[:, keys, cut] = jnp.zeros_like(ref[:, keys, cut])


def flatten(flat, base, matrix, row, wide):
    for part in range(wide):
        flat[pl.ds(row - base + part, matrix.shape[0], stride=wide)] = matrix[
            :, part * LANES : (part + 1) * LANES
        ]


def flatten_vector(flat, row, vector):
    for part in range(vector.shape[-1] // LANES):
        flat[row + part : row + part + 1] = vector[:, part * LANES : (part + 1) * LANES]


def send_rows(plan, place_ref, flat, base, parts, low, high):
    plane_at, core_at = place_ref[1], place_ref[2]
    for device in range(low * PLANE * CORES, high * PLANE * CORES):
        row = plan.first_row(device) - base
        parts[
            (device % CORES) ^ core_at,
            (device // CORES % PLANE) ^ plane_at,
            device // (PLANE * CORES) - low,
        ] = flat[row : row + plan.rows].astype(BF16)


class Sums:
    def __init__(self, **widths):
        for name, width in widths.items():
            setattr(self, name, jnp.zeros((8, width), F32))


def layer(plan, steps, local_rows):
    group, tiles, count = plan.group, 2 * steps, steps * TOKENS
    base = ROW_OUT - 4
    deep = plan.deep - plan.lead
    names = (
        "x_in", "cot_in", "wq", "wo", "wi", "wb", "normed", "packed", "scores", "probs", "cap",
        "attended", "middle", "hats", "inverses", "normed_two", "cots", "inner", "grad_act",
        "activated", "grad_inner", "grad_normed", "branch", "out_blocks", "acc_in", "acc_back",
        "acc_out", "flat", "parts_in", "sems",
    )

    def kernel(place_ref, both, w_qkv, w_out, w_in, w_back, vectors, bias_in, *refs):
        packed_out, logsum, out, branch_out, keep, send, first = refs[:7]
        r = dict(zip(names, refs[7:]))
        x_in, cot_in, packed, middle, hats = (
            r[n] for n in ("x_in", "cot_in", "packed", "middle", "hats")
        )
        scores, probs, cap, attended = (r[n] for n in ("scores", "probs", "cap", "attended"))
        normed, normed_two, cots = r["normed"], r["normed_two"], r["cots"]
        inner, grad_act, activated, grad_inner = (
            r[n] for n in ("inner", "grad_act", "activated", "grad_inner")
        )
        inverses, grad_normed, branch, flat = (
            r[n] for n in ("inverses", "grad_normed", "branch", "flat")
        )
        copies = Copies(r["sems"])
        waits = {}
        arriving = [[copies.start(both.at[:, 0, 0], x_in.at[0])]]
        arriving[0].append(copies.start(w_qkv, r["wq"]))
        arriving.append([copies.start(both.at[:, 1, 0], x_in.at[1])])
        arriving[1].append(copies.start(w_out, r["wo"]))
        arriving.append([copies.start(both.at[:, 0, 1], cot_in.at[0])])
        arriving[2] += [copies.start(w_in, r["wi"]), copies.start(w_back, r["wb"])]
        arriving[2] += [
            copies.start(both.at[:, step, 0], x_in.at[step]) for step in range(2, steps)
        ]
        arriving.append(
            [copies.start(both.at[:, step, 1], cot_in.at[step]) for step in range(1, steps)]
        )
        outs = []

        def arrive():
            for copy in arriving.pop(0):
                copy.wait()

        cap[...] = jnp.where(allowed(vectors[SPAN : SPAN + 1, 0:1]), jnp.inf, -1e30)
        clear_later(probs)
        sums = Sums(gain=D, shift=D, cot=D, **{f"bias{p}": D for p in range(FF // D)})

        def read_tokens(step):
            def one(index):
                members = slice(index * SUB, (index + 1) * SUB)
                value = x_in[step, members].astype(F32)
                hat, _ = center(value)
                hat = hat * vectors[0:1] + vectors[1:2]
                for side, (x_rows, n_rows) in enumerate(zip(split(value), split(hat))):
                    size = x_rows.shape[0]
                    start = (2 * step + side) * TILE + index * size
                    middle[start : start + size] = x_rows
                    normed[start : start + size] = n_rows.astype(BF16)

            return [lambda i=i: one(i) for i in range(group // SUB)]

        def read_cots(step):
            def one(index):
                members = slice(index * SUB, (index + 1) * SUB)
                for side, rows in enumerate(split(cot_in[step, members].astype(F32))):
                    size = rows.shape[0]
                    start = (2 * step + side) * TILE + index * size
                    cots[start : start + size] = rows.astype(BF16)
                    sums.cot = sums.cot + fold(rows)

            return [lambda i=i: one(i) for i in range(group // SUB)]

        def attention(tile):
            rows = tile_rows(tile)
            slot = tile % 2

            def project(part):
                cut = slice(part * D, (part + 1) * D)
                packed[rows, cut] = nn(normed[rows], r["wq"][:, cut]).astype(BF16)

            def score():
                scores[slot] = nt(two_heads(packed[rows, D : 2 * D]), packed[rows, :D])

            def soften(keys, part, head):
                value = jnp.minimum(scores[slot, keys, part] * SCORE_RATE, caps(cap, keys, part))
                peak = jnp.max(value, axis=0, keepdims=True)
                terms = jnp.exp2(value - peak)
                total = jnp.sum(terms, axis=0, keepdims=True)
                probs[slot, keys, part] = (terms * (1.0 / total)).astype(BF16)
                row = tile * HEADS + head
                logsum[row : row + 1, part] = peak + jnp.log2(total)

            def mix():
                attended[rows] = tn(probs[slot], two_heads(packed[rows, 2 * D :])).astype(BF16)

            def add():
                middle[rows] = middle[rows] + nn(attended[rows], r["wo"][...])

            def norm(piece):
                hat, inverse = center(middle[piece])
                hats[piece] = hat
                inverses[piece] = jnp.broadcast_to(inverse, (PIECE, LANES))
                normed_two[piece] = (hat * vectors[2:3] + vectors[3:4]).astype(BF16)

            return (
                [lambda p=p: project(p) for p in range(3)],
                [score] + [lambda q=q: soften(*q) for q in quarters()],
                [mix, add] + [lambda p=p: norm(p) for p in pieces_of(tile, PIECE)],
            )

        def expand(tile, part):
            rows, cut = tile_rows(tile), slice(part * D, (part + 1) * D)
            slot = part

            def up():
                inner[slot] = nn(normed_two[rows], r["wi"][:, cut])

            def down():
                grad_act[slot] = nt(cots[rows], r["wb"][cut, :])

            return up, down

        def activate(tile, part, index):
            cut = slice(part * D, (part + 1) * D)
            slot = part
            inside = slice(index * SLAB, (index + 1) * SLAB)
            rows = slice(tile * TILE + index * SLAB, tile * TILE + (index + 1) * SLAB)
            value = inner[slot, inside] + bias_in[0:1, cut]
            cube = value * (GELU_CUBE * (value * value))
            angle = GELU_RATE * value + cube
            bend = jnp.tanh(angle)
            gate = 0.5 * bend + 0.5
            activated[rows, cut] = (value * gate).astype(BF16)
            slope = gate * ((1.0 - bend) * (angle + (cube + cube)) + 1.0)
            grad = grad_act[slot, inside] * slope
            grad_inner[rows, cut] = grad.astype(BF16)
            name = f"bias{part}"
            setattr(sums, name, getattr(sums, name) + fold(grad))

        def hidden(tile):
            listed = []
            slabs = TILE // SLAB
            for part in range(FF // D):
                ahead = expand(tile, part + 1) if part + 1 < FF // D else ()
                for index in range(slabs):
                    if ahead and index % (slabs // 2) == 0:
                        listed.append(ahead[index // (slabs // 2)])
                    listed.append(lambda p=part, i=index: activate(tile, p, i))
            return listed

        def finish(tile):
            rows = tile_rows(tile)

            def second():
                middle[rows] = middle[rows] + nn(activated[rows], r["wb"][...])

            def back():
                grad_normed[rows] = nt(grad_inner[rows], r["wi"][...])

            def norm_back(piece):
                hat, grad = hats[piece], grad_normed[piece]
                inverse = jnp.concatenate([inverses[piece]] * 2, axis=1)
                sums.gain = sums.gain + fold(grad * hat)
                sums.shift = sums.shift + fold(grad)
                grad = cots[piece].astype(F32) + center_back(grad * vectors[2:3], hat, inverse)
                branch[piece] = grad.astype(BF16)

            return [second, back] + [lambda p=p: norm_back(p) for p in pieces_of(tile, PIECE)]

        def release(step):
            rows = step_rows(step)
            kept = {}

            def write(index):
                part = TALL // 4
                sides = []
                for side in range(2):
                    start = (2 * step + side) * TILE + index * part * HALF
                    sides.append(middle[start : start + part * HALF] + vectors[4:5])
                block = r["out_blocks"].at[step]
                block[index * part : (index + 1) * part] = join(*sides).astype(BF16)

            def turn_cots():
                kept["cots"] = cots[rows].T

            def turn_normed():
                kept["normed"] = normed_two[rows].T

            def add_to(ref, cut, value):
                if step == 0:
                    ref[:, cut] = value
                else:
                    ref[:, cut] += value

            def weigh(part):
                cut = slice(part * D, (part + 1) * D)
                add_to(r["acc_back"], cut, nn(kept["cots"], activated[rows, cut]))

            def weigh_in(part):
                cut = slice(part * D, (part + 1) * D)
                add_to(r["acc_in"], cut, nn(kept["normed"], grad_inner[rows, cut]))

            def weigh_out():
                add_to(r["acc_out"], slice(0, D), tn(attended[rows], branch[rows]))

            parts = range(FF // D)
            weights = [turn_cots] + [lambda p=p: weigh(p) for p in parts]
            weights += [turn_normed] + [lambda p=p: weigh_in(p) for p in parts]
            return weights, [lambda p=p: write(p) for p in parts] + [weigh_out]

        def send_packed(step):
            rows = step_rows(step)
            outs.append(copies.start(packed.at[rows], packed_out.at[rows]))

        def send_step(step):
            rows = step_rows(step)
            outs.append(copies.start(branch.at[rows], branch_out.at[rows]))
            outs.append(
                copies.start(
                    r["out_blocks"].at[step], out.at[:, step * BLOCK : (step + 1) * BLOCK]
                )
            )

        stages = [attention(tile) for tile in range(tiles)]
        weights, closing = zip(*[release(step) for step in range(steps)])
        arrive()
        for one in read_tokens(0):
            one()
        arrive()
        interleave(stages[0][0], read_tokens(1))
        interleave(stages[1][0], stages[0][1])
        arrive()
        interleave(stages[2][0], stages[1][1], stages[0][2], read_cots(0))
        for one in expand(0, 0):
            one()
        for tile in range(tiles):
            if tile == 1:
                arrive()
                send_packed(0)
            if tile == 3:
                send_packed(1)
            if tile > 4 and tile % 2:
                send_step((tile - 5) // 2)
            lists = [hidden(tile)]
            if tile + 3 < tiles:
                lists.append(stages[tile + 3][0])
            if tile + 2 < tiles:
                lists.append(stages[tile + 2][1])
            if tile + 1 < tiles:
                lists.append(stages[tile + 1][2] + list(expand(tile + 1, 0)))
            if tile % 2 == 0 and tile // 2 + 2 < steps:
                lists.append(read_tokens(tile // 2 + 2))
            if tile % 2 and (tile + 1) // 2 < steps:
                lists.append(read_cots((tile + 1) // 2))
            if tile:
                lists.append(finish(tile - 1))
            if tile > 1 and tile % 2 == 0:
                lists.append(weights[tile // 2 - 1])
            if tile > 1 and tile % 2:
                lists.append(closing[(tile - 3) // 2])
            interleave(*lists)
        last = steps - 1
        send_packed(last)
        send_step(last - 1)
        interleave(finish(tiles - 1), weights[last])
        for one in closing[last]:
            one()
        send_step(last)
        flatten(flat, base, r["acc_back"][...].T, ROW_BACK, 2)
        flatten(flat, base, r["acc_in"][...], ROW_IN, 8)
        flatten(flat, base, r["acc_out"][...], ROW_OUT, 2)
        flatten_vector(flat, ROW_GAIN_TWO - base, column_sum(sums.gain))
        flatten_vector(flat, ROW_SHIFT_TWO - base, column_sum(sums.shift))
        flatten_vector(flat, ROW_BIAS_BACK - base, column_sum(sums.cot))
        for part in range(FF // D):
            flatten_vector(
                flat, ROW_BIAS_IN - base + 2 * part, column_sum(getattr(sums, f"bias{part}"))
            )
        first[...] = flat[ROW_OUT - base : ROW_OUT - base + 8]
        send_rows(
            plan, place_ref, flat, base, r["parts_in"], plan.lead, plan.deep
        )
        outs.append(copies.start(r["parts_in"].at[1], send))
        outs.append(copies.start(r["parts_in"].at[0], keep))
        for copy in outs:
            copy.wait()

    vmem = pl.BlockSpec(memory_space=pltpu.VMEM)
    hbm = pl.BlockSpec(memory_space=pl.ANY)
    shape = jax.ShapeDtypeStruct
    parts = (PLANE, deep, plan.rows, LANES)
    moved = pltpu.VMEM((steps, group, local_rows, BLOCK, D), BF16)
    wide = lambda width, kind: pltpu.VMEM((count, width), kind)
    pair = lambda rows, kind: pltpu.VMEM((2, rows, TILE), kind)
    scratch = dict(
        x_in=moved,
        cot_in=moved,
        wq=pltpu.VMEM((D, 3 * D), BF16),
        wo=pltpu.VMEM((D, D), BF16),
        wi=pltpu.VMEM((D, FF), BF16),
        wb=pltpu.VMEM((FF, D), BF16),
        normed=wide(D, BF16),
        packed=wide(3 * D, BF16),
        scores=pair(HEADS * TILE, F32),
        probs=pair(HEADS * TILE, BF16),
        cap=pltpu.VMEM((TILE, TILE), F32),
        attended=wide(D, BF16),
        middle=wide(D, F32),
        hats=wide(D, F32),
        inverses=wide(LANES, F32),
        normed_two=wide(D, BF16),
        cots=wide(D, BF16),
        inner=pltpu.VMEM((FF // D, TILE, D), F32),
        grad_act=pltpu.VMEM((FF // D, TILE, D), F32),
        activated=wide(FF, BF16),
        grad_inner=wide(FF, BF16),
        grad_normed=wide(D, F32),
        branch=wide(D, BF16),
        out_blocks=pltpu.VMEM((steps, TALL, BLOCK, D), BF16),
        acc_in=pltpu.VMEM((D, FF), F32),
        acc_back=pltpu.VMEM((D, FF), F32),
        acc_out=pltpu.VMEM((D, D), F32),
        flat=pltpu.VMEM((ROWS - base + plan.rows, LANES), F32),
        parts_in=pltpu.VMEM((CORES,) + parts, BF16),
        sems=pltpu.SemaphoreType.DMA((6 + 5 * steps,)),
    )
    return pl.pallas_call(
        kernel,
        in_specs=[pl.BlockSpec(memory_space=pltpu.SMEM)] + [hbm] * 5 + [vmem] * 2,
        out_specs=[hbm, vmem, hbm, hbm, hbm, hbm, vmem],
        out_shape=[
            shape((count, 3 * D), BF16),
            shape((-(-tiles * HEADS // 8) * 8, TILE), F32),
            shape((TALL, steps * BLOCK, D), BF16),
            shape((count, D), BF16),
            shape(parts, BF16),
            shape(parts, BF16),
            shape((8, LANES), F32),
        ],
        scratch_shapes=[scratch[name] for name in names],
        compiler_params=pltpu.CompilerParams(vmem_limit_bytes=VMEM_BYTES),
        cost_estimate=pl.CostEstimate(
            flops=15 * 10**9, bytes_accessed=10**7, transcendentals=2 * 10**6
        ),
        name="layer",
    )


def back(plan, steps, local_rows):
    group, tiles, count = plan.group, 2 * steps, steps * TOKENS
    names = (
        "x_in", "packed_in", "branch_in", "wq", "wo", "hats", "inverses", "normed", "grad_att",
        "scores", "grad_probs", "probs", "grad_scores", "grad_packed", "grad_normed", "x_blocks",
        "cap", "acc", "flat", "parts_in", "sems",
    )

    def kernel(place_ref, both, packed, branch, w_qkv, w_out, vectors, logsum, first, *refs):
        grad_x, keep, send = refs[:3]
        r = dict(zip(names, refs[3:]))
        x_in, packed_in, branch_in = r["x_in"], r["packed_in"], r["branch_in"]
        hats, inverses, normed, cap = r["hats"], r["inverses"], r["normed"], r["cap"]
        grad_att, scores, grad_probs = r["grad_att"], r["scores"], r["grad_probs"]
        probs, grad_scores = r["probs"], r["grad_scores"]
        grad_packed, grad_normed, flat = r["grad_packed"], r["grad_normed"], r["flat"]
        copies = Copies(r["sems"])
        arriving = []
        for step in range(steps):
            rows = step_rows(step)
            arriving.append([copies.start(branch.at[rows], branch_in.at[rows])])
            if step == 0:
                arriving[0].append(copies.start(w_out, r["wo"]))
            arriving[step].append(copies.start(packed.at[rows], packed_in.at[rows]))
            arriving[step].append(copies.start(both.at[:, step, 0], x_in.at[step]))
            if step == 0:
                arriving[0].append(copies.start(w_qkv, r["wq"]))

        def arrive():
            for copy in arriving.pop(0):
                copy.wait()

        outs = []
        cap[...] = jnp.where(allowed(vectors[SPAN : SPAN + 1, 0:1]), jnp.inf, -1e30)
        clear_later(probs, grad_scores)
        sums = Sums(gain=D, shift=D)
        scale = HEAD**-0.5

        def start(tile):
            rows, slot = tile_rows(tile), tile % 2

            def project():
                grad_att[rows] = nt(branch_in[rows], r["wo"][...]).astype(BF16)

            def score():
                scores[slot] = nt(two_heads(packed_in[rows, D : 2 * D]), packed_in[rows, :D])

            def spread():
                grad_probs[slot] = nt(two_heads(packed_in[rows, 2 * D :]), grad_att[rows])

            return [project, score, spread]

        def soften(tile):
            slot = tile % 2

            def one(keys, part, head):
                value = jnp.minimum(scores[slot, keys, part] * SCORE_RATE, caps(cap, keys, part))
                row = tile * HEADS + head
                prob = jnp.exp2(value - logsum[row : row + 1, part])
                weighted = prob * grad_probs[slot, keys, part]
                total = jnp.sum(weighted, axis=0, keepdims=True)
                probs[slot, keys, part] = prob.astype(BF16)
                grad_scores[slot, keys, part] = (weighted - prob * total).astype(BF16)

            return [lambda q=q: one(*q) for q in quarters()]

        def gather(tile):
            rows, slot = tile_rows(tile), tile % 2

            def queries():
                wide = two_heads(packed_in[rows, D : 2 * D])
                grad_packed[rows, :D] = (tn(grad_scores[slot], wide) * scale).astype(BF16)

            def keys():
                value = own_heads(nn(grad_scores[slot], packed_in[rows, :D]))
                grad_packed[rows, D : 2 * D] = (value * scale).astype(BF16)

            def values():
                value = own_heads(nn(probs[slot], grad_att[rows]))
                grad_packed[rows, 2 * D :] = value.astype(BF16)

            return [queries, keys, values]

        def read_tokens(step):
            def one(index):
                members = slice(index * SUB, (index + 1) * SUB)
                hat, inverse = center(x_in[step, members].astype(F32))
                inverse = jnp.broadcast_to(inverse, hat.shape[:-1] + (LANES,))
                for side, (h_rows, i_rows) in enumerate(zip(split(hat), split(inverse))):
                    size = h_rows.shape[0]
                    begin = (2 * step + side) * TILE + index * size
                    hats[begin : begin + size] = h_rows
                    inverses[begin : begin + size] = i_rows
                    normed[begin : begin + size] = (
                        h_rows * vectors[0:1] + vectors[1:2]
                    ).astype(BF16)

            return [lambda i=i: one(i) for i in range(group // SUB)]

        def finish(tile):
            rows = tile_rows(tile)

            def spread():
                grad_normed[rows] = nt(grad_packed[rows], r["wq"][...])

            def norm_back(piece):
                hat, grad = hats[piece], grad_normed[piece]
                inverse = jnp.concatenate([inverses[piece]] * 2, axis=1)
                sums.gain = sums.gain + fold(grad * hat)
                sums.shift = sums.shift + fold(grad)
                grad = branch_in[piece].astype(F32) + center_back(
                    grad * vectors[0:1], hat, inverse
                )
                grad_normed[piece] = grad

            return [spread] + [lambda p=p: norm_back(p) for p in pieces_of(tile, PIECE)]

        def release(step):
            rows = step_rows(step)
            kept = {}

            def write(index):
                part = TALL // 4
                sides = []
                for side in range(2):
                    begin = (2 * step + side) * TILE + index * part * HALF
                    sides.append(grad_normed[begin : begin + part * HALF])
                block = r["x_blocks"].at[step]
                block[index * part : (index + 1) * part] = join(*sides).astype(BF16)

            def turn():
                kept["normed"] = normed[rows].T

            def weigh(part):
                cut = slice(part * D, (part + 1) * D)
                value = nn(kept["normed"], grad_packed[rows, cut])
                if step == 0:
                    r["acc"][:, cut] = value
                else:
                    r["acc"][:, cut] += value

            return (
                [lambda i=i: write(i) for i in range(4)]
                + [turn]
                + [lambda p=p: weigh(p) for p in range(3)]
            )

        def send_step(step):
            outs.append(
                copies.start(
                    r["x_blocks"].at[step], grad_x.at[:, step * BLOCK : (step + 1) * BLOCK]
                )
            )

        released = [release(step) for step in range(steps)]
        arrive()
        for one in start(0):
            one()
        interleave(soften(0), start(1), read_tokens(0))
        for tile in range(tiles):
            if tile % 2 == 0 and tile + 2 < tiles:
                arrive()
            if tile > 4 and tile % 2:
                send_step((tile - 5) // 2)
            lists = [gather(tile)]
            if tile + 1 < tiles:
                lists.append(soften(tile + 1))
            if tile + 2 < tiles:
                lists.append(start(tile + 2))
            if tile % 2 and (tile + 1) // 2 < steps:
                lists.append(read_tokens((tile + 1) // 2))
            if tile:
                lists.append(finish(tile - 1))
            if tile > 1 and tile % 2:
                lists.append(released[(tile - 3) // 2])
            interleave(*lists)
        send_step(steps - 2)
        interleave(finish(tiles - 1), released[steps - 1][4:])
        for one in released[steps - 1][:4]:
            one()
        send_step(steps - 1)
        flatten(flat, 0, r["acc"][...], ROW_QKV, 6)
        flatten_vector(flat, ROW_GAIN_ONE, column_sum(sums.gain))
        flatten_vector(flat, ROW_SHIFT_ONE, column_sum(sums.shift))
        flat[ROW_OUT : ROW_OUT + 8] = first[...]
        send_rows(plan, place_ref, flat, 0, r["parts_in"], 0, plan.lead)
        outs.append(copies.start(r["parts_in"].at[1], send))
        outs.append(copies.start(r["parts_in"].at[0], keep))
        for copy in outs:
            copy.wait()

    vmem = pl.BlockSpec(memory_space=pltpu.VMEM)
    hbm = pl.BlockSpec(memory_space=pl.ANY)
    shape = jax.ShapeDtypeStruct
    parts = (PLANE, plan.lead, plan.rows, LANES)
    wide = lambda width, kind: pltpu.VMEM((count, width), kind)
    pair = lambda kind: pltpu.VMEM((2, HEADS * TILE, TILE), kind)
    scratch = dict(
        x_in=pltpu.VMEM((steps, group, local_rows, BLOCK, D), BF16),
        packed_in=wide(3 * D, BF16),
        branch_in=wide(D, BF16),
        wq=pltpu.VMEM((D, 3 * D), BF16),
        wo=pltpu.VMEM((D, D), BF16),
        hats=wide(D, F32),
        inverses=wide(LANES, F32),
        normed=wide(D, BF16),
        grad_att=wide(D, BF16),
        scores=pair(F32),
        grad_probs=pair(F32),
        probs=pair(BF16),
        grad_scores=pair(BF16),
        grad_packed=wide(3 * D, BF16),
        grad_normed=wide(D, F32),
        x_blocks=pltpu.VMEM((steps, TALL, BLOCK, D), BF16),
        cap=pltpu.VMEM((TILE, TILE), F32),
        acc=pltpu.VMEM((D, 3 * D), F32),
        flat=pltpu.VMEM((ROW_OUT + plan.rows + 8, LANES), F32),
        parts_in=pltpu.VMEM((CORES,) + parts, BF16),
        sems=pltpu.SemaphoreType.DMA((4 + 4 * steps,)),
    )
    return pl.pallas_call(
        kernel,
        in_specs=[pl.BlockSpec(memory_space=pltpu.SMEM)] + [hbm] * 5 + [vmem] * 3,
        out_specs=[hbm] * 3,
        out_shape=[
            shape((TALL, steps * BLOCK, D), BF16),
            shape(parts, BF16),
            shape(parts, BF16),
        ],
        scratch_shapes=[scratch[name] for name in names],
        compiler_params=pltpu.CompilerParams(vmem_limit_bytes=VMEM_BYTES),
        cost_estimate=pl.CostEstimate(
            flops=10 * 10**9, bytes_accessed=8 * 10**6, transcendentals=10**6
        ),
        name="back",
    )


def cut_kernel(group, steps):
    def kernel(rows_ref, cot_ref, out_ref):
        for member in range(group):
            for step in range(steps):
                column = (member * steps + step) * BLOCK
                for kind, ref in enumerate((rows_ref, cot_ref)):
                    out_ref[member, step, kind] = ref[:, column : column + BLOCK]

    return kernel


def local(mesh_shape, tokens, column_rows, cotangent, flat_params):
    seq = mesh_shape["seq"]
    local_rows, columns = tokens.shape[1], tokens.shape[2]
    group = TALL // local_rows
    owned = columns // group
    steps = owned // BLOCK
    plan = Plan(seq, group, flat_params.shape[0])
    seq_at = lax.axis_index("seq")
    core_at = lax.axis_index("dp")
    deep_at, plane_at = seq_at // PLANE, seq_at % PLANE
    holder = seq_at % group * owned // STRIDE * (seq * STRIDE // columns)
    place = jnp.stack([deep_at, plane_at, core_at, holder]).astype(jnp.int32)
    shift = plan.shard * (seq_at * CORES + core_at) % LANES
    groups = [[group * g + i for i in range(group)] for g in range(seq // group)]
    deep_groups = [[PLANE * z + q for z in range(plan.deep)] for q in range(PLANE)]

    def exchange(blocks):
        return lax.all_to_all(blocks, "seq", 0, 0, axis_index_groups=groups, tiled=True)

    def to_rows(cols):
        moved = exchange(cols.reshape(group, local_rows, owned, D))
        return moved.transpose(1, 0, 2, 3).reshape(tokens.shape)

    def swap_seq(value, distance):
        return lax.ppermute(value, "seq", [(i, i ^ distance) for i in range(seq)])

    def swap_core(value):
        return lax.ppermute(value, "dp", [(0, 1), (1, 0)])

    wide = jnp.pad(flat_params, (LANES, plan.rows * LANES - plan.shard))
    own = lax.dynamic_slice(wide, (LANES - shift,), (plan.rows * LANES,))
    index = lax.iota(jnp.int32, plan.rows * LANES)
    own = jnp.where(index >= (plan.rows - 1) * LANES, column_rows[0, 0].astype(BF16), own)
    own = own.reshape(plan.rows, LANES)
    if plan.pairwise:
        arrived = [swap_seq(own, PLANE * k) for k in range(1, plan.deep)]
        deep = jnp.stack([own] + arrived)
    else:
        arrived = [own]
        deep = lax.all_gather(own, "seq", axis=0, axis_index_groups=deep_groups)
    vmem = pl.BlockSpec(memory_space=pltpu.VMEM)
    both = pl.pallas_call(
        cut_kernel(group, steps),
        out_shape=jax.ShapeDtypeStruct((group, steps, 2, local_rows, BLOCK, D), BF16),
        in_specs=[vmem, vmem],
        out_specs=vmem,
        compiler_params=pltpu.CompilerParams(vmem_limit_bytes=VMEM_BYTES),
        name="cut",
    )(tokens.reshape(local_rows, columns, D), cotangent.reshape(local_rows, columns, D))
    deep, both = lax.optimization_barrier((deep, both))
    both = exchange(both)
    plane = [deep] + [swap_seq(deep, k) for k in range(1, PLANE)]
    pieces = plane + [swap_core(piece) for piece in plane]
    w_qkv, w_out, w_in, w_back, vectors, bias_in = prepare(plan)(place, *pieces)

    packed, logsum, out, branch, keep, send, first = layer(plan, steps, local_rows)(
        place, both, w_qkv, w_out, w_in, w_back, vectors, bias_in
    )

    moved_out = exchange(out.reshape(group, local_rows, owned, D))

    def core_sum(keep, send):
        return keep.astype(F32) + swap_core(send).astype(F32)

    def plane_swap(value):
        sent = value.astype(BF16)
        return [value[0]] + [swap_seq(sent[k], k) for k in range(1, PLANE)]

    def added(pieces):
        total = pieces[0]
        for piece in pieces[1:]:
            total = total + piece.astype(F32)
        return total

    later = added(plane_swap(core_sum(keep, send)))

    grad_x, lead_keep, lead_send = back(plan, steps, local_rows)(
        place, both, packed, branch, w_qkv, w_out, vectors, logsum, first
    )
    lead_send, moved_out, later = lax.optimization_barrier((lead_send, moved_out, later))
    lead = plane_swap(core_sum(lead_keep, lead_send))
    total = jnp.concatenate([added(lead), later], axis=0)
    moved_x = exchange(grad_x.reshape(group, local_rows, owned, D))
    total, moved_x, moved_out = lax.optimization_barrier((total, moved_x, moved_out))
    layer_out = moved_out.transpose(1, 0, 2, 3).reshape(tokens.shape)
    input_grad = moved_x.transpose(1, 0, 2, 3).reshape(tokens.shape).astype(F32)
    if plan.pairwise:
        sent = total.astype(BF16)
        result = lax.dynamic_index_in_dim(total, deep_at, 0, keepdims=False)
        for k in range(1, plan.deep):
            piece = lax.dynamic_index_in_dim(sent, deep_at ^ k, 0, keepdims=False)
            result = result + swap_seq(piece, PLANE * k).astype(F32)
    else:
        moved = lax.all_to_all(
            total.astype(BF16), "seq", 0, 0, axis_index_groups=deep_groups, tiled=True
        )
        result = jnp.sum(moved.astype(F32), axis=0)
    param_grad = lax.dynamic_slice(result.reshape(-1), (shift,), (plan.shard,))
    return layer_out, input_grad, param_grad


def solution(mesh):
    shape = dict(mesh.shape)
    rows = P("dp", "seq", None, None)
    flat = P(("seq", "dp"))
    return jax.shard_map(
        lambda *args: local(shape, *args),
        mesh=mesh,
        in_specs=(rows, P("dp", "seq"), rows, flat),
        out_specs=(rows, rows, flat),
        check_vma=False,
    )
```

```python
import jax
import jax.numpy as jnp
from jax import lax
from jax.experimental import pallas as pl
from jax.experimental.pallas import tpu as pltpu
from jax.sharding import PartitionSpec as P

D = 256
FF = 1024
HEADS = 2
HEAD = D // HEADS
TALL = 32
STRIDE = 96
EPSILON = 1e-05
LANES = 128
PLANE = 4
CORES = 2
BLOCK = 16
HALF = 8
TOKENS = TALL * BLOCK
TILE = TALL * HALF
VMEM_BYTES = 63 * 1024 * 1024

ROW_GAIN_ONE = 0
ROW_SHIFT_ONE = 2
ROW_QKV = 4
ROW_OUT = ROW_QKV + 6 * D
ROW_GAIN_TWO = ROW_OUT + 2 * D
ROW_SHIFT_TWO = ROW_GAIN_TWO + 2
ROW_IN = ROW_SHIFT_TWO + 2
ROW_BIAS_IN = ROW_IN + 8 * D
ROW_BACK = ROW_BIAS_IN + 8
ROW_BIAS_BACK = ROW_BACK + 2 * FF
ROWS = ROW_BIAS_BACK + 2

SPAN = 5

F32 = jnp.float32
BF16 = jnp.bfloat16


def nn(left, right):
    return lax.dot_general(left, right, (((1,), (0,)), ((), ())), preferred_element_type=F32)


def nt(left, right):
    return lax.dot_general(left, right, (((1,), (1,)), ((), ())), preferred_element_type=F32)


def tn(left, right):
    return lax.dot_general(left, right, (((0,), (0,)), ((), ())), preferred_element_type=F32)


def center(value):
    offset = value - jnp.mean(value, axis=-1, keepdims=True)
    inverse = lax.rsqrt(jnp.mean(offset * offset, axis=-1, keepdims=True) + EPSILON)
    return offset * inverse, inverse


def center_back(grad_hat, hat, inverse):
    mean_one = jnp.mean(grad_hat, axis=-1, keepdims=True)
    mean_two = jnp.mean(grad_hat * hat, axis=-1, keepdims=True)
    return inverse * (grad_hat - mean_one - hat * mean_two)


def allowed(span):
    key = lax.broadcasted_iota(jnp.int32, (TILE, TILE), 0)
    query = lax.broadcasted_iota(jnp.int32, (TILE, TILE), 1)
    same_column = (key % HALF) == (query % HALF)
    half_tile = TILE // 2
    same_image = (key // half_tile == query // half_tile) | (span >= TALL)
    return same_column & (key <= query) & same_image


class Plan:
    def __init__(self, seq, group, shard):
        self.shard = shard
        self.group = group
        self.deep = seq // PLANE
        self.count = seq * CORES
        self.pairwise = self.deep == 4
        rows = (shard + LANES - 2) // LANES + 2
        self.rows = -(-rows // 16) * 16
        self.lead = -(-(ROW_OUT * LANES) // (PLANE * CORES * shard))

    def first_row(self, device):
        return self.shard * device // LANES


def prepare(plan):
    def kernel(place_ref, *refs):
        sources, rest = refs[: CORES * PLANE], refs[CORES * PLANE :]
        w_qkv, w_out, w_in, w_back, vectors, bias_in, held, flat, sems = rest
        deep_at, plane_at, core_at = place_ref[0], place_ref[1], place_ref[2]
        copies = []
        for core in range(CORES):
            for plane in range(PLANE):
                source = sources[core * PLANE + plane]
                for deep in range(plan.deep):
                    slot = deep ^ deep_at if plan.pairwise else deep
                    copies.append(
                        pltpu.make_async_copy(
                            source.at[deep],
                            held.at[slot, plane ^ plane_at, core ^ core_at],
                            sems.at[len(copies)],
                        )
                    )
        for copy in copies:
            copy.start()
        for copy in copies:
            copy.wait()
        for device in range(plan.count):
            row = plan.first_row(device)
            value = held[device // 8, device // 2 % PLANE, device % CORES].astype(F32)
            if plan.shard * device % LANES:
                before = flat[row : row + 1]
                flat[row : row + plan.rows] = value
                flat[row : row + 1] = flat[row : row + 1] + before
            else:
                flat[row : row + plan.rows] = value
        for ref, row, wide in (
            (w_qkv, ROW_QKV, 6),
            (w_out, ROW_OUT, 2),
            (w_in, ROW_IN, 8),
            (w_back, ROW_BACK, 2),
        ):
            for part in range(wide):
                ref[:, part * LANES : (part + 1) * LANES] = flat[
                    pl.ds(row + part, ref.shape[0], stride=wide)
                ].astype(BF16)
        for index, row in enumerate(
            (ROW_GAIN_ONE, ROW_SHIFT_ONE, ROW_GAIN_TWO, ROW_SHIFT_TWO, ROW_BIAS_BACK)
        ):
            for part in range(2):
                vectors[index : index + 1, part * LANES : (part + 1) * LANES] = flat[
                    row + part : row + part + 1
                ]
        holder = place_ref[3]
        vectors[SPAN : SPAN + 1, :LANES] = held[holder // PLANE, holder % PLANE, core_at][
            plan.rows - 1 :
        ].astype(F32)
        for part in range(8):
            bias_in[0:1, part * LANES : (part + 1) * LANES] = flat[
                ROW_BIAS_IN + part : ROW_BIAS_IN + part + 1
            ]

    shapes = [((D, 3 * D), BF16), ((D, D), BF16), ((D, FF), BF16), ((FF, D), BF16)]
    shapes += [((8, D), F32), ((8, FF), F32)]
    return pl.pallas_call(
        kernel,
        out_shape=[jax.ShapeDtypeStruct(shape, kind) for shape, kind in shapes],
        in_specs=[pl.BlockSpec(memory_space=pltpu.SMEM)]
        + [pl.BlockSpec(memory_space=pl.ANY)] * (CORES * PLANE),
        out_specs=[pl.BlockSpec(memory_space=pltpu.VMEM)] * len(shapes),
        scratch_shapes=[
            pltpu.VMEM((plan.deep, PLANE, CORES, plan.rows, LANES), BF16),
            pltpu.VMEM((ROWS + plan.rows + 8, LANES), F32),
            pltpu.SemaphoreType.DMA((plan.count,)),
        ],
        compiler_params=pltpu.CompilerParams(vmem_limit_bytes=VMEM_BYTES),
        cost_estimate=pl.CostEstimate(flops=25500000000, bytes_accessed=4 * 10**6, transcendentals=0),
        name="prepare",
    )


SUB = 2
LOG2E = 1.4426950408889634
SCORE_RATE = HEAD**-0.5 * LOG2E
PIECE = 128
SLAB = 16
GELU_RATE = (2.0 / jnp.pi) ** 0.5
GELU_CUBE = GELU_RATE * 0.044715


def interleave(*lists):
    keyed = []
    for order, steps in enumerate(lists):
        for index, step in enumerate(steps):
            keyed.append(((index + 0.5) / len(steps), order, index, step))
    for _, _, _, step in sorted(keyed, key=lambda entry: entry[:3]):
        step()


def fold(value):
    return jnp.sum(value.reshape(-1, 8, value.shape[-1]), axis=0)


def column_sum(value):
    return jnp.sum(value, axis=0, keepdims=True)


class Copies:
    def __init__(self, sems):
        self.sems = sems
        self.used = 0

    def start(self, source, target):
        copy = pltpu.make_async_copy(source, target, self.sems.at[self.used])
        self.used += 1
        copy.start()
        return copy


def tile_rows(tile):
    return slice(tile * TILE, (tile + 1) * TILE)


def step_rows(step):
    return slice(step * TOKENS, (step + 1) * TOKENS)


def pieces_of(tile, size):
    return [
        slice(start, start + size) for start in range(tile * TILE, (tile + 1) * TILE, size)
    ]


def split(block):
    width = block.shape[-1]
    return [
        block[:, :, side * HALF : (side + 1) * HALF].reshape(-1, width) for side in range(2)
    ]


def join(left, right):
    width = left.shape[-1]
    return jnp.concatenate(
        [left.reshape(-1, HALF, width), right.reshape(-1, HALF, width)], axis=1
    )


def two_heads(value):
    blank = jnp.zeros((value.shape[0], HEAD), value.dtype)
    return jnp.concatenate(
        [
            jnp.concatenate([value[:, :HEAD], blank], axis=1),
            jnp.concatenate([blank, value[:, HEAD:]], axis=1),
        ],
        axis=0,
    )


def own_heads(value):
    rows = value.shape[0] // 2
    return jnp.concatenate([value[:rows, :HEAD], value[rows:, HEAD:]], axis=1)


def quarters():
    for head in range(HEADS):
        for part in range(TILE // LANES):
            yield (
                slice(head * TILE, head * TILE + (part + 1) * LANES),
                slice(part * LANES, (part + 1) * LANES),
                head,
            )


def caps(cap, keys, part):
    return cap[: keys.stop - keys.start, part]


def clear_later(*refs):
    for ref in refs:
        for head in range(HEADS):
            for part in range(TILE // LANES - 1):
                keys = slice(head * TILE + (part + 1) * LANES, (head + 1) * TILE)
                cut = slice(part * LANES, (part + 1) * LANES)
                ref[:, keys, cut] = jnp.zeros_like(ref[:, keys, cut])


def flatten(flat, base, matrix, row, wide):
    for part in range(wide):
        flat[pl.ds(row - base + part, matrix.shape[0], stride=wide)] = matrix[
            :, part * LANES : (part + 1) * LANES
        ]


def flatten_vector(flat, row, vector):
    for part in range(vector.shape[-1] // LANES):
        flat[row + part : row + part + 1] = vector[:, part * LANES : (part + 1) * LANES]


def send_rows(plan, place_ref, flat, base, parts, low, high):
    plane_at, core_at = place_ref[1], place_ref[2]
    for device in range(low * PLANE * CORES, high * PLANE * CORES):
        row = plan.first_row(device) - base
        parts[
            (device % CORES) ^ core_at,
            (device // CORES % PLANE) ^ plane_at,
            device // (PLANE * CORES) - low,
        ] = flat[row : row + plan.rows].astype(BF16)


class Sums:
    def __init__(self, **widths):
        for name, width in widths.items():
            setattr(self, name, jnp.zeros((8, width), F32))


def layer(plan, steps, local_rows):
    group, tiles, count = plan.group, 2 * steps, steps * TOKENS
    base = ROW_OUT - 4
    deep = plan.deep - plan.lead
    names = (
        "x_in", "cot_in", "wq", "wo", "wi", "wb", "normed", "packed", "scores", "probs", "cap",
        "attended", "middle", "hats", "inverses", "normed_two", "cots", "inner", "grad_act",
        "activated", "grad_inner", "grad_normed", "branch", "out_blocks", "acc_in", "acc_back",
        "acc_out", "flat", "parts_in", "sems",
    )

    def kernel(place_ref, both, w_qkv, w_out, w_in, w_back, vectors, bias_in, *refs):
        packed_out, logsum, out, branch_out, keep, send, first = refs[:7]
        r = dict(zip(names, refs[7:]))
        x_in, cot_in, packed, middle, hats = (
            r[n] for n in ("x_in", "cot_in", "packed", "middle", "hats")
        )
        scores, probs, cap, attended = (r[n] for n in ("scores", "probs", "cap", "attended"))
        normed, normed_two, cots = r["normed"], r["normed_two"], r["cots"]
        inner, grad_act, activated, grad_inner = (
            r[n] for n in ("inner", "grad_act", "activated", "grad_inner")
        )
        inverses, grad_normed, branch, flat = (
            r[n] for n in ("inverses", "grad_normed", "branch", "flat")
        )
        copies = Copies(r["sems"])
        waits = {}
        arriving = [[copies.start(both.at[:, 0, 0], x_in.at[0])]]
        arriving[0].append(copies.start(w_qkv, r["wq"]))
        arriving.append([copies.start(both.at[:, 1, 0], x_in.at[1])])
        arriving[1].append(copies.start(w_out, r["wo"]))
        arriving.append([copies.start(both.at[:, 0, 1], cot_in.at[0])])
        arriving[2] += [copies.start(w_in, r["wi"]), copies.start(w_back, r["wb"])]
        arriving[2] += [
            copies.start(both.at[:, step, 0], x_in.at[step]) for step in range(2, steps)
        ]
        arriving.append(
            [copies.start(both.at[:, step, 1], cot_in.at[step]) for step in range(1, steps)]
        )
        outs = []

        def arrive():
            for copy in arriving.pop(0):
                copy.wait()

        cap[...] = jnp.where(allowed(vectors[SPAN : SPAN + 1, 0:1]), jnp.inf, -1e30)
        clear_later(probs)
        sums = Sums(gain=D, shift=D, cot=D, **{f"bias{p}": D for p in range(FF // D)})

        def read_tokens(step):
            def one(index):
                members = slice(index * SUB, (index + 1) * SUB)
                value = x_in[step, members].astype(F32)
                hat, _ = center(value)
                hat = hat * vectors[0:1] + vectors[1:2]
                for side, (x_rows, n_rows) in enumerate(zip(split(value), split(hat))):
                    size = x_rows.shape[0]
                    start = (2 * step + side) * TILE + index * size
                    middle[start : start + size] = x_rows
                    normed[start : start + size] = n_rows.astype(BF16)

            return [lambda i=i: one(i) for i in range(group // SUB)]

        def read_cots(step):
            def one(index):
                members = slice(index * SUB, (index + 1) * SUB)
                for side, rows in enumerate(split(cot_in[step, members].astype(F32))):
                    size = rows.shape[0]
                    start = (2 * step + side) * TILE + index * size
                    cots[start : start + size] = rows.astype(BF16)
                    sums.cot = sums.cot + fold(rows)

            return [lambda i=i: one(i) for i in range(group // SUB)]

        def attention(tile):
            rows = tile_rows(tile)
            slot = tile % 2

            def project(part):
                cut = slice(part * D, (part + 1) * D)
                packed[rows, cut] = nn(normed[rows], r["wq"][:, cut]).astype(BF16)

            def score():
                scores[slot] = nt(two_heads(packed[rows, D : 2 * D]), packed[rows, :D])

            def soften(keys, part, head):
                value = jnp.minimum(scores[slot, keys, part] * SCORE_RATE, caps(cap, keys, part))
                peak = jnp.max(value, axis=0, keepdims=True)
                terms = jnp.exp2(value - peak)
                total = jnp.sum(terms, axis=0, keepdims=True)
                probs[slot, keys, part] = (terms * (1.0 / total)).astype(BF16)
                row = tile * HEADS + head
                logsum[row : row + 1, part] = peak + jnp.log2(total)

            def mix():
                attended[rows] = tn(probs[slot], two_heads(packed[rows, 2 * D :])).astype(BF16)

            def add():
                middle[rows] = middle[rows] + nn(attended[rows], r["wo"][...])

            def norm(piece):
                hat, inverse = center(middle[piece])
                hats[piece] = hat
                inverses[piece] = jnp.broadcast_to(inverse, (PIECE, LANES))
                normed_two[piece] = (hat * vectors[2:3] + vectors[3:4]).astype(BF16)

            return (
                [lambda p=p: project(p) for p in range(3)],
                [score] + [lambda q=q: soften(*q) for q in quarters()],
                [mix, add] + [lambda p=p: norm(p) for p in pieces_of(tile, PIECE)],
            )

        def expand(tile, part):
            rows, cut = tile_rows(tile), slice(part * D, (part + 1) * D)
            slot = part

            def up():
                inner[slot] = nn(normed_two[rows], r["wi"][:, cut])

            def down():
                grad_act[slot] = nt(cots[rows], r["wb"][cut, :])

            return up, down

        def activate(tile, part, index):
            cut = slice(part * D, (part + 1) * D)
            slot = part
            inside = slice(index * SLAB, (index + 1) * SLAB)
            rows = slice(tile * TILE + index * SLAB, tile * TILE + (index + 1) * SLAB)
            value = inner[slot, inside] + bias_in[0:1, cut]
            curve = GELU_CUBE * (value * value)
            bend = jnp.tanh(value * (GELU_RATE + curve))
            gate = 0.5 * bend + 0.5
            activated[rows, cut] = (value * gate).astype(BF16)
            rise = (gate * (1.0 - bend)) * value
            slope = gate + rise * (GELU_RATE + 3.0 * curve)
            grad = grad_act[slot, inside] * slope
            grad_inner[rows, cut] = grad.astype(BF16)
            name = f"bias{part}"
            setattr(sums, name, getattr(sums, name) + fold(grad))

        def hidden(tile):
            listed = []
            slabs = TILE // SLAB
            for part in range(FF // D):
                ahead = expand(tile, part + 1) if part + 1 < FF // D else ()
                for index in range(slabs):
                    if ahead and index % (slabs // 2) == 0:
                        listed.append(ahead[index // (slabs // 2)])
                    listed.append(lambda p=part, i=index: activate(tile, p, i))
            return listed

        def finish(tile):
            rows = tile_rows(tile)

            def second():
                middle[rows] = middle[rows] + nn(activated[rows], r["wb"][...])

            def back():
                grad_normed[rows] = nt(grad_inner[rows], r["wi"][...])

            def norm_back(piece):
                hat, grad = hats[piece], grad_normed[piece]
                inverse = jnp.concatenate([inverses[piece]] * 2, axis=1)
                sums.gain = sums.gain + fold(grad * hat)
                sums.shift = sums.shift + fold(grad)
                grad = cots[piece].astype(F32) + center_back(grad * vectors[2:3], hat, inverse)
                branch[piece] = grad.astype(BF16)

            return [second, back] + [lambda p=p: norm_back(p) for p in pieces_of(tile, PIECE)]

        def release(step):
            rows = step_rows(step)
            kept = {}

            def write(index):
                part = TALL // 4
                sides = []
                for side in range(2):
                    start = (2 * step + side) * TILE + index * part * HALF
                    sides.append(middle[start : start + part * HALF] + vectors[4:5])
                block = r["out_blocks"].at[step]
                block[index * part : (index + 1) * part] = join(*sides).astype(BF16)

            def turn_cots():
                kept["cots"] = cots[rows].T

            def turn_normed():
                kept["normed"] = normed_two[rows].T

            def add_to(ref, cut, value):
                if step == 0:
                    ref[:, cut] = value
                else:
                    ref[:, cut] += value

            def weigh(part):
                cut = slice(part * D, (part + 1) * D)
                add_to(r["acc_back"], cut, nn(kept["cots"], activated[rows, cut]))

            def weigh_in(part):
                cut = slice(part * D, (part + 1) * D)
                add_to(r["acc_in"], cut, nn(kept["normed"], grad_inner[rows, cut]))

            def weigh_out():
                add_to(r["acc_out"], slice(0, D), tn(attended[rows], branch[rows]))

            parts = range(FF // D)
            weights = [turn_cots] + [lambda p=p: weigh(p) for p in parts]
            weights += [turn_normed] + [lambda p=p: weigh_in(p) for p in parts]
            return weights, [lambda p=p: write(p) for p in parts] + [weigh_out]

        def send_packed(step):
            rows = step_rows(step)
            outs.append(copies.start(packed.at[rows], packed_out.at[rows]))

        def send_step(step):
            rows = step_rows(step)
            outs.append(copies.start(branch.at[rows], branch_out.at[rows]))
            outs.append(
                copies.start(
                    r["out_blocks"].at[step], out.at[:, step * BLOCK : (step + 1) * BLOCK]
                )
            )

        stages = [attention(tile) for tile in range(tiles)]
        weights, closing = zip(*[release(step) for step in range(steps)])
        arrive()
        for one in read_tokens(0):
            one()
        arrive()
        interleave(stages[0][0], read_tokens(1))
        interleave(stages[1][0], stages[0][1])
        arrive()
        interleave(stages[2][0], stages[1][1], stages[0][2], read_cots(0))
        for one in expand(0, 0):
            one()
        for tile in range(tiles):
            if tile == 1:
                arrive()
                send_packed(0)
            if tile == 3:
                send_packed(1)
            if tile > 4 and tile % 2:
                send_step((tile - 5) // 2)
            lists = [hidden(tile)]
            if tile + 3 < tiles:
                lists.append(stages[tile + 3][0])
            if tile + 2 < tiles:
                lists.append(stages[tile + 2][1])
            if tile + 1 < tiles:
                lists.append(stages[tile + 1][2] + list(expand(tile + 1, 0)))
            if tile % 2 == 0 and tile // 2 + 2 < steps:
                lists.append(read_tokens(tile // 2 + 2))
            if tile % 2 and (tile + 1) // 2 < steps:
                lists.append(read_cots((tile + 1) // 2))
            if tile:
                lists.append(finish(tile - 1))
            if tile > 1 and tile % 2 == 0:
                lists.append(weights[tile // 2 - 1])
            if tile > 1 and tile % 2:
                lists.append(closing[(tile - 3) // 2])
            interleave(*lists)
        last = steps - 1
        send_packed(last)
        send_step(last - 1)
        interleave(finish(tiles - 1), weights[last])
        for one in closing[last]:
            one()
        send_step(last)
        flatten(flat, base, r["acc_back"][...].T, ROW_BACK, 2)
        flatten(flat, base, r["acc_in"][...], ROW_IN, 8)
        flatten(flat, base, r["acc_out"][...], ROW_OUT, 2)
        flatten_vector(flat, ROW_GAIN_TWO - base, column_sum(sums.gain))
        flatten_vector(flat, ROW_SHIFT_TWO - base, column_sum(sums.shift))
        flatten_vector(flat, ROW_BIAS_BACK - base, column_sum(sums.cot))
        for part in range(FF // D):
            flatten_vector(
                flat, ROW_BIAS_IN - base + 2 * part, column_sum(getattr(sums, f"bias{part}"))
            )
        first[...] = flat[ROW_OUT - base : ROW_OUT - base + 8]
        send_rows(
            plan, place_ref, flat, base, r["parts_in"], plan.lead, plan.deep
        )
        outs.append(copies.start(r["parts_in"].at[1], send))
        outs.append(copies.start(r["parts_in"].at[0], keep))
        for copy in outs:
            copy.wait()

    vmem = pl.BlockSpec(memory_space=pltpu.VMEM)
    hbm = pl.BlockSpec(memory_space=pl.ANY)
    shape = jax.ShapeDtypeStruct
    parts = (PLANE, deep, plan.rows, LANES)
    moved = pltpu.VMEM((steps, group, local_rows, BLOCK, D), BF16)
    wide = lambda width, kind: pltpu.VMEM((count, width), kind)
    pair = lambda rows, kind: pltpu.VMEM((2, rows, TILE), kind)
    scratch = dict(
        x_in=moved,
        cot_in=moved,
        wq=pltpu.VMEM((D, 3 * D), BF16),
        wo=pltpu.VMEM((D, D), BF16),
        wi=pltpu.VMEM((D, FF), BF16),
        wb=pltpu.VMEM((FF, D), BF16),
        normed=wide(D, BF16),
        packed=wide(3 * D, BF16),
        scores=pair(HEADS * TILE, F32),
        probs=pair(HEADS * TILE, BF16),
        cap=pltpu.VMEM((TILE, TILE), F32),
        attended=wide(D, BF16),
        middle=wide(D, F32),
        hats=wide(D, F32),
        inverses=wide(LANES, F32),
        normed_two=wide(D, BF16),
        cots=wide(D, BF16),
        inner=pltpu.VMEM((FF // D, TILE, D), F32),
        grad_act=pltpu.VMEM((FF // D, TILE, D), F32),
        activated=wide(FF, BF16),
        grad_inner=wide(FF, BF16),
        grad_normed=wide(D, F32),
        branch=wide(D, BF16),
        out_blocks=pltpu.VMEM((steps, TALL, BLOCK, D), BF16),
        acc_in=pltpu.VMEM((D, FF), F32),
        acc_back=pltpu.VMEM((D, FF), F32),
        acc_out=pltpu.VMEM((D, D), F32),
        flat=pltpu.VMEM((ROWS - base + plan.rows, LANES), F32),
        parts_in=pltpu.VMEM((CORES,) + parts, BF16),
        sems=pltpu.SemaphoreType.DMA((6 + 5 * steps,)),
    )
    return pl.pallas_call(
        kernel,
        in_specs=[pl.BlockSpec(memory_space=pltpu.SMEM)] + [hbm] * 5 + [vmem] * 2,
        out_specs=[hbm, vmem, hbm, hbm, hbm, hbm, vmem],
        out_shape=[
            shape((count, 3 * D), BF16),
            shape((-(-tiles * HEADS // 8) * 8, TILE), F32),
            shape((TALL, steps * BLOCK, D), BF16),
            shape((count, D), BF16),
            shape(parts, BF16),
            shape(parts, BF16),
            shape((8, LANES), F32),
        ],
        scratch_shapes=[scratch[name] for name in names],
        compiler_params=pltpu.CompilerParams(vmem_limit_bytes=VMEM_BYTES),
        cost_estimate=pl.CostEstimate(
            flops=15 * 10**9, bytes_accessed=10**7, transcendentals=2 * 10**6
        ),
        name="layer",
    )


def back(plan, steps, local_rows):
    group, tiles, count = plan.group, 2 * steps, steps * TOKENS
    names = (
        "x_in", "packed_in", "branch_in", "wq", "wo", "hats", "inverses", "normed", "grad_att",
        "scores", "grad_probs", "probs", "grad_scores", "grad_packed", "grad_normed", "x_blocks",
        "cap", "acc", "flat", "parts_in", "sems",
    )

    def kernel(place_ref, both, packed, branch, w_qkv, w_out, vectors, logsum, first, *refs):
        grad_x, keep, send = refs[:3]
        r = dict(zip(names, refs[3:]))
        x_in, packed_in, branch_in = r["x_in"], r["packed_in"], r["branch_in"]
        hats, inverses, normed, cap = r["hats"], r["inverses"], r["normed"], r["cap"]
        grad_att, scores, grad_probs = r["grad_att"], r["scores"], r["grad_probs"]
        probs, grad_scores = r["probs"], r["grad_scores"]
        grad_packed, grad_normed, flat = r["grad_packed"], r["grad_normed"], r["flat"]
        copies = Copies(r["sems"])
        arriving = []
        for step in range(steps):
            rows = step_rows(step)
            arriving.append([copies.start(branch.at[rows], branch_in.at[rows])])
            if step == 0:
                arriving[0].append(copies.start(w_out, r["wo"]))
            arriving[step].append(copies.start(packed.at[rows], packed_in.at[rows]))
            arriving[step].append(copies.start(both.at[:, step, 0], x_in.at[step]))
            if step == 0:
                arriving[0].append(copies.start(w_qkv, r["wq"]))

        def arrive():
            for copy in arriving.pop(0):
                copy.wait()

        outs = []
        cap[...] = jnp.where(allowed(vectors[SPAN : SPAN + 1, 0:1]), jnp.inf, -1e30)
        clear_later(probs, grad_scores)
        sums = Sums(gain=D, shift=D)
        scale = HEAD**-0.5

        def start(tile):
            rows, slot = tile_rows(tile), tile % 2

            def project():
                grad_att[rows] = nt(branch_in[rows], r["wo"][...]).astype(BF16)

            def score():
                scores[slot] = nt(two_heads(packed_in[rows, D : 2 * D]), packed_in[rows, :D])

            def spread():
                grad_probs[slot] = nt(two_heads(packed_in[rows, 2 * D :]), grad_att[rows])

            return [project, score, spread]

        def soften(tile):
            slot = tile % 2

            def one(keys, part, head):
                value = jnp.minimum(scores[slot, keys, part] * SCORE_RATE, caps(cap, keys, part))
                row = tile * HEADS + head
                prob = jnp.exp2(value - logsum[row : row + 1, part])
                weighted = prob * grad_probs[slot, keys, part]
                total = jnp.sum(weighted, axis=0, keepdims=True)
                probs[slot, keys, part] = prob.astype(BF16)
                grad_scores[slot, keys, part] = (weighted - prob * total).astype(BF16)

            return [lambda q=q: one(*q) for q in quarters()]

        def gather(tile):
            rows, slot = tile_rows(tile), tile % 2

            def queries():
                wide = two_heads(packed_in[rows, D : 2 * D])
                grad_packed[rows, :D] = (tn(grad_scores[slot], wide) * scale).astype(BF16)

            def keys():
                value = own_heads(nn(grad_scores[slot], packed_in[rows, :D]))
                grad_packed[rows, D : 2 * D] = (value * scale).astype(BF16)

            def values():
                value = own_heads(nn(probs[slot], grad_att[rows]))
                grad_packed[rows, 2 * D :] = value.astype(BF16)

            return [queries, keys, values]

        def read_tokens(step):
            def one(index):
                members = slice(index * SUB, (index + 1) * SUB)
                hat, inverse = center(x_in[step, members].astype(F32))
                inverse = jnp.broadcast_to(inverse, hat.shape[:-1] + (LANES,))
                for side, (h_rows, i_rows) in enumerate(zip(split(hat), split(inverse))):
                    size = h_rows.shape[0]
                    begin = (2 * step + side) * TILE + index * size
                    hats[begin : begin + size] = h_rows
                    inverses[begin : begin + size] = i_rows
                    normed[begin : begin + size] = (
                        h_rows * vectors[0:1] + vectors[1:2]
                    ).astype(BF16)

            return [lambda i=i: one(i) for i in range(group // SUB)]

        def finish(tile):
            rows = tile_rows(tile)

            def spread():
                grad_normed[rows] = nt(grad_packed[rows], r["wq"][...])

            def norm_back(piece):
                hat, grad = hats[piece], grad_normed[piece]
                inverse = jnp.concatenate([inverses[piece]] * 2, axis=1)
                sums.gain = sums.gain + fold(grad * hat)
                sums.shift = sums.shift + fold(grad)
                grad = branch_in[piece].astype(F32) + center_back(
                    grad * vectors[0:1], hat, inverse
                )
                grad_normed[piece] = grad

            return [spread] + [lambda p=p: norm_back(p) for p in pieces_of(tile, PIECE)]

        def release(step):
            rows = step_rows(step)
            kept = {}

            def write(index):
                part = TALL // 4
                sides = []
                for side in range(2):
                    begin = (2 * step + side) * TILE + index * part * HALF
                    sides.append(grad_normed[begin : begin + part * HALF])
                block = r["x_blocks"].at[step]
                block[index * part : (index + 1) * part] = join(*sides).astype(BF16)

            def turn():
                kept["normed"] = normed[rows].T

            def weigh(part):
                cut = slice(part * D, (part + 1) * D)
                value = nn(kept["normed"], grad_packed[rows, cut])
                if step == 0:
                    r["acc"][:, cut] = value
                else:
                    r["acc"][:, cut] += value

            return (
                [lambda i=i: write(i) for i in range(4)]
                + [turn]
                + [lambda p=p: weigh(p) for p in range(3)]
            )

        def send_step(step):
            outs.append(
                copies.start(
                    r["x_blocks"].at[step], grad_x.at[:, step * BLOCK : (step + 1) * BLOCK]
                )
            )

        released = [release(step) for step in range(steps)]
        arrive()
        for one in start(0):
            one()
        interleave(soften(0), start(1), read_tokens(0))
        for tile in range(tiles):
            if tile % 2 == 0 and tile + 2 < tiles:
                arrive()
            if tile > 4 and tile % 2:
                send_step((tile - 5) // 2)
            lists = [gather(tile)]
            if tile + 1 < tiles:
                lists.append(soften(tile + 1))
            if tile + 2 < tiles:
                lists.append(start(tile + 2))
            if tile % 2 and (tile + 1) // 2 < steps:
                lists.append(read_tokens((tile + 1) // 2))
            if tile:
                lists.append(finish(tile - 1))
            if tile > 1 and tile % 2:
                lists.append(released[(tile - 3) // 2])
            interleave(*lists)
        send_step(steps - 2)
        interleave(finish(tiles - 1), released[steps - 1][4:])
        for one in released[steps - 1][:4]:
            one()
        send_step(steps - 1)
        flatten(flat, 0, r["acc"][...], ROW_QKV, 6)
        flatten_vector(flat, ROW_GAIN_ONE, column_sum(sums.gain))
        flatten_vector(flat, ROW_SHIFT_ONE, column_sum(sums.shift))
        flat[ROW_OUT : ROW_OUT + 8] = first[...]
        send_rows(plan, place_ref, flat, 0, r["parts_in"], 0, plan.lead)
        outs.append(copies.start(r["parts_in"].at[1], send))
        outs.append(copies.start(r["parts_in"].at[0], keep))
        for copy in outs:
            copy.wait()

    vmem = pl.BlockSpec(memory_space=pltpu.VMEM)
    hbm = pl.BlockSpec(memory_space=pl.ANY)
    shape = jax.ShapeDtypeStruct
    parts = (PLANE, plan.lead, plan.rows, LANES)
    wide = lambda width, kind: pltpu.VMEM((count, width), kind)
    pair = lambda kind: pltpu.VMEM((2, HEADS * TILE, TILE), kind)
    scratch = dict(
        x_in=pltpu.VMEM((steps, group, local_rows, BLOCK, D), BF16),
        packed_in=wide(3 * D, BF16),
        branch_in=wide(D, BF16),
        wq=pltpu.VMEM((D, 3 * D), BF16),
        wo=pltpu.VMEM((D, D), BF16),
        hats=wide(D, F32),
        inverses=wide(LANES, F32),
        normed=wide(D, BF16),
        grad_att=wide(D, BF16),
        scores=pair(F32),
        grad_probs=pair(F32),
        probs=pair(BF16),
        grad_scores=pair(BF16),
        grad_packed=wide(3 * D, BF16),
        grad_normed=wide(D, F32),
        x_blocks=pltpu.VMEM((steps, TALL, BLOCK, D), BF16),
        cap=pltpu.VMEM((TILE, TILE), F32),
        acc=pltpu.VMEM((D, 3 * D), F32),
        flat=pltpu.VMEM((ROW_OUT + plan.rows + 8, LANES), F32),
        parts_in=pltpu.VMEM((CORES,) + parts, BF16),
        sems=pltpu.SemaphoreType.DMA((4 + 4 * steps,)),
    )
    return pl.pallas_call(
        kernel,
        in_specs=[pl.BlockSpec(memory_space=pltpu.SMEM)] + [hbm] * 5 + [vmem] * 3,
        out_specs=[hbm] * 3,
        out_shape=[
            shape((TALL, steps * BLOCK, D), BF16),
            shape(parts, BF16),
            shape(parts, BF16),
        ],
        scratch_shapes=[scratch[name] for name in names],
        compiler_params=pltpu.CompilerParams(vmem_limit_bytes=VMEM_BYTES),
        cost_estimate=pl.CostEstimate(
            flops=10 * 10**9, bytes_accessed=8 * 10**6, transcendentals=10**6
        ),
        name="back",
    )


def cut_kernel(group, steps):
    def kernel(rows_ref, cot_ref, out_ref):
        for member in range(group):
            for step in range(steps):
                column = (member * steps + step) * BLOCK
                for kind, ref in enumerate((rows_ref, cot_ref)):
                    out_ref[member, step, kind] = ref[:, column : column + BLOCK]

    return kernel


def local(mesh_shape, tokens, column_rows, cotangent, flat_params):
    seq = mesh_shape["seq"]
    local_rows, columns = tokens.shape[1], tokens.shape[2]
    group = TALL // local_rows
    owned = columns // group
    steps = owned // BLOCK
    plan = Plan(seq, group, flat_params.shape[0])
    seq_at = lax.axis_index("seq")
    core_at = lax.axis_index("dp")
    deep_at, plane_at = seq_at // PLANE, seq_at % PLANE
    holder = seq_at % group * owned // STRIDE * (seq * STRIDE // columns)
    place = jnp.stack([deep_at, plane_at, core_at, holder]).astype(jnp.int32)
    shift = plan.shard * (seq_at * CORES + core_at) % LANES
    groups = [[group * g + i for i in range(group)] for g in range(seq // group)]
    deep_groups = [[PLANE * z + q for z in range(plan.deep)] for q in range(PLANE)]

    def exchange(blocks):
        return lax.all_to_all(blocks, "seq", 0, 0, axis_index_groups=groups, tiled=True)

    def to_rows(cols):
        moved = exchange(cols.reshape(group, local_rows, owned, D))
        return moved.transpose(1, 0, 2, 3).reshape(tokens.shape)

    def swap_seq(value, distance):
        return lax.ppermute(value, "seq", [(i, i ^ distance) for i in range(seq)])

    def swap_core(value):
        return lax.ppermute(value, "dp", [(0, 1), (1, 0)])

    wide = jnp.pad(flat_params, (LANES, plan.rows * LANES - plan.shard))
    own = lax.dynamic_slice(wide, (LANES - shift,), (plan.rows * LANES,))
    index = lax.iota(jnp.int32, plan.rows * LANES)
    own = jnp.where(index >= (plan.rows - 1) * LANES, column_rows[0, 0].astype(BF16), own)
    own = own.reshape(plan.rows, LANES)
    if plan.pairwise:
        arrived = [swap_seq(own, PLANE * k) for k in range(1, plan.deep)]
        deep = jnp.stack([own] + arrived)
    else:
        arrived = [own]
        deep = lax.all_gather(own, "seq", axis=0, axis_index_groups=deep_groups)
    vmem = pl.BlockSpec(memory_space=pltpu.VMEM)
    both = pl.pallas_call(
        cut_kernel(group, steps),
        out_shape=jax.ShapeDtypeStruct((group, steps, 2, local_rows, BLOCK, D), BF16),
        in_specs=[vmem, vmem],
        out_specs=vmem,
        compiler_params=pltpu.CompilerParams(vmem_limit_bytes=VMEM_BYTES),
        name="cut",
    )(tokens.reshape(local_rows, columns, D), cotangent.reshape(local_rows, columns, D))
    deep, both = lax.optimization_barrier((deep, both))
    both = exchange(both)
    plane = [deep] + [swap_seq(deep, k) for k in range(1, PLANE)]
    pieces = plane + [swap_core(piece) for piece in plane]
    w_qkv, w_out, w_in, w_back, vectors, bias_in = prepare(plan)(place, *pieces)

    packed, logsum, out, branch, keep, send, first = layer(plan, steps, local_rows)(
        place, both, w_qkv, w_out, w_in, w_back, vectors, bias_in
    )

    moved_out = exchange(out.reshape(group, local_rows, owned, D))

    def core_sum(keep, send):
        return keep.astype(F32) + swap_core(send).astype(F32)

    def plane_swap(value):
        sent = value.astype(BF16)
        return [value[0]] + [swap_seq(sent[k], k) for k in range(1, PLANE)]

    def added(pieces):
        total = pieces[0]
        for piece in pieces[1:]:
            total = total + piece.astype(F32)
        return total

    later = added(plane_swap(core_sum(keep, send)))

    grad_x, lead_keep, lead_send = back(plan, steps, local_rows)(
        place, both, packed, branch, w_qkv, w_out, vectors, logsum, first
    )
    lead_send, moved_out, later = lax.optimization_barrier((lead_send, moved_out, later))
    lead = plane_swap(core_sum(lead_keep, lead_send))
    total = jnp.concatenate([added(lead), later], axis=0)
    moved_x = exchange(grad_x.reshape(group, local_rows, owned, D))
    total, moved_x, moved_out = lax.optimization_barrier((total, moved_x, moved_out))
    layer_out = moved_out.transpose(1, 0, 2, 3).reshape(tokens.shape)
    input_grad = moved_x.transpose(1, 0, 2, 3).reshape(tokens.shape).astype(F32)
    if plan.pairwise:
        sent = total.astype(BF16)
        result = lax.dynamic_index_in_dim(total, deep_at, 0, keepdims=False)
        for k in range(1, plan.deep):
            piece = lax.dynamic_index_in_dim(sent, deep_at ^ k, 0, keepdims=False)
            result = result + swap_seq(piece, PLANE * k).astype(F32)
    else:
        moved = lax.all_to_all(
            total.astype(BF16), "seq", 0, 0, axis_index_groups=deep_groups, tiled=True
        )
        result = jnp.sum(moved.astype(F32), axis=0)
    param_grad = lax.dynamic_slice(result.reshape(-1), (shift,), (plan.shard,))
    return layer_out, input_grad, param_grad


def solution(mesh):
    shape = dict(mesh.shape)
    rows = P("dp", "seq", None, None)
    flat = P(("seq", "dp"))
    return jax.shard_map(
        lambda *args: local(shape, *args),
        mesh=mesh,
        in_specs=(rows, P("dp", "seq"), rows, flat),
        out_specs=(rows, rows, flat),
        check_vma=False,
    )
```

```python
import jax
import jax.numpy as jnp
from jax import lax
from jax.experimental import pallas as pl
from jax.experimental.pallas import tpu as pltpu
from jax.sharding import PartitionSpec as P

D = 256
FF = 1024
HEADS = 2
HEAD = D // HEADS
TALL = 32
STRIDE = 96
EPSILON = 1e-05
LANES = 128
PLANE = 4
CORES = 2
BLOCK = 16
HALF = 8
TOKENS = TALL * BLOCK
TILE = TALL * HALF
VMEM_BYTES = 63 * 1024 * 1024

ROW_GAIN_ONE = 0
ROW_SHIFT_ONE = 2
ROW_QKV = 4
ROW_OUT = ROW_QKV + 6 * D
ROW_GAIN_TWO = ROW_OUT + 2 * D
ROW_SHIFT_TWO = ROW_GAIN_TWO + 2
ROW_IN = ROW_SHIFT_TWO + 2
ROW_BIAS_IN = ROW_IN + 8 * D
ROW_BACK = ROW_BIAS_IN + 8
ROW_BIAS_BACK = ROW_BACK + 2 * FF
ROWS = ROW_BIAS_BACK + 2

SPAN = 5

F32 = jnp.float32
BF16 = jnp.bfloat16


def nn(left, right):
    return lax.dot_general(left, right, (((1,), (0,)), ((), ())), preferred_element_type=F32)


def nt(left, right):
    return lax.dot_general(left, right, (((1,), (1,)), ((), ())), preferred_element_type=F32)


def tn(left, right):
    return lax.dot_general(left, right, (((0,), (0,)), ((), ())), preferred_element_type=F32)


def center(value):
    offset = value - jnp.mean(value, axis=-1, keepdims=True)
    inverse = lax.rsqrt(jnp.mean(offset * offset, axis=-1, keepdims=True) + EPSILON)
    return offset * inverse, inverse


def center_back(grad_hat, hat, inverse):
    mean_one = jnp.mean(grad_hat, axis=-1, keepdims=True)
    mean_two = jnp.mean(grad_hat * hat, axis=-1, keepdims=True)
    return inverse * (grad_hat - mean_one - hat * mean_two)


def allowed(span):
    key = lax.broadcasted_iota(jnp.int32, (TILE, TILE), 0)
    query = lax.broadcasted_iota(jnp.int32, (TILE, TILE), 1)
    same_column = (key % HALF) == (query % HALF)
    half_tile = TILE // 2
    same_image = (key // half_tile == query // half_tile) | (span >= TALL)
    return same_column & (key <= query) & same_image


class Plan:
    def __init__(self, seq, group, shard):
        self.shard = shard
        self.group = group
        self.deep = seq // PLANE
        self.count = seq * CORES
        self.pairwise = self.deep == 4
        rows = (shard + LANES - 2) // LANES + 2
        self.rows = -(-rows // 16) * 16
        self.lead = -(-(ROW_OUT * LANES) // (PLANE * CORES * shard))

    def first_row(self, device):
        return self.shard * device // LANES


def prepare(plan):
    def kernel(place_ref, *refs):
        sources, rest = refs[: CORES * PLANE], refs[CORES * PLANE :]
        w_qkv, w_out, w_in, w_back, vectors, bias_in, held, flat, sems = rest
        deep_at, plane_at, core_at = place_ref[0], place_ref[1], place_ref[2]
        copies = []
        for core in range(CORES):
            for plane in range(PLANE):
                source = sources[core * PLANE + plane]
                for deep in range(plan.deep):
                    slot = deep ^ deep_at if plan.pairwise else deep
                    copies.append(
                        pltpu.make_async_copy(
                            source.at[deep],
                            held.at[slot, plane ^ plane_at, core ^ core_at],
                            sems.at[len(copies)],
                        )
                    )
        for copy in copies:
            copy.start()
        for copy in copies:
            copy.wait()
        for device in range(plan.count):
            row = plan.first_row(device)
            value = held[device // 8, device // 2 % PLANE, device % CORES].astype(F32)
            if plan.shard * device % LANES:
                before = flat[row : row + 1]
                flat[row : row + plan.rows] = value
                flat[row : row + 1] = flat[row : row + 1] + before
            else:
                flat[row : row + plan.rows] = value
        for ref, row, wide in (
            (w_qkv, ROW_QKV, 6),
            (w_out, ROW_OUT, 2),
            (w_in, ROW_IN, 8),
            (w_back, ROW_BACK, 2),
        ):
            for part in range(wide):
                ref[:, part * LANES : (part + 1) * LANES] = flat[
                    pl.ds(row + part, ref.shape[0], stride=wide)
                ].astype(BF16)
        for index, row in enumerate(
            (ROW_GAIN_ONE, ROW_SHIFT_ONE, ROW_GAIN_TWO, ROW_SHIFT_TWO, ROW_BIAS_BACK)
        ):
            for part in range(2):
                vectors[index : index + 1, part * LANES : (part + 1) * LANES] = flat[
                    row + part : row + part + 1
                ]
        holder = place_ref[3]
        vectors[SPAN : SPAN + 1, :LANES] = held[holder // PLANE, holder % PLANE, core_at][
            plan.rows - 1 :
        ].astype(F32)
        for part in range(8):
            bias_in[0:1, part * LANES : (part + 1) * LANES] = flat[
                ROW_BIAS_IN + part : ROW_BIAS_IN + part + 1
            ]

    shapes = [((D, 3 * D), BF16), ((D, D), BF16), ((D, FF), BF16), ((FF, D), BF16)]
    shapes += [((8, D), F32), ((8, FF), F32)]
    return pl.pallas_call(
        kernel,
        out_shape=[jax.ShapeDtypeStruct(shape, kind) for shape, kind in shapes],
        in_specs=[pl.BlockSpec(memory_space=pltpu.SMEM)]
        + [pl.BlockSpec(memory_space=pl.ANY)] * (CORES * PLANE),
        out_specs=[pl.BlockSpec(memory_space=pltpu.VMEM)] * len(shapes),
        scratch_shapes=[
            pltpu.VMEM((plan.deep, PLANE, CORES, plan.rows, LANES), BF16),
            pltpu.VMEM((ROWS + plan.rows + 8, LANES), F32),
            pltpu.SemaphoreType.DMA((plan.count,)),
        ],
        compiler_params=pltpu.CompilerParams(vmem_limit_bytes=VMEM_BYTES),
        cost_estimate=pl.CostEstimate(flops=25500000000, bytes_accessed=4 * 10**6, transcendentals=0),
        name="prepare",
    )


SUB = 2
LOG2E = 1.4426950408889634
SCORE_RATE = HEAD**-0.5 * LOG2E
PIECE = 128
SLAB = 16
GELU_RATE = (2.0 / jnp.pi) ** 0.5
GELU_CUBE = GELU_RATE * 0.044715


def interleave(*lists):
    keyed = []
    for order, steps in enumerate(lists):
        for index, step in enumerate(steps):
            keyed.append(((index + 0.5) / len(steps), order, index, step))
    for _, _, _, step in sorted(keyed, key=lambda entry: entry[:3]):
        step()


def fold(value):
    return jnp.sum(value.reshape(-1, 8, value.shape[-1]), axis=0)


def column_sum(value):
    return jnp.sum(value, axis=0, keepdims=True)


class Copies:
    def __init__(self, sems):
        self.sems = sems
        self.used = 0

    def start(self, source, target):
        copy = pltpu.make_async_copy(source, target, self.sems.at[self.used])
        self.used += 1
        copy.start()
        return copy


def tile_rows(tile):
    return slice(tile * TILE, (tile + 1) * TILE)


def step_rows(step):
    return slice(step * TOKENS, (step + 1) * TOKENS)


def pieces_of(tile, size):
    return [
        slice(start, start + size) for start in range(tile * TILE, (tile + 1) * TILE, size)
    ]


def split(block):
    width = block.shape[-1]
    return [
        block[:, :, side * HALF : (side + 1) * HALF].reshape(-1, width) for side in range(2)
    ]


def join(left, right):
    width = left.shape[-1]
    return jnp.concatenate(
        [left.reshape(-1, HALF, width), right.reshape(-1, HALF, width)], axis=1
    )


def two_heads(value):
    blank = jnp.zeros((value.shape[0], HEAD), value.dtype)
    return jnp.concatenate(
        [
            jnp.concatenate([value[:, :HEAD], blank], axis=1),
            jnp.concatenate([blank, value[:, HEAD:]], axis=1),
        ],
        axis=0,
    )


def own_heads(value):
    rows = value.shape[0] // 2
    return jnp.concatenate([value[:rows, :HEAD], value[rows:, HEAD:]], axis=1)


def quarters():
    for head in range(HEADS):
        for part in range(TILE // LANES):
            yield (
                slice(head * TILE, head * TILE + (part + 1) * LANES),
                slice(part * LANES, (part + 1) * LANES),
                head,
            )


def caps(cap, keys, part):
    return cap[: keys.stop - keys.start, part]


def clear_later(*refs):
    for ref in refs:
        for head in range(HEADS):
            for part in range(TILE // LANES - 1):
                keys = slice(head * TILE + (part + 1) * LANES, (head + 1) * TILE)
                cut = slice(part * LANES, (part + 1) * LANES)
                ref[:, keys, cut] = jnp.zeros_like(ref[:, keys, cut])


def flatten(flat, base, matrix, row, wide):
    for part in range(wide):
        flat[pl.ds(row - base + part, matrix.shape[0], stride=wide)] = matrix[
            :, part * LANES : (part + 1) * LANES
        ]


def flatten_vector(flat, row, vector):
    for part in range(vector.shape[-1] // LANES):
        flat[row + part : row + part + 1] = vector[:, part * LANES : (part + 1) * LANES]


def send_rows(plan, place_ref, flat, base, parts, low, high):
    plane_at, core_at = place_ref[1], place_ref[2]
    for device in range(low * PLANE * CORES, high * PLANE * CORES):
        row = plan.first_row(device) - base
        parts[
            (device % CORES) ^ core_at,
            (device // CORES % PLANE) ^ plane_at,
            device // (PLANE * CORES) - low,
        ] = flat[row : row + plan.rows].astype(BF16)


class Sums:
    def __init__(self, **widths):
        for name, width in widths.items():
            setattr(self, name, jnp.zeros((8, width), F32))


def layer(plan, steps, local_rows):
    group, tiles, count = plan.group, 2 * steps, steps * TOKENS
    base = ROW_OUT - 4
    deep = plan.deep - plan.lead
    names = (
        "x_in", "cot_in", "wq", "wo", "wi", "wb", "normed", "packed", "scores", "probs", "cap",
        "attended", "middle", "hats", "inverses", "normed_two", "cots", "inner", "grad_act",
        "activated", "grad_inner", "grad_normed", "branch", "out_blocks", "acc_in", "acc_back",
        "acc_out", "flat", "parts_in", "sems",
    )

    def kernel(place_ref, both, w_qkv, w_out, w_in, w_back, vectors, bias_in, *refs):
        packed_out, logsum, out, branch_out, keep, send, first = refs[:7]
        r = dict(zip(names, refs[7:]))
        x_in, cot_in, packed, middle, hats = (
            r[n] for n in ("x_in", "cot_in", "packed", "middle", "hats")
        )
        scores, probs, cap, attended = (r[n] for n in ("scores", "probs", "cap", "attended"))
        normed, normed_two, cots = r["normed"], r["normed_two"], r["cots"]
        inner, grad_act, activated, grad_inner = (
            r[n] for n in ("inner", "grad_act", "activated", "grad_inner")
        )
        inverses, grad_normed, branch, flat = (
            r[n] for n in ("inverses", "grad_normed", "branch", "flat")
        )
        copies = Copies(r["sems"])
        waits = {}
        arriving = [[copies.start(both.at[:, 0, 0], x_in.at[0])]]
        arriving[0].append(copies.start(w_qkv, r["wq"]))
        arriving.append([copies.start(both.at[:, 1, 0], x_in.at[1])])
        arriving[1].append(copies.start(w_out, r["wo"]))
        arriving.append([copies.start(both.at[:, 0, 1], cot_in.at[0])])
        arriving[2] += [copies.start(w_in, r["wi"]), copies.start(w_back, r["wb"])]
        arriving[2] += [
            copies.start(both.at[:, step, 0], x_in.at[step]) for step in range(2, steps)
        ]
        arriving.append(
            [copies.start(both.at[:, step, 1], cot_in.at[step]) for step in range(1, steps)]
        )
        outs = []

        def arrive():
            for copy in arriving.pop(0):
                copy.wait()

        cap[...] = jnp.where(allowed(vectors[SPAN : SPAN + 1, 0:1]), jnp.inf, -1e30)
        clear_later(probs)
        sums = Sums(gain=D, shift=D, cot=D, **{f"bias{p}": D for p in range(FF // D)})

        def read_tokens(step):
            def one(index):
                members = slice(index * SUB, (index + 1) * SUB)
                value = x_in[step, members].astype(F32)
                hat, _ = center(value)
                hat = hat * vectors[0:1] + vectors[1:2]
                for side, (x_rows, n_rows) in enumerate(zip(split(value), split(hat))):
                    size = x_rows.shape[0]
                    start = (2 * step + side) * TILE + index * size
                    middle[start : start + size] = x_rows
                    normed[start : start + size] = n_rows.astype(BF16)

            return [lambda i=i: one(i) for i in range(group // SUB)]

        def read_cots(step):
            def one(index):
                members = slice(index * SUB, (index + 1) * SUB)
                for side, rows in enumerate(split(cot_in[step, members].astype(F32))):
                    size = rows.shape[0]
                    start = (2 * step + side) * TILE + index * size
                    cots[start : start + size] = rows.astype(BF16)
                    sums.cot = sums.cot + fold(rows)

            return [lambda i=i: one(i) for i in range(group // SUB)]

        def attention(tile):
            rows = tile_rows(tile)
            slot = tile % 2

            def project(part):
                cut = slice(part * D, (part + 1) * D)
                packed[rows, cut] = nn(normed[rows], r["wq"][:, cut]).astype(BF16)

            def score():
                scores[slot] = nt(two_heads(packed[rows, D : 2 * D]), packed[rows, :D])

            def soften(keys, part, head):
                value = jnp.minimum(scores[slot, keys, part] * SCORE_RATE, caps(cap, keys, part))
                peak = jnp.max(value, axis=0, keepdims=True)
                terms = jnp.exp2(value - peak)
                total = jnp.sum(terms, axis=0, keepdims=True)
                probs[slot, keys, part] = (terms * (1.0 / total)).astype(BF16)
                row = tile * HEADS + head
                logsum[row : row + 1, part] = peak + jnp.log2(total)

            def mix():
                attended[rows] = tn(probs[slot], two_heads(packed[rows, 2 * D :])).astype(BF16)

            def add():
                middle[rows] = middle[rows] + nn(attended[rows], r["wo"][...])

            def norm(piece):
                hat, inverse = center(middle[piece])
                hats[piece] = hat
                inverses[piece] = jnp.broadcast_to(inverse, (PIECE, LANES))
                normed_two[piece] = (hat * vectors[2:3] + vectors[3:4]).astype(BF16)

            return (
                [lambda p=p: project(p) for p in range(3)],
                [score] + [lambda q=q: soften(*q) for q in quarters()],
                [mix, add] + [lambda p=p: norm(p) for p in pieces_of(tile, PIECE)],
            )

        def expand(tile, part):
            rows, cut = tile_rows(tile), slice(part * D, (part + 1) * D)
            slot = part

            def up():
                inner[slot] = nn(normed_two[rows], r["wi"][:, cut])

            def down():
                grad_act[slot] = nt(cots[rows], r["wb"][cut, :])

            return up, down

        def activate(tile, part, index):
            cut = slice(part * D, (part + 1) * D)
            slot = part
            inside = slice(index * SLAB, (index + 1) * SLAB)
            rows = slice(tile * TILE + index * SLAB, tile * TILE + (index + 1) * SLAB)
            value = inner[slot, inside] + bias_in[0:1, cut]
            curve = GELU_CUBE * (value * value)
            bend = jnp.tanh(value * (GELU_RATE + curve))
            gate = 0.5 * bend + 0.5
            activated[rows, cut] = (value * gate).astype(BF16)
            rise = (gate * (1.0 - bend)) * value
            slope = gate + rise * (GELU_RATE + 3.0 * curve)
            grad = grad_act[slot, inside] * slope
            grad_inner[rows, cut] = grad.astype(BF16)
            name = f"bias{part}"
            setattr(sums, name, getattr(sums, name) + fold(grad))

        def hidden(tile):
            listed = []
            slabs = TILE // SLAB
            for part in range(FF // D):
                ahead = expand(tile, part + 1) if part + 1 < FF // D else ()
                for index in range(slabs):
                    if ahead and index % (slabs // 2) == 0:
                        listed.append(ahead[index // (slabs // 2)])
                    listed.append(lambda p=part, i=index: activate(tile, p, i))
            return listed

        def finish(tile):
            rows = tile_rows(tile)

            def second():
                middle[rows] = middle[rows] + nn(activated[rows], r["wb"][...])

            def back():
                grad_normed[rows] = nt(grad_inner[rows], r["wi"][...])

            def norm_back(piece):
                hat, grad = hats[piece], grad_normed[piece]
                inverse = jnp.concatenate([inverses[piece]] * 2, axis=1)
                sums.gain = sums.gain + fold(grad * hat)
                sums.shift = sums.shift + fold(grad)
                grad = cots[piece].astype(F32) + center_back(grad * vectors[2:3], hat, inverse)
                branch[piece] = grad.astype(BF16)

            return [second, back] + [lambda p=p: norm_back(p) for p in pieces_of(tile, PIECE)]

        def release(step):
            rows = step_rows(step)
            kept = {}

            def write(index):
                part = TALL // 4
                sides = []
                for side in range(2):
                    start = (2 * step + side) * TILE + index * part * HALF
                    sides.append(middle[start : start + part * HALF] + vectors[4:5])
                block = r["out_blocks"].at[step]
                block[index * part : (index + 1) * part] = join(*sides).astype(BF16)

            def turn_cots():
                kept["cots"] = cots[rows].T

            def turn_normed():
                kept["normed"] = normed_two[rows].T

            def add_to(ref, cut, value):
                if step == 0:
                    ref[:, cut] = value
                else:
                    ref[:, cut] += value

            def weigh(part):
                cut = slice(part * D, (part + 1) * D)
                add_to(r["acc_back"], cut, nn(kept["cots"], activated[rows, cut]))

            def weigh_in(part):
                cut = slice(part * D, (part + 1) * D)
                add_to(r["acc_in"], cut, nn(kept["normed"], grad_inner[rows, cut]))

            def weigh_out():
                add_to(r["acc_out"], slice(0, D), tn(attended[rows], branch[rows]))

            parts = range(FF // D)
            weights = [turn_cots] + [lambda p=p: weigh(p) for p in parts]
            weights += [turn_normed] + [lambda p=p: weigh_in(p) for p in parts]
            return weights, [lambda p=p: write(p) for p in parts] + [weigh_out]

        def send_packed(step):
            rows = step_rows(step)
            outs.append(copies.start(packed.at[rows], packed_out.at[rows]))

        def send_step(step):
            rows = step_rows(step)
            outs.append(copies.start(branch.at[rows], branch_out.at[rows]))
            outs.append(
                copies.start(
                    r["out_blocks"].at[step], out.at[:, step * BLOCK : (step + 1) * BLOCK]
                )
            )

        stages = [attention(tile) for tile in range(tiles)]
        weights, closing = zip(*[release(step) for step in range(steps)])
        arrive()
        for one in read_tokens(0):
            one()
        arrive()
        interleave(stages[0][0], read_tokens(1))
        interleave(stages[1][0], stages[0][1])
        arrive()
        interleave(stages[2][0], stages[1][1], stages[0][2], read_cots(0))
        for one in expand(0, 0):
            one()
        for tile in range(tiles):
            if tile == 1:
                arrive()
                send_packed(0)
            if tile == 3:
                send_packed(1)
            if tile > 4 and tile % 2:
                send_step((tile - 5) // 2)
            lists = [hidden(tile)]
            if tile + 3 < tiles:
                lists.append(stages[tile + 3][0])
            if tile + 2 < tiles:
                lists.append(stages[tile + 2][1])
            if tile + 1 < tiles:
                lists.append(stages[tile + 1][2] + list(expand(tile + 1, 0)))
            if tile % 2 == 0 and tile // 2 + 2 < steps:
                lists.append(read_tokens(tile // 2 + 2))
            if tile % 2 and (tile + 1) // 2 < steps:
                lists.append(read_cots((tile + 1) // 2))
            if tile:
                lists.append(finish(tile - 1))
            if tile > 1 and tile % 2 == 0:
                lists.append(weights[tile // 2 - 1])
            if tile > 1 and tile % 2:
                lists.append(closing[(tile - 3) // 2])
            interleave(*lists)
        last = steps - 1
        send_packed(last)
        send_step(last - 1)
        half = len(weights[last]) // 2
        interleave(finish(tiles - 1), weights[last][:half])
        turned = [lambda: flatten(flat, base, r["acc_back"][...].T, ROW_BACK, 2)]
        interleave(weights[last][half:], turned, closing[last])
        send_step(last)
        flatten(flat, base, r["acc_in"][...], ROW_IN, 8)
        flatten(flat, base, r["acc_out"][...], ROW_OUT, 2)
        flatten_vector(flat, ROW_GAIN_TWO - base, column_sum(sums.gain))
        flatten_vector(flat, ROW_SHIFT_TWO - base, column_sum(sums.shift))
        flatten_vector(flat, ROW_BIAS_BACK - base, column_sum(sums.cot))
        for part in range(FF // D):
            flatten_vector(
                flat, ROW_BIAS_IN - base + 2 * part, column_sum(getattr(sums, f"bias{part}"))
            )
        first[...] = flat[ROW_OUT - base : ROW_OUT - base + 8]
        send_rows(
            plan, place_ref, flat, base, r["parts_in"], plan.lead, plan.deep
        )
        outs.append(copies.start(r["parts_in"].at[1], send))
        outs.append(copies.start(r["parts_in"].at[0], keep))
        for copy in outs:
            copy.wait()

    vmem = pl.BlockSpec(memory_space=pltpu.VMEM)
    hbm = pl.BlockSpec(memory_space=pl.ANY)
    shape = jax.ShapeDtypeStruct
    parts = (PLANE, deep, plan.rows, LANES)
    moved = pltpu.VMEM((steps, group, local_rows, BLOCK, D), BF16)
    wide = lambda width, kind: pltpu.VMEM((count, width), kind)
    pair = lambda rows, kind: pltpu.VMEM((2, rows, TILE), kind)
    scratch = dict(
        x_in=moved,
        cot_in=moved,
        wq=pltpu.VMEM((D, 3 * D), BF16),
        wo=pltpu.VMEM((D, D), BF16),
        wi=pltpu.VMEM((D, FF), BF16),
        wb=pltpu.VMEM((FF, D), BF16),
        normed=wide(D, BF16),
        packed=wide(3 * D, BF16),
        scores=pair(HEADS * TILE, F32),
        probs=pair(HEADS * TILE, BF16),
        cap=pltpu.VMEM((TILE, TILE), F32),
        attended=wide(D, BF16),
        middle=wide(D, F32),
        hats=wide(D, F32),
        inverses=wide(LANES, F32),
        normed_two=wide(D, BF16),
        cots=wide(D, BF16),
        inner=pltpu.VMEM((FF // D, TILE, D), F32),
        grad_act=pltpu.VMEM((FF // D, TILE, D), F32),
        activated=wide(FF, BF16),
        grad_inner=wide(FF, BF16),
        grad_normed=wide(D, F32),
        branch=wide(D, BF16),
        out_blocks=pltpu.VMEM((steps, TALL, BLOCK, D), BF16),
        acc_in=pltpu.VMEM((D, FF), F32),
        acc_back=pltpu.VMEM((D, FF), F32),
        acc_out=pltpu.VMEM((D, D), F32),
        flat=pltpu.VMEM((ROWS - base + plan.rows, LANES), F32),
        parts_in=pltpu.VMEM((CORES,) + parts, BF16),
        sems=pltpu.SemaphoreType.DMA((6 + 5 * steps,)),
    )
    return pl.pallas_call(
        kernel,
        in_specs=[pl.BlockSpec(memory_space=pltpu.SMEM)] + [hbm] * 5 + [vmem] * 2,
        out_specs=[hbm, vmem, hbm, hbm, hbm, hbm, vmem],
        out_shape=[
            shape((count, 3 * D), BF16),
            shape((-(-tiles * HEADS // 8) * 8, TILE), F32),
            shape((TALL, steps * BLOCK, D), BF16),
            shape((count, D), BF16),
            shape(parts, BF16),
            shape(parts, BF16),
            shape((8, LANES), F32),
        ],
        scratch_shapes=[scratch[name] for name in names],
        compiler_params=pltpu.CompilerParams(vmem_limit_bytes=VMEM_BYTES),
        cost_estimate=pl.CostEstimate(
            flops=15 * 10**9, bytes_accessed=10**7, transcendentals=2 * 10**6
        ),
        name="layer",
    )


def back(plan, steps, local_rows):
    group, tiles, count = plan.group, 2 * steps, steps * TOKENS
    names = (
        "x_in", "packed_in", "branch_in", "wq", "wo", "hats", "inverses", "normed", "grad_att",
        "scores", "grad_probs", "probs", "grad_scores", "grad_packed", "grad_normed", "x_blocks",
        "cap", "acc", "flat", "parts_in", "sems",
    )

    def kernel(place_ref, both, packed, branch, w_qkv, w_out, vectors, logsum, first, *refs):
        grad_x, keep, send = refs[:3]
        r = dict(zip(names, refs[3:]))
        x_in, packed_in, branch_in = r["x_in"], r["packed_in"], r["branch_in"]
        hats, inverses, normed, cap = r["hats"], r["inverses"], r["normed"], r["cap"]
        grad_att, scores, grad_probs = r["grad_att"], r["scores"], r["grad_probs"]
        probs, grad_scores = r["probs"], r["grad_scores"]
        grad_packed, grad_normed, flat = r["grad_packed"], r["grad_normed"], r["flat"]
        copies = Copies(r["sems"])
        arriving = []
        for step in range(steps):
            rows = step_rows(step)
            arriving.append([copies.start(branch.at[rows], branch_in.at[rows])])
            if step == 0:
                arriving[0].append(copies.start(w_out, r["wo"]))
            arriving[step].append(copies.start(packed.at[rows], packed_in.at[rows]))
            arriving[step].append(copies.start(both.at[:, step, 0], x_in.at[step]))
            if step == 0:
                arriving[0].append(copies.start(w_qkv, r["wq"]))

        def arrive():
            for copy in arriving.pop(0):
                copy.wait()

        outs = []
        cap[...] = jnp.where(allowed(vectors[SPAN : SPAN + 1, 0:1]), jnp.inf, -1e30)
        clear_later(probs, grad_scores)
        sums = Sums(gain=D, shift=D)
        scale = HEAD**-0.5

        def start(tile):
            rows, slot = tile_rows(tile), tile % 2

            def project():
                grad_att[rows] = nt(branch_in[rows], r["wo"][...]).astype(BF16)

            def score():
                scores[slot] = nt(two_heads(packed_in[rows, D : 2 * D]), packed_in[rows, :D])

            def spread():
                grad_probs[slot] = nt(two_heads(packed_in[rows, 2 * D :]), grad_att[rows])

            return [project, score, spread]

        def soften(tile):
            slot = tile % 2

            def one(keys, part, head):
                value = jnp.minimum(scores[slot, keys, part] * SCORE_RATE, caps(cap, keys, part))
                row = tile * HEADS + head
                prob = jnp.exp2(value - logsum[row : row + 1, part])
                weighted = prob * grad_probs[slot, keys, part]
                total = jnp.sum(weighted, axis=0, keepdims=True)
                probs[slot, keys, part] = prob.astype(BF16)
                grad_scores[slot, keys, part] = (weighted - prob * total).astype(BF16)

            return [lambda q=q: one(*q) for q in quarters()]

        def gather(tile):
            rows, slot = tile_rows(tile), tile % 2

            def queries():
                wide = two_heads(packed_in[rows, D : 2 * D])
                grad_packed[rows, :D] = (tn(grad_scores[slot], wide) * scale).astype(BF16)

            def keys():
                value = own_heads(nn(grad_scores[slot], packed_in[rows, :D]))
                grad_packed[rows, D : 2 * D] = (value * scale).astype(BF16)

            def values():
                value = own_heads(nn(probs[slot], grad_att[rows]))
                grad_packed[rows, 2 * D :] = value.astype(BF16)

            return [queries, keys, values]

        def read_tokens(step):
            def one(index):
                members = slice(index * SUB, (index + 1) * SUB)
                hat, inverse = center(x_in[step, members].astype(F32))
                inverse = jnp.broadcast_to(inverse, hat.shape[:-1] + (LANES,))
                for side, (h_rows, i_rows) in enumerate(zip(split(hat), split(inverse))):
                    size = h_rows.shape[0]
                    begin = (2 * step + side) * TILE + index * size
                    hats[begin : begin + size] = h_rows
                    inverses[begin : begin + size] = i_rows
                    normed[begin : begin + size] = (
                        h_rows * vectors[0:1] + vectors[1:2]
                    ).astype(BF16)

            return [lambda i=i: one(i) for i in range(group // SUB)]

        def finish(tile):
            rows = tile_rows(tile)

            def spread():
                grad_normed[rows] = nt(grad_packed[rows], r["wq"][...])

            def norm_back(piece):
                hat, grad = hats[piece], grad_normed[piece]
                inverse = jnp.concatenate([inverses[piece]] * 2, axis=1)
                sums.gain = sums.gain + fold(grad * hat)
                sums.shift = sums.shift + fold(grad)
                grad = branch_in[piece].astype(F32) + center_back(
                    grad * vectors[0:1], hat, inverse
                )
                grad_normed[piece] = grad

            return [spread] + [lambda p=p: norm_back(p) for p in pieces_of(tile, PIECE)]

        def release(step):
            rows = step_rows(step)
            kept = {}

            def write(index):
                part = TALL // 4
                sides = []
                for side in range(2):
                    begin = (2 * step + side) * TILE + index * part * HALF
                    sides.append(grad_normed[begin : begin + part * HALF])
                block = r["x_blocks"].at[step]
                block[index * part : (index + 1) * part] = join(*sides).astype(BF16)

            def turn():
                kept["normed"] = normed[rows].T

            def weigh(part):
                cut = slice(part * D, (part + 1) * D)
                value = nn(kept["normed"], grad_packed[rows, cut])
                if step == 0:
                    r["acc"][:, cut] = value
                else:
                    r["acc"][:, cut] += value

            return (
                [lambda i=i: write(i) for i in range(4)]
                + [turn]
                + [lambda p=p: weigh(p) for p in range(3)]
            )

        def send_step(step):
            outs.append(
                copies.start(
                    r["x_blocks"].at[step], grad_x.at[:, step * BLOCK : (step + 1) * BLOCK]
                )
            )

        released = [release(step) for step in range(steps)]
        arrive()
        for one in start(0):
            one()
        interleave(soften(0), start(1), read_tokens(0))
        for tile in range(tiles):
            if tile % 2 == 0 and tile + 2 < tiles:
                arrive()
            if tile > 4 and tile % 2:
                send_step((tile - 5) // 2)
            lists = [gather(tile)]
            if tile + 1 < tiles:
                lists.append(soften(tile + 1))
            if tile + 2 < tiles:
                lists.append(start(tile + 2))
            if tile % 2 and (tile + 1) // 2 < steps:
                lists.append(read_tokens((tile + 1) // 2))
            if tile:
                lists.append(finish(tile - 1))
            if tile > 1 and tile % 2:
                lists.append(released[(tile - 3) // 2])
            interleave(*lists)
        send_step(steps - 2)
        interleave(finish(tiles - 1), released[steps - 1][4:])
        for one in released[steps - 1][:4]:
            one()
        send_step(steps - 1)
        flatten(flat, 0, r["acc"][...], ROW_QKV, 6)
        flatten_vector(flat, ROW_GAIN_ONE, column_sum(sums.gain))
        flatten_vector(flat, ROW_SHIFT_ONE, column_sum(sums.shift))
        flat[ROW_OUT : ROW_OUT + 8] = first[...]
        send_rows(plan, place_ref, flat, 0, r["parts_in"], 0, plan.lead)
        outs.append(copies.start(r["parts_in"].at[1], send))
        outs.append(copies.start(r["parts_in"].at[0], keep))
        for copy in outs:
            copy.wait()

    vmem = pl.BlockSpec(memory_space=pltpu.VMEM)
    hbm = pl.BlockSpec(memory_space=pl.ANY)
    shape = jax.ShapeDtypeStruct
    parts = (PLANE, plan.lead, plan.rows, LANES)
    wide = lambda width, kind: pltpu.VMEM((count, width), kind)
    pair = lambda kind: pltpu.VMEM((2, HEADS * TILE, TILE), kind)
    scratch = dict(
        x_in=pltpu.VMEM((steps, group, local_rows, BLOCK, D), BF16),
        packed_in=wide(3 * D, BF16),
        branch_in=wide(D, BF16),
        wq=pltpu.VMEM((D, 3 * D), BF16),
        wo=pltpu.VMEM((D, D), BF16),
        hats=wide(D, F32),
        inverses=wide(LANES, F32),
        normed=wide(D, BF16),
        grad_att=wide(D, BF16),
        scores=pair(F32),
        grad_probs=pair(F32),
        probs=pair(BF16),
        grad_scores=pair(BF16),
        grad_packed=wide(3 * D, BF16),
        grad_normed=wide(D, F32),
        x_blocks=pltpu.VMEM((steps, TALL, BLOCK, D), BF16),
        cap=pltpu.VMEM((TILE, TILE), F32),
        acc=pltpu.VMEM((D, 3 * D), F32),
        flat=pltpu.VMEM((ROW_OUT + plan.rows + 8, LANES), F32),
        parts_in=pltpu.VMEM((CORES,) + parts, BF16),
        sems=pltpu.SemaphoreType.DMA((4 + 4 * steps,)),
    )
    return pl.pallas_call(
        kernel,
        in_specs=[pl.BlockSpec(memory_space=pltpu.SMEM)] + [hbm] * 5 + [vmem] * 3,
        out_specs=[hbm] * 3,
        out_shape=[
            shape((TALL, steps * BLOCK, D), BF16),
            shape(parts, BF16),
            shape(parts, BF16),
        ],
        scratch_shapes=[scratch[name] for name in names],
        compiler_params=pltpu.CompilerParams(vmem_limit_bytes=VMEM_BYTES),
        cost_estimate=pl.CostEstimate(
            flops=10 * 10**9, bytes_accessed=8 * 10**6, transcendentals=10**6
        ),
        name="back",
    )


def cut_kernel(group, steps):
    def kernel(rows_ref, cot_ref, out_ref):
        for member in range(group):
            for step in range(steps):
                column = (member * steps + step) * BLOCK
                for kind, ref in enumerate((rows_ref, cot_ref)):
                    out_ref[member, step, kind] = ref[:, column : column + BLOCK]

    return kernel


def local(mesh_shape, tokens, column_rows, cotangent, flat_params):
    seq = mesh_shape["seq"]
    local_rows, columns = tokens.shape[1], tokens.shape[2]
    group = TALL // local_rows
    owned = columns // group
    steps = owned // BLOCK
    plan = Plan(seq, group, flat_params.shape[0])
    seq_at = lax.axis_index("seq")
    core_at = lax.axis_index("dp")
    deep_at, plane_at = seq_at // PLANE, seq_at % PLANE
    holder = seq_at % group * owned // STRIDE * (seq * STRIDE // columns)
    place = jnp.stack([deep_at, plane_at, core_at, holder]).astype(jnp.int32)
    shift = plan.shard * (seq_at * CORES + core_at) % LANES
    groups = [[group * g + i for i in range(group)] for g in range(seq // group)]
    deep_groups = [[PLANE * z + q for z in range(plan.deep)] for q in range(PLANE)]

    def exchange(blocks):
        return lax.all_to_all(blocks, "seq", 0, 0, axis_index_groups=groups, tiled=True)

    def to_rows(cols):
        moved = exchange(cols.reshape(group, local_rows, owned, D))
        return moved.transpose(1, 0, 2, 3).reshape(tokens.shape)

    def swap_seq(value, distance):
        return lax.ppermute(value, "seq", [(i, i ^ distance) for i in range(seq)])

    def swap_core(value):
        return lax.ppermute(value, "dp", [(0, 1), (1, 0)])

    wide = jnp.pad(flat_params, (LANES, plan.rows * LANES - plan.shard))
    own = lax.dynamic_slice(wide, (LANES - shift,), (plan.rows * LANES,))
    index = lax.iota(jnp.int32, plan.rows * LANES)
    own = jnp.where(index >= (plan.rows - 1) * LANES, column_rows[0, 0].astype(BF16), own)
    own = own.reshape(plan.rows, LANES)
    if plan.pairwise:
        arrived = [swap_seq(own, PLANE * k) for k in range(1, plan.deep)]
        deep = jnp.stack([own] + arrived)
    else:
        arrived = [own]
        deep = lax.all_gather(own, "seq", axis=0, axis_index_groups=deep_groups)
    vmem = pl.BlockSpec(memory_space=pltpu.VMEM)
    both = pl.pallas_call(
        cut_kernel(group, steps),
        out_shape=jax.ShapeDtypeStruct((group, steps, 2, local_rows, BLOCK, D), BF16),
        in_specs=[vmem, vmem],
        out_specs=vmem,
        compiler_params=pltpu.CompilerParams(vmem_limit_bytes=VMEM_BYTES),
        name="cut",
    )(tokens.reshape(local_rows, columns, D), cotangent.reshape(local_rows, columns, D))
    deep, both = lax.optimization_barrier((deep, both))
    both = exchange(both)
    plane = [deep] + [swap_seq(deep, k) for k in range(1, PLANE)]
    pieces = plane + [swap_core(piece) for piece in plane]
    w_qkv, w_out, w_in, w_back, vectors, bias_in = prepare(plan)(place, *pieces)

    packed, logsum, out, branch, keep, send, first = layer(plan, steps, local_rows)(
        place, both, w_qkv, w_out, w_in, w_back, vectors, bias_in
    )

    moved_out = exchange(out.reshape(group, local_rows, owned, D))

    def core_sum(keep, send):
        return keep.astype(F32) + swap_core(send).astype(F32)

    def plane_swap(value):
        sent = value.astype(BF16)
        return [value[0]] + [swap_seq(sent[k], k) for k in range(1, PLANE)]

    def added(pieces):
        total = pieces[0]
        for piece in pieces[1:]:
            total = total + piece.astype(F32)
        return total

    later = added(plane_swap(core_sum(keep, send)))

    grad_x, lead_keep, lead_send = back(plan, steps, local_rows)(
        place, both, packed, branch, w_qkv, w_out, vectors, logsum, first
    )
    lead_send, moved_out, later = lax.optimization_barrier((lead_send, moved_out, later))
    lead = plane_swap(core_sum(lead_keep, lead_send))
    total = jnp.concatenate([added(lead), later], axis=0)
    moved_x = exchange(grad_x.reshape(group, local_rows, owned, D))
    total, moved_x, moved_out = lax.optimization_barrier((total, moved_x, moved_out))
    layer_out = moved_out.transpose(1, 0, 2, 3).reshape(tokens.shape)
    input_grad = moved_x.transpose(1, 0, 2, 3).reshape(tokens.shape).astype(F32)
    if plan.pairwise:
        sent = total.astype(BF16)
        result = lax.dynamic_index_in_dim(total, deep_at, 0, keepdims=False)
        for k in range(1, plan.deep):
            piece = lax.dynamic_index_in_dim(sent, deep_at ^ k, 0, keepdims=False)
            result = result + swap_seq(piece, PLANE * k).astype(F32)
    else:
        moved = lax.all_to_all(
            total.astype(BF16), "seq", 0, 0, axis_index_groups=deep_groups, tiled=True
        )
        result = jnp.sum(moved.astype(F32), axis=0)
    param_grad = lax.dynamic_slice(result.reshape(-1), (shift,), (plan.shard,))
    return layer_out, input_grad, param_grad


def solution(mesh):
    shape = dict(mesh.shape)
    rows = P("dp", "seq", None, None)
    flat = P(("seq", "dp"))
    return jax.shard_map(
        lambda *args: local(shape, *args),
        mesh=mesh,
        in_specs=(rows, P("dp", "seq"), rows, flat),
        out_specs=(rows, rows, flat),
        check_vma=False,
    )
```
